256 devices in a mesh: leaf: 32 (over y, z), lvl: 8 (over x, core).
Axes of the slice: x: 4, y: 4, z: 8, core: 2. Of those that a mesh axis runs over, the one named last changes fastest.
Arguments:
- targets: float32 [64, 131072], P(None, ('leaf', 'lvl')), may hold values from -6 to 6
- tree_pos: int32 [131072], P(('leaf', 'lvl')), may hold values from 0 to 131071, as said below
- coords: float32 [8, 131072], P(None, ('leaf', 'lvl')), may hold values from -5 to 5
- ubasis: float32 [1024, 64, 128], P(('leaf', 'lvl')), may hold values from -0.5 to 0.5
- transfer_one: float32 [1024, 64, 64], P(('leaf', 'lvl')), may hold values from -0.375 to 0.375
- transfer_two: float32 [256, 64, 64], P(('leaf', 'lvl')), may hold values from -0.25 to 0.25
- anchors_one: float32 [256, 8, 64], P(('leaf', 'lvl')), may hold values from -5 to 5
- anchors_two: float32 [32, 8, 64], P('leaf'), may hold values from -5 to 5
- near_list: int32 [1024, 7], P(('leaf', 'lvl')), may hold values from 0 to 1023, as said below
- far_one: int32 [256, 4], P(('leaf', 'lvl')), may hold values from 0 to 255, as said below
- far_two: int32 [32, 4], P('leaf'), may hold values from 0 to 31, as said below
Outputs:
- coeffs: float32 [64, 131072], P(None, ('leaf', 'lvl'))
- residual: float32 [64, 131072], P(None, ('leaf', 'lvl'))
The draws below stay inside these ranges and needn't reach their ends.
Inputs may be any that keep to these rules, and one draw needn't show every extreme that they name: `tree_pos`: A permutation; of the 512 entries of each aligned block of user points, exactly 2 lie in each aligned block of 512 tree positions. near_list[near_list[c, k], k] = c and near_list[c, k] != c; the partner lies in the same window of 8 consecutive leaf clusters as c, windows starting at multiples of 8 for even k and at 4 plus such multiples for odd k, counted cyclically over the 1024 clusters. far_one[far_one[d, k], k] = d, far_one[d, k] != d, and far_one[d, k] // 8 = d // 8. far_two[far_two[e, k], k] = e and far_two[e, k] != e.
All inputs are finite; a program needn't handle non-finite values.
Results may differ from the reference program's by a relative error of at most 0.0003.
Values sent between devices are 32-bit elements; how exact they have to be, the bound alone decides.
A program may use at most 64 MiB of HBM per device.

```python
from functools import partial
import jax
import jax.numpy as jnp
from jax import lax

R = 64
PB = 128
KS = 64
DIM = 8
NM = 7
F1 = 4
F2 = 4
ITERS = 2
LC = 4
NL = 1024
PTS_DEV = 512
NPTS = 131072
SEND = 2
ML1 = 256
SUBS = 8
GROUPS = 32
DEVICES = 256


def pair_partners(key, item_count):
    shuffled = jax.random.permutation(key, item_count).astype(jnp.int32)
    even_items = shuffled[0::2]
    odd_items = shuffled[1::2]
    partner = jnp.zeros((item_count,), jnp.int32)
    partner = partner.at[even_items].set(odd_items)
    partner = partner.at[odd_items].set(even_items)
    return partner


def draw_near_list(key, part):
    key = jax.random.fold_in(key, 11)
    windows = NL // (2 * LC)
    columns = []
    for column in range(NM):
        window_keys = jax.random.split(jax.random.fold_in(key, column), windows)
        partner = jax.vmap(partial(pair_partners, item_count=2 * LC))(window_keys)
        starts = (jnp.arange(windows, dtype=jnp.int32) * (2 * LC))[:, None]
        shift_by = column % 2 * LC
        placed = ((partner + starts + shift_by) % NL).reshape(-1)
        columns.append(jnp.roll(placed, shift_by))
    return jnp.stack(columns, axis=1).astype(jnp.int32)


def draw_far_one(key, part):
    key = jax.random.fold_in(key, 23)
    columns = []
    for column in range(F1):
        group_keys = jax.random.split(jax.random.fold_in(key, column), GROUPS)
        partner = jax.vmap(partial(pair_partners, item_count=SUBS))(group_keys)
        starts = (jnp.arange(GROUPS, dtype=jnp.int32) * SUBS)[:, None]
        columns.append((partner + starts).reshape(-1))
    return jnp.stack(columns, axis=1).astype(jnp.int32)


def draw_far_two(key, part):
    key = jax.random.fold_in(key, 29)
    columns = []
    for column in range(F2):
        columns.append(pair_partners(jax.random.fold_in(key, column), GROUPS))
    return jnp.stack(columns, axis=1).astype(jnp.int32)


def draw_tree_pos(key, part):
    key = jax.random.fold_in(key, 37)
    source_keys = jax.random.split(jax.random.fold_in(key, 1), DEVICES)
    places = jax.vmap(partial(jax.random.permutation, x=PTS_DEV))(source_keys).astype(jnp.int32)
    destination = places // SEND
    rank_in = places % SEND
    slot_index = jnp.arange(DEVICES, dtype=jnp.int32)[:, None] * SEND + rank_in
    target_keys = jax.random.split(jax.random.fold_in(key, 2), DEVICES)
    shuffles = jax.vmap(partial(jax.random.permutation, x=PTS_DEV))(target_keys).astype(jnp.int32)
    within = shuffles[destination, slot_index]
    return (destination * PTS_DEV + within).reshape(-1).astype(jnp.int32)


def levels(rng, shape, cuts, least, high):
    level = 1.0
    for dim, shards_of in cuts:
        heights = jax.random.uniform(jax.random.fold_in(jax.random.fold_in(rng, 6), dim), (shards_of,), jnp.float32, least / len(cuts), high / len(cuts))
        level = level * jnp.repeat(jnp.exp(heights), shape[dim] // shards_of).reshape((-1,) + (1,) * (len(shape) - 1 - dim))
    return level


def normal_values(key, extent, deviation, reach, cuts=(), kind=jnp.bfloat16):
    array = deviation * jax.random.normal(key, extent, jnp.float32)
    if cuts:
        array = array * levels(key, extent, cuts, -0.22, 0.18)
    return jnp.clip(array, -reach, reach).astype(kind)


def setup_inputs(seed: int = 0) -> dict:
    key_of = jax.random.split(jax.random.key(seed), 12)
    return {
        "targets": normal_values(key_of[0], (R, NPTS), 1.0, 6.0, ((1, 256),), jnp.float32),
        "tree_pos": draw_tree_pos(jax.random.fold_in(key_of[11], 71), 0),
        "coords": normal_values(key_of[2], (DIM, NPTS), 1.0, 5.0, ((1, 256),), jnp.float32),
        "ubasis": normal_values(key_of[3], (NL, KS, PB), PB ** -0.5, 0.5, ((0, 256),), jnp.float32),
        "transfer_one": normal_values(key_of[4], (NL, KS, KS), (LC * KS) ** -0.5, 0.375, ((0, 256),), jnp.float32),
        "transfer_two": normal_values(key_of[5], (ML1, KS, KS), (SUBS * KS) ** -0.5, 0.25, ((0, 256),), jnp.float32),
        "anchors_one": normal_values(key_of[6], (ML1, DIM, KS), 1.0, 5.0, ((0, 256),), jnp.float32),
        "anchors_two": normal_values(key_of[7], (GROUPS, DIM, KS), 1.0, 5.0, ((0, 32),), jnp.float32),
        "near_list": draw_near_list(jax.random.fold_in(key_of[11], 71), 0),
        "far_one": draw_far_one(jax.random.fold_in(key_of[11], 71), 0),
        "far_two": draw_far_two(jax.random.fold_in(key_of[11], 71), 0),
    }


PRECISE = lax.Precision.HIGHEST
RIDGE = 1.0
EPSILON = 1e-6


def kernel_block(left_pts, right_pts):
    left_sq = jnp.sum(left_pts * left_pts, axis=1)
    right_sq = jnp.sum(right_pts * right_pts, axis=1)
    cross = jnp.einsum('bdm,bdn->bmn', left_pts, right_pts, precision=PRECISE)
    distance = left_sq[:, :, None] + right_sq[:, None, :] - 2.0 * cross
    return jnp.exp(-distance / DIM)


def apply_operator(vector, points, ubasis, transfer_one, transfer_two, anchors_one, anchors_two, near_list, far_one, far_two):
    vec_blocks = vector.reshape(R, NL, PB)

    def near_batch(first_id):
        cluster_ids = first_id + jnp.arange(LC, dtype=jnp.int32)
        own_points = jnp.take(points, cluster_ids, axis=0)
        accumulated = jnp.einsum('rcq,cqp->rcp', jnp.take(vec_blocks, cluster_ids, axis=1), kernel_block(own_points, own_points), precision=PRECISE)
        for column in range(NM):
            partner_ids = jnp.take(near_list[:, column], cluster_ids)
            coupling = kernel_block(jnp.take(points, partner_ids, axis=0), own_points)
            accumulated = accumulated + jnp.einsum('rcq,cqp->rcp', jnp.take(vec_blocks, partner_ids, axis=1), coupling, precision=PRECISE)
        return accumulated

    first_ids = jnp.arange(DEVICES, dtype=jnp.int32) * LC
    near_sum = lax.map(near_batch, first_ids)
    near_sum = jnp.transpose(near_sum, (1, 0, 2, 3)).reshape(R, NL * PB)
    near_sum = near_sum * ((PB * (NM + 1)) ** -0.5)

    leaf_skel = jnp.einsum('rcq,ckq->rck', vec_blocks, ubasis, precision=PRECISE)
    lower_four = transfer_one.reshape(ML1, LC, KS, KS)
    upper_four = transfer_two.reshape(GROUPS, SUBS, KS, KS)
    level_one = jnp.einsum('rdck,dckj->rdj', leaf_skel.reshape(R, ML1, LC, KS), lower_four, precision=PRECISE)
    level_two = jnp.einsum('rgsk,gskj->rgj', level_one.reshape(R, GROUPS, SUBS, KS), upper_four, precision=PRECISE)

    far_lower = jnp.zeros((R, ML1, KS), jnp.float32)
    for column in range(F1):
        partner_ids = far_one[:, column]
        coupling = kernel_block(jnp.take(anchors_one, partner_ids, axis=0), anchors_one)
        far_lower = far_lower + jnp.einsum('rdk,dkj->rdj', jnp.take(level_one, partner_ids, axis=1), coupling, precision=PRECISE)
    far_upper = jnp.zeros((R, GROUPS, KS), jnp.float32)
    for column in range(F2):
        partner_ids = far_two[:, column]
        coupling = kernel_block(jnp.take(anchors_two, partner_ids, axis=0), anchors_two)
        far_upper = far_upper + jnp.einsum('rek,ekj->rej', jnp.take(level_two, partner_ids, axis=1), coupling, precision=PRECISE)

    down_two = jnp.einsum('rgj,gskj->rgsk', far_upper * (F2 ** -0.5), upper_four, precision=PRECISE).reshape(R, ML1, KS)
    level_pot = far_lower * (F1 ** -0.5) + down_two
    leaf_pot = jnp.einsum('rdj,dckj->rdck', level_pot, lower_four, precision=PRECISE).reshape(R, NL, KS)
    far_out = jnp.einsum('rck,ckq->rcq', leaf_pot, ubasis, precision=PRECISE).reshape(R, NL * PB)
    return near_sum + far_out


def reference(targets, tree_pos, coords, ubasis, transfer_one, transfer_two, anchors_one, anchors_two, near_list, far_one, far_two):
    tree_vals = jnp.zeros((R, NPTS), jnp.float32).at[:, tree_pos].set(targets)
    points = jnp.transpose(coords.reshape(DIM, NL, PB), (1, 0, 2))

    def operate(vector):
        return apply_operator(vector, points, ubasis, transfer_one, transfer_two, anchors_one, anchors_two, near_list, far_one, far_two)

    right_side = operate(tree_vals)
    solution = jnp.zeros((R, NPTS), jnp.float32)
    resid_vec = right_side
    direction = right_side
    norm_now = jnp.sum(resid_vec * resid_vec, axis=1)
    for turn_index in range(ITERS):
        image_vec = operate(direction)
        a_image = operate(image_vec) + RIDGE * direction
        curvature = jnp.sum(direction * a_image, axis=1)
        step_size = norm_now / (curvature + EPSILON)
        solution = solution + step_size[:, None] * direction
        resid_vec = resid_vec - step_size[:, None] * a_image
        if turn_index + 1 < ITERS:
            fresh_norm = jnp.sum(resid_vec * resid_vec, axis=1)
            direction = resid_vec + (fresh_norm / (norm_now + EPSILON))[:, None] * direction
            norm_now = fresh_norm
    coeffs = jnp.take(solution, tree_pos, axis=1)
    residual = jnp.take(resid_vec, tree_pos, axis=1)
    return (coeffs, residual)
```

```python
import jax
import jax.numpy as jnp
from jax import lax
from jax.experimental import pallas as pl
from jax.experimental.pallas import tpu as pltpu
from jax.sharding import PartitionSpec as P

F32 = jnp.float32
BF16 = jnp.bfloat16
MESH = pl.DeviceIdType.MESH
PRECISE = lax.Precision.HIGHEST
DIM = 8
RIDGE = 1.0
EPSILON = 1e-6
APPLIES = 5
LANES = 128


def dot(a, b, ca=1, cb=0):
    return lax.dot_general(a, b, (((ca,), (cb,)), ((), ())), preferred_element_type=F32)


def dot_precise(a, b):
    return lax.dot_general(
        a, b, (((1,), (0,)), ((), ())), precision=PRECISE, preferred_element_type=F32
    )


def split2(x):
    hi = x.astype(BF16)
    return hi, (x - hi.astype(F32)).astype(BF16)


def split3(x):
    hi = x.astype(BF16)
    rest = x - hi.astype(F32)
    mid = rest.astype(BF16)
    return hi, mid, (rest - mid.astype(F32)).astype(BF16)


def dot_split(a, b_hi, b_lo):
    rows = a.shape[0]
    a_hi, a_lo = split2(a)
    both = dot(jnp.concatenate([a_hi, a_lo], axis=0), b_hi)
    return both[:rows] + both[rows:] + dot(a_hi, b_lo)


def iota(shape, dim):
    return lax.broadcasted_iota(jnp.int32, shape, dim)


def augmented(x):
    n = x.shape[1]
    x1, x2, x3 = (p.astype(F32) for p in split3(x))
    sq = jnp.sum(x * x, axis=0, keepdims=True) * (-1.0 / DIM)
    n1, n2, n3 = (p.astype(F32) for p in split3(sq))
    row = iota((8, n), 0)
    lead = jnp.where(row == 0, n1, jnp.where(row == 1, n2, n3))
    tail = jnp.where(row == 3, n1, jnp.where(row == 4, n2, n3))
    zero = jnp.zeros((8, n), F32)
    src_norm = jnp.where(row < 3, lead, jnp.where(row < 6, 1.0, 0.0))
    dst_norm = jnp.where(row < 3, 1.0, jnp.where(row < 6, tail, 0.0))
    q = 2.0 / DIM
    src = jnp.concatenate([x1, x1, x2, x1, x3, x2, src_norm, zero], axis=0)
    dst = jnp.concatenate([x1 * q, x2 * q, x1 * q, x3 * q, x1 * q, x2 * q, dst_norm, zero], axis=0)
    return src, dst


def pack(onehot, x):
    total = None
    for part in split3(x):
        zero = jnp.zeros_like(part)
        wide = jnp.concatenate(
            [jnp.concatenate([part, zero], axis=1), jnp.concatenate([zero, part], axis=1)], axis=0
        )
        term = dot(onehot, wide, 1, 1)
        total = term if total is None else total + term
    return total


def unpack(onehot, g):
    half = g.shape[1] // 2
    cols = onehot.shape[1] // 2
    gt = jnp.transpose(g)
    total = None
    for part in split3(gt):
        term = dot(part, onehot)
        total = term if total is None else total + term
    return total[:half, :cols] + total[half:, cols:]


def kernel(
    sizes,
    targets, tree_pos, coords, ubasis, transfer_one, transfer_two, anchors_one, anchors_two,
    near_list, far_one, far_two,
    coeffs, residual,
    oh_user, oh_tree, s_a, r_a, s_b, r_b, s_c, r_c, s_d, r_d,
    r_coords, s_anch, r_anch, s_top, r_top,
    src_pts, w_hi, w_lo, k1_hi, k1_lo, k2_hi, k2_lo, c_hi, c_lo, ct_hi, ct_lo,
    vbuf, pbuf, acc, r_halo, s1, r1, s2, r2, s3, r3, step_ref, norm_ref,
    set_send, set_recv, send_sem, halo_sem, stage_sem,
):
    n_leaf, n_lvl = sizes
    leaf, lvl = lax.axis_index("leaf"), lax.axis_index("lvl")
    rows, pts = targets.shape
    clusters = ubasis.shape[0]
    points = ubasis.shape[2]
    total = n_leaf * n_lvl * clusters
    near_lists = near_list.shape[1]

    def lvl_peer(k):
        return lax.rem(lvl + k, n_lvl)

    def leaf_peer(k):
        return lax.rem(leaf + k, n_leaf)

    ring = leaf * n_lvl + lvl
    n_all = n_leaf * n_lvl
    after = lax.rem(ring + 1, n_all)
    before = lax.rem(ring + n_all - 1, n_all)
    after_id = (after // n_lvl, lax.rem(after, n_lvl))
    before_id = (before // n_lvl, lax.rem(before, n_lvl))

    def copy(src, dst, send, recv, device):
        pltpu.make_async_remote_copy(
            src_ref=src, dst_ref=dst, send_sem=send, recv_sem=recv,
            device_id=device, device_id_type=MESH,
        ).start()

    def wait(ref, sem):
        pltpu.make_async_copy(ref, ref, sem).wait()

    def over_lvl(src, dst, send, recv):
        for k in range(1, n_lvl):
            peer = lvl_peer(k)
            copy(src(peer), dst, send, recv, (leaf, peer))

    def over_leaf(src, dst, send, recv):
        for k in range(1, n_leaf):
            peer = leaf_peer(k)
            copy(src(peer), dst, send, recv, (peer, lvl))

    barrier = pltpu.get_barrier_semaphore()
    for k in range(1, n_lvl):
        pl.semaphore_signal(barrier, inc=1, device_id=(leaf, lvl_peer(k)), device_id_type=MESH)
    for k in range(1, n_leaf):
        pl.semaphore_signal(barrier, inc=1, device_id=(leaf_peer(k), lvl), device_id_type=MESH)
    pl.semaphore_signal(barrier, inc=1, device_id=after_id, device_id_type=MESH)
    pl.semaphore_signal(barrier, inc=1, device_id=before_id, device_id_type=MESH)

    lane = iota((8, LANES), 1)
    low = lane < LANES // 2
    row8 = iota((8, LANES), 0)
    ranks = anchors_one.shape[2]
    own_one = jnp.concatenate([anchors_one[0], anchors_one[0]], axis=1)
    own_two = jnp.concatenate([anchors_two[0], anchors_two[0]], axis=1)
    partner = jnp.full((8, LANES), -1.0, F32)
    for k in range(far_one.shape[1]):
        value = lax.rem(far_one[0, k], n_lvl).astype(F32)
        partner = jnp.where(row8 == k, value, partner)
    s_anch[0] = own_one
    s_anch[1] = partner
    r_anch[lvl] = s_anch[...]
    s_top[...] = own_two
    r_top[leaf] = own_two

    n_dev = n_leaf * n_lvl
    tp = tree_pos[...]
    dest = lax.div(tp, pts)
    place = lax.rem(dest, n_lvl) * n_leaf + lax.div(dest, n_lvl)
    hit = iota((n_dev, pts), 0) == place
    hit16 = hit.astype(F32).astype(BF16)
    earlier = (iota((pts, pts), 0) < iota((pts, pts), 1)).astype(F32).astype(BF16)
    seen = dot(hit16, earlier)
    oh_user[:, :pts] = jnp.where(hit & (seen < 0.5), 1.0, 0.0).astype(BF16)
    oh_user[:, pts:] = jnp.where(hit & (seen > 0.5), 1.0, 0.0).astype(BF16)
    s_a[:, 0] = pack(oh_user[...], targets[...]).reshape(n_lvl, n_leaf, LANES)
    pos = jnp.broadcast_to(lax.rem(tp, pts).astype(F32), (rows, pts))
    s_a[:, 1] = pack(oh_user[...], pos).reshape(n_lvl, n_leaf, LANES)
    r_a[lvl] = s_a[lvl]

    pl.semaphore_wait(barrier, n_lvl + n_leaf)

    over_lvl(lambda p: s_a.at[p], r_a.at[lvl], set_send.at[0], set_recv.at[0])
    copy(coords, r_coords.at[0], set_send.at[1], set_recv.at[1], after_id)
    copy(coords, r_coords.at[1], set_send.at[2], set_recv.at[2], before_id)
    over_lvl(lambda p: s_anch, r_anch.at[lvl], set_send.at[3], set_recv.at[3])
    over_leaf(lambda p: s_top, r_top.at[leaf], set_send.at[4], set_recv.at[4])

    bt = jnp.concatenate(
        [dot_precise(jnp.transpose(transfer_one[c]), ubasis[c]) for c in range(clusters)], axis=1
    )
    b2t = dot_precise(jnp.transpose(transfer_two[0]), bt)
    ct = jnp.concatenate([bt, b2t], axis=0)
    ct_hi[...], ct_lo[...] = split2(ct)
    c_hi[...], c_lo[...] = split2(jnp.transpose(ct))

    wait(r_a.at[pl.ds(0, n_lvl - 1)], set_recv.at[0])
    for kind in range(2):
        s_b[:, kind] = jnp.swapaxes(r_a[:, kind], 0, 1)
    r_b[leaf] = s_b[leaf]
    over_leaf(lambda p: s_b.at[p], r_b.at[leaf], set_send.at[5], set_recv.at[5])

    wait(r_coords.at[0], set_recv.at[1])
    wait(r_coords.at[1], set_recv.at[2])
    src, dst = augmented(coords[...])
    src_pts[pts : 2 * pts] = jnp.transpose(src).astype(BF16)
    src_pts[:pts] = jnp.transpose(augmented(r_coords[0])[0]).astype(BF16)
    src_pts[2 * pts :] = jnp.transpose(augmented(r_coords[1])[0]).astype(BF16)
    dst = dst.astype(BF16)
    first = ring * clusters - clusters
    near_scale = (points * (near_lists + 1)) ** (-0.5)

    def near_rows(n, carry):
        at = pl.ds(pl.multiple_of(n * points, points), points)
        value = jnp.exp(dot(src_pts[at, :], dst))
        parts = []
        for c in range(clusters):
            weight = (n == c + clusters).astype(jnp.int32)
            for k in range(near_lists):
                rel = lax.rem(near_list[c, k] - first + total, total)
                weight = weight + (rel == n).astype(jnp.int32)
            scaled = weight.astype(F32) * near_scale
            parts.append(value[:, c * points : (c + 1) * points] * scaled)
        hi, lo = split2(jnp.concatenate(parts, axis=1))
        w_hi[at, :] = hi
        w_lo[at, :] = lo
        return carry

    lax.fori_loop(0, 3 * clusters, near_rows, 0)

    def lanes_of(get):
        tiles = []
        for m in range(n_lvl // 2):
            tiles.append(jnp.where(low, get(2 * m), get(2 * m + 1)))
        return jnp.concatenate(tiles, axis=1)

    wait(r_anch.at[pl.ds(0, n_lvl - 1)], set_recv.at[3])
    src, dst = augmented(lanes_of(lambda p: r_anch[p, 0]))
    wide = n_lvl * ranks
    partners = lanes_of(lambda p: r_anch[p, 1])
    owner = lax.div(iota((wide, wide), 0), ranks).astype(F32)
    count = jnp.zeros((wide, wide), F32)
    for k in range(far_one.shape[1]):
        count = count + jnp.where(owner == partners[k : k + 1], 1.0, 0.0)
    value = jnp.exp(dot(jnp.transpose(src).astype(BF16), dst.astype(BF16)))
    k1_hi[...], k1_lo[...] = split2(value * count * (far_one.shape[1] ** (-0.5)))

    def chosen(get):
        picks = []
        for k in range(far_two.shape[1]):
            which = far_two[0, k]
            value = get(0)
            for q in range(1, n_leaf):
                value = jnp.where(which == q, get(q), value)
            picks.append(value)
        return picks

    wait(r_top.at[pl.ds(0, n_leaf - 1)], set_recv.at[4])
    tops = chosen(lambda q: r_top[q])
    src, _ = augmented(
        jnp.concatenate([jnp.where(low, tops[m], tops[m + 1]) for m in (0, 2)], axis=1)
    )
    _, dst = augmented(own_two)
    value = jnp.exp(dot(jnp.transpose(src).astype(BF16), dst.astype(BF16)))
    value = jnp.where(iota(value.shape, 1) < LANES // 2, 0.0, value)
    k2_hi[...], k2_lo[...] = split2(value * (far_two.shape[1] ** (-0.5)))

    wait(r_b.at[pl.ds(0, n_leaf - 1)], set_recv.at[5])
    got_pos = r_b[:, 1].reshape(n_dev, LANES).astype(jnp.int32)
    column = iota((n_dev, pts), 1)
    oh_tree[:, :pts] = jnp.where(column == got_pos[:, 0:1], 1.0, 0.0).astype(BF16)
    half = LANES // 2
    oh_tree[:, pts:] = jnp.where(column == got_pos[:, half : half + 1], 1.0, 0.0).astype(BF16)
    vbuf[0] = unpack(oh_tree[...], r_b[:, 0].reshape(n_dev, LANES))
    pbuf[...] = jnp.zeros_like(pbuf)

    def apply(i, carry):
        copy(vbuf.at[i], r_halo.at[i, 0], send_sem.at[i, 0], halo_sem.at[i, 0], after_id)
        copy(vbuf.at[i], r_halo.at[i, 1], send_sem.at[i, 1], halo_sem.at[i, 1], before_id)
        v = vbuf[i]
        tu = dot_split(v, c_hi[...], c_lo[...])
        p = pbuf[...]
        q1 = jnp.sum(p * p, axis=1, keepdims=True)
        q2 = jnp.sum(v * v, axis=1, keepdims=True)
        sums = jnp.where(iota((rows, LANES), 1) < LANES // 4, q1, q2)
        s1[i, :, 0] = tu.reshape(n_lvl, 8, LANES)
        s1[i, :, 1] = sums.reshape(n_lvl, 8, LANES)
        r1[i, lvl] = s1[i, lvl]
        over_lvl(lambda peer: s1.at[i, peer], r1.at[i, lvl], send_sem.at[i, 2], stage_sem.at[i, 0])
        acc[...] = dot_split(v, w_hi[pts : 2 * pts], w_lo[pts : 2 * pts])

        wait(r1.at[i, pl.ds(0, n_lvl - 1)], stage_sem.at[i, 0])
        got = r1[i]
        up = jnp.sum(got[:, 0], axis=0)
        part_sums = jnp.sum(got[:, 1], axis=0)
        message = jnp.where(low, part_sums, up)
        s2[i] = message
        r2[i, leaf] = message
        over_leaf(lambda peer: s2.at[i], r2.at[i, leaf], send_sem.at[i, 3], stage_sem.at[i, 1])

        tiles = [
            jnp.where(low, got[2 * m, 0], pltpu.roll(got[2 * m + 1, 0], half, 1))
            for m in range(n_lvl // 2)
        ]
        f1 = dot_split(jnp.concatenate(tiles, axis=1), k1_hi[...], k1_lo[...])
        wait(r_halo.at[i, 0], halo_sem.at[i, 0])
        near = acc[...] + dot_split(r_halo[i, 0], w_hi[:pts], w_lo[:pts])
        wait(r_halo.at[i, 1], halo_sem.at[i, 1])
        acc[...] = near + dot_split(r_halo[i, 1], w_hi[2 * pts :], w_lo[2 * pts :])

        wait(r2.at[i, pl.ds(0, n_leaf - 1)], stage_sem.at[i, 1])
        all_sums = jnp.sum(r2[i], axis=0)
        ups = chosen(lambda q: r2[i, q])
        tiles = [jnp.where(low, pltpu.roll(ups[m], half, 1), ups[m + 1]) for m in (0, 2)]
        f2 = dot_split(jnp.concatenate(tiles, axis=1), k2_hi[...], k2_lo[...])
        for d in range(n_lvl):
            tile = f1[:, (d // 2) * LANES : (d // 2 + 1) * LANES]
            if d % 2:
                tile = pltpu.roll(tile, half, 1)
            s3[i, d, 0] = jnp.where(low, tile, f2)
            s3[i, d, 1] = all_sums
        r3[i, lvl] = s3[i, lvl]
        over_lvl(lambda peer: s3.at[i, peer], r3.at[i, lvl], send_sem.at[i, 4], stage_sem.at[i, 2])
        wait(r3.at[i, pl.ds(0, n_lvl - 1)], stage_sem.at[i, 2])
        pots = r3[i, :, 0].reshape(rows, LANES)
        sums = r3[i, :, 1].reshape(rows, LANES)
        sum_p = sums[:, 0:1]
        sum_v = sums[:, LANES // 4 : LANES // 4 + 1]
        out = acc[...] + dot_split(pots, ct_hi[...], ct_lo[...])

        @pl.when(i < 2)
        def _():
            vbuf[i + 1] = out

        @pl.when(i == 0)
        def _():
            pbuf[...] = out

        @pl.when(i == 2)
        def _():
            step = sum_p / (sum_p + sum_v + EPSILON)
            norm_ref[0] = jnp.broadcast_to(sum_p, (rows, LANES))
            step_ref[...] = jnp.broadcast_to(step, (rows, LANES))
            d0 = vbuf[1]
            vbuf[3] = d0 - step * (out + RIDGE * d0)

        @pl.when(i == 3)
        def _():
            beta = sum_v / (norm_ref[0][:, 0:1] + EPSILON)
            norm_ref[1] = jnp.broadcast_to(sum_v, (rows, LANES))
            pbuf[...] = vbuf[3] + beta * vbuf[1]
            vbuf[4] = out + beta * vbuf[2]

        @pl.when(i == 4)
        def _():
            step = norm_ref[1][:, 0:1] / (sum_p + sum_v + EPSILON)
            d1 = pbuf[...]
            sol = step_ref[...][:, 0:1] * vbuf[1] + step * d1
            res = vbuf[3] - step * (out + RIDGE * d1)
            s_c[:, 0] = pack(oh_tree[...], sol).reshape(n_leaf, n_lvl, LANES)
            s_c[:, 1] = pack(oh_tree[...], res).reshape(n_leaf, n_lvl, LANES)

        wait(vbuf.at[i], send_sem.at[i, 0])
        wait(vbuf.at[i], send_sem.at[i, 1])
        wait(r1.at[i, pl.ds(0, n_lvl - 1)], send_sem.at[i, 2])
        wait(r2.at[i, pl.ds(0, n_leaf - 1)], send_sem.at[i, 3])
        wait(r3.at[i, pl.ds(0, n_lvl - 1)], send_sem.at[i, 4])
        return carry

    lax.fori_loop(0, APPLIES, apply, 0)

    r_c[leaf] = s_c[leaf]
    over_leaf(lambda p: s_c.at[p], r_c.at[leaf], set_send.at[6], set_recv.at[6])
    wait(r_c.at[pl.ds(0, n_leaf - 1)], set_recv.at[6])
    for kind in range(2):
        s_d[:, kind] = jnp.swapaxes(r_c[:, kind], 0, 1)
    r_d[lvl] = s_d[lvl]
    over_lvl(lambda p: s_d.at[p], r_d.at[lvl], set_send.at[7], set_recv.at[7])
    wait(r_d.at[pl.ds(0, n_lvl - 1)], set_recv.at[7])
    coeffs[...] = unpack(oh_user[...], r_d[:, 0].reshape(n_dev, LANES))
    residual[...] = unpack(oh_user[...], r_d[:, 1].reshape(n_dev, LANES))

    wait(r_a.at[pl.ds(0, n_lvl - 1)], set_send.at[0])
    wait(r_coords.at[0], set_send.at[1])
    wait(r_coords.at[1], set_send.at[2])
    wait(r_anch.at[pl.ds(0, n_lvl - 1)], set_send.at[3])
    wait(r_top.at[pl.ds(0, n_leaf - 1)], set_send.at[4])
    wait(r_b.at[pl.ds(0, n_leaf - 1)], set_send.at[5])
    wait(r_c.at[pl.ds(0, n_leaf - 1)], set_send.at[6])
    wait(r_d.at[pl.ds(0, n_lvl - 1)], set_send.at[7])


def on_device(
    targets, tree_pos, coords, ubasis, transfer_one, transfer_two, anchors_one, anchors_two,
    near_list, far_one, far_two,
):
    rows, pts = targets.shape
    n_leaf, n_lvl = lax.axis_size("leaf"), lax.axis_size("lvl")
    n_dev = n_leaf * n_lvl
    dim = coords.shape[0]
    vmem = pl.BlockSpec(memory_space=pltpu.VMEM)
    smem = pl.BlockSpec(memory_space=pltpu.SMEM)
    V = pltpu.VMEM
    wide = n_lvl * anchors_one.shape[2]
    deep = far_two.shape[1] * anchors_two.shape[2]
    scratch = [
        V((n_dev, 2 * pts), BF16), V((n_dev, 2 * pts), BF16),
        V((n_lvl, 2, n_leaf, LANES), F32), V((n_lvl, 2, n_leaf, LANES), F32),
        V((n_leaf, 2, n_lvl, LANES), F32), V((n_leaf, 2, n_lvl, LANES), F32),
        V((n_leaf, 2, n_lvl, LANES), F32), V((n_leaf, 2, n_lvl, LANES), F32),
        V((n_lvl, 2, n_leaf, LANES), F32), V((n_lvl, 2, n_leaf, LANES), F32),
        V((2, dim, pts), F32),
        V((2, 8, LANES), F32), V((n_lvl, 2, 8, LANES), F32),
        V((8, LANES), F32), V((n_leaf, 8, LANES), F32),
        V((3 * pts, 64), BF16),
        V((3 * pts, pts), BF16), V((3 * pts, pts), BF16),
        V((wide, wide), BF16), V((wide, wide), BF16),
        V((deep, LANES), BF16), V((deep, LANES), BF16),
        V((pts, LANES), BF16), V((pts, LANES), BF16),
        V((LANES, pts), BF16), V((LANES, pts), BF16),
        V((APPLIES, rows, pts), F32), V((rows, pts), F32), V((rows, pts), F32),
        V((APPLIES, 2, rows, pts), F32),
        V((APPLIES, n_lvl, 2, 8, LANES), F32), V((APPLIES, n_lvl, 2, 8, LANES), F32),
        V((APPLIES, 8, LANES), F32), V((APPLIES, n_leaf, 8, LANES), F32),
        V((APPLIES, n_lvl, 2, 8, LANES), F32), V((APPLIES, n_lvl, 2, 8, LANES), F32),
        V((rows, LANES), F32), V((2, rows, LANES), F32),
        pltpu.SemaphoreType.DMA((8,)), pltpu.SemaphoreType.DMA((8,)),
        pltpu.SemaphoreType.DMA((APPLIES, 5)), pltpu.SemaphoreType.DMA((APPLIES, 2)),
        pltpu.SemaphoreType.DMA((APPLIES, 3)),
    ]
    out = jax.ShapeDtypeStruct((rows, pts), F32)
    body = lambda *refs: kernel((n_leaf, n_lvl), *refs)
    return pl.pallas_call(
        body,
        out_shape=(out, out),
        in_specs=[vmem] * 8 + [smem] * 3,
        out_specs=(vmem, vmem),
        scratch_shapes=scratch,
        compiler_params=pltpu.CompilerParams(
            collective_id=0, has_side_effects=True, vmem_limit_bytes=48 * 1024 * 1024
        ),
    )(
        targets, tree_pos.reshape(1, pts), coords, ubasis, transfer_one, transfer_two,
        anchors_one, anchors_two, near_list, far_one, far_two,
    )


def solution(mesh):
    both = ("leaf", "lvl")
    return jax.shard_map(
        on_device,
        mesh=mesh,
        in_specs=(
            P(None, both), P(both), P(None, both), P(both, None, None), P(both, None, None),
            P(both, None, None), P(both, None, None), P("leaf", None, None),
            P(both, None), P(both, None), P("leaf", None),
        ),
        out_specs=(P(None, both), P(None, both)),
        check_vma=False,
    )
```

```python
import jax
import jax.numpy as jnp
from jax import lax
from jax.experimental import pallas as pl
from jax.experimental.pallas import tpu as pltpu
from jax.sharding import PartitionSpec as P

F32 = jnp.float32
BF16 = jnp.bfloat16
MESH = pl.DeviceIdType.MESH
PRECISE = lax.Precision.HIGHEST
DIM = 8
RIDGE = 1.0
EPSILON = 1e-6
APPLIES = 5
LANES = 128


def dot(a, b, ca=1, cb=0):
    return lax.dot_general(a, b, (((ca,), (cb,)), ((), ())), preferred_element_type=F32)


def dot_precise(a, b):
    return lax.dot_general(
        a, b, (((1,), (0,)), ((), ())), precision=PRECISE, preferred_element_type=F32
    )


def split2(x):
    hi = x.astype(BF16)
    return hi, (x - hi.astype(F32)).astype(BF16)


def split3(x):
    hi = x.astype(BF16)
    rest = x - hi.astype(F32)
    mid = rest.astype(BF16)
    return hi, mid, (rest - mid.astype(F32)).astype(BF16)


def dot_split(a, b_hi, b_lo):
    rows = a.shape[0]
    a_hi, a_lo = split2(a)
    both = dot(jnp.concatenate([a_hi, a_lo], axis=0), b_hi)
    return both[:rows] + both[rows:] + dot(a_hi, b_lo)


def iota(shape, dim):
    return lax.broadcasted_iota(jnp.int32, shape, dim)


def augmented(x):
    n = x.shape[1]
    x1, x2, x3 = (p.astype(F32) for p in split3(x))
    sq = jnp.sum(x * x, axis=0, keepdims=True) * (-1.0 / DIM)
    n1, n2, n3 = (p.astype(F32) for p in split3(sq))
    row = iota((8, n), 0)
    lead = jnp.where(row == 0, n1, jnp.where(row == 1, n2, n3))
    tail = jnp.where(row == 3, n1, jnp.where(row == 4, n2, n3))
    zero = jnp.zeros((8, n), F32)
    src_norm = jnp.where(row < 3, lead, jnp.where(row < 6, 1.0, 0.0))
    dst_norm = jnp.where(row < 3, 1.0, jnp.where(row < 6, tail, 0.0))
    q = 2.0 / DIM
    src = jnp.concatenate([x1, x1, x2, x1, x3, x2, src_norm, zero], axis=0)
    dst = jnp.concatenate([x1 * q, x2 * q, x1 * q, x3 * q, x1 * q, x2 * q, dst_norm, zero], axis=0)
    return src, dst


def pack(onehot, x):
    total = None
    for part in split3(x):
        zero = jnp.zeros_like(part)
        wide = jnp.concatenate(
            [jnp.concatenate([part, zero], axis=1), jnp.concatenate([zero, part], axis=1)], axis=0
        )
        term = dot(onehot, wide, 1, 1)
        total = term if total is None else total + term
    return total


def unpack(onehot, g):
    half = g.shape[1] // 2
    cols = onehot.shape[1] // 2
    gt = jnp.transpose(g)
    total = None
    for part in split3(gt):
        term = dot(part, onehot)
        total = term if total is None else total + term
    return total[:half, :cols] + total[half:, cols:]


def kernel(
    sizes,
    targets_h, tree_pos_h, coords_h, ubasis_h, transfer_one_h, transfer_two_h, anchors_one_h,
    anchors_two_h, near_list, far_one, far_two,
    coeffs, residual,
    targets, tree_pos, coords, ubasis, transfer_one, transfer_two, anchors_one, anchors_two,
    oh_user, oh_tree, s_a, r_a, s_b, r_b, s_c, r_c, s_d, r_d,
    r_coords, s_anch, r_anch, s_top, r_top, s_g, r_g, ct_full, r_ct,
    src_pts, w_hi, w_lo, k1_hi, k1_lo, k2_hi, k2_lo, c_hi, c_lo, ct_hi, ct_lo, m_hi, m_lo,
    tg_hi, tg_lo,
    wbuf, acc, r_halo, qbuf, s1, r1, s2, r2, s3, r3,
    in_sem, set_send, set_recv, halo_send, halo_recv, send1, recv1, send2, recv2, send3, recv3,
):
    n_leaf, n_lvl = sizes
    n_dev = n_leaf * n_lvl
    leaf, lvl = lax.axis_index("leaf"), lax.axis_index("lvl")
    rows, pts = targets.shape
    clusters = ubasis.shape[0]
    points = ubasis.shape[2]
    ranks = ubasis.shape[1]
    half = LANES // 2
    total = n_dev * clusters
    near_lists = near_list.shape[1]
    lower_count = far_one.shape[1]
    upper_count = far_two.shape[1]

    inputs = []
    pairs = (
        (tree_pos_h, tree_pos), (targets_h, targets), (transfer_one_h, transfer_one),
        (ubasis_h, ubasis), (transfer_two_h, transfer_two), (coords_h, coords),
        (anchors_one_h, anchors_one), (anchors_two_h, anchors_two),
    )
    for k, (hbm, vmem) in enumerate(pairs):
        inputs.append(pltpu.make_async_copy(hbm, vmem, in_sem.at[k]))
        inputs[-1].start()

    def lvl_peer(k):
        return lax.rem(lvl + k, n_lvl)

    def leaf_peer(k):
        return lax.rem(leaf + k, n_leaf)

    ring = leaf * n_lvl + lvl
    after = lax.rem(ring + 1, n_dev)
    before = lax.rem(ring + n_dev - 1, n_dev)
    after_id = (after // n_lvl, lax.rem(after, n_lvl))
    before_id = (before // n_lvl, lax.rem(before, n_lvl))

    def copy(src, dst, send, recv, device):
        pltpu.make_async_remote_copy(
            src_ref=src, dst_ref=dst, send_sem=send, recv_sem=recv,
            device_id=device, device_id_type=MESH,
        ).start()

    def wait(ref, sem):
        pltpu.make_async_copy(ref, ref, sem).wait()

    def over_lvl(src, dst, send, recv):
        for k in range(1, n_lvl):
            peer = lvl_peer(k)
            copy(src(peer), dst, send, recv, (leaf, peer))

    def over_leaf(src, dst, send, recv):
        for k in range(1, n_leaf):
            peer = leaf_peer(k)
            copy(src(peer), dst, send, recv, (peer, lvl))

    barrier = pltpu.get_barrier_semaphore()
    for k in range(1, n_leaf):
        pl.semaphore_signal(barrier, inc=1, device_id=(leaf_peer(k), lvl), device_id_type=MESH)
    for k in range(1, n_lvl):
        pl.semaphore_signal(barrier, inc=1, device_id=(leaf, lvl_peer(k)), device_id_type=MESH)
    pl.semaphore_signal(barrier, inc=1, device_id=after_id, device_id_type=MESH)
    pl.semaphore_signal(barrier, inc=1, device_id=before_id, device_id_type=MESH)

    lane = iota((8, LANES), 1)
    low = lane < half
    row8 = iota((8, LANES), 0)
    low_rows = iota((rows, LANES), 1) < half

    inputs[0].wait()
    tp = tree_pos[...]
    dest = lax.div(tp, pts)
    place = lax.rem(dest, n_lvl) * n_leaf + lax.div(dest, n_lvl)
    hit = iota((n_dev, pts), 0) == place
    hit16 = hit.astype(F32).astype(BF16)
    earlier = (iota((pts, pts), 0) < iota((pts, pts), 1)).astype(F32).astype(BF16)
    seen = dot(hit16, earlier)
    oh_user[:, :pts] = jnp.where(hit & (seen < 0.5), 1.0, 0.0).astype(BF16)
    oh_user[:, pts:] = jnp.where(hit & (seen > 0.5), 1.0, 0.0).astype(BF16)
    inputs[1].wait()
    s_a[:, 0] = pack(oh_user[...], targets[...]).reshape(n_lvl, n_leaf, LANES)
    pos = jnp.broadcast_to(lax.rem(tp, pts).astype(F32), (rows, pts))
    s_a[:, 1] = pack(oh_user[...], pos).reshape(n_lvl, n_leaf, LANES)
    r_a[lvl] = s_a[lvl]

    for k in range(2, len(pairs)):
        inputs[k].wait()
    own_one = jnp.concatenate([anchors_one[0], anchors_one[0]], axis=1)
    own_two = jnp.concatenate([anchors_two[0], anchors_two[0]], axis=1)
    partner = jnp.full((8, LANES), -1.0, F32)
    for k in range(lower_count):
        value = lax.rem(far_one[0, k], n_lvl).astype(F32)
        partner = jnp.where(row8 == k, value, partner)
    s_anch[0] = own_one
    s_anch[1] = partner
    r_anch[lvl] = s_anch[...]
    partner = jnp.full((8, LANES), -1.0, F32)
    for k in range(upper_count):
        partner = jnp.where(row8 == k, far_two[0, k].astype(F32), partner)
    s_top[0] = own_two
    s_top[1] = partner
    r_top[leaf] = s_top[...]

    pl.semaphore_wait(barrier, n_lvl + n_leaf)

    over_lvl(lambda p: s_a.at[p], r_a.at[lvl], set_send.at[0], set_recv.at[0])
    copy(coords, r_coords.at[0], set_send.at[1], set_recv.at[1], after_id)
    copy(coords, r_coords.at[1], set_send.at[2], set_recv.at[2], before_id)
    over_lvl(lambda p: s_anch, r_anch.at[lvl], set_send.at[3], set_recv.at[3])
    over_leaf(lambda p: s_top, r_top.at[leaf], set_send.at[4], set_recv.at[4])

    bt = jnp.concatenate(
        [dot_precise(jnp.transpose(transfer_one[c]), ubasis[c]) for c in range(clusters)], axis=1
    )
    b2t = dot_precise(jnp.transpose(transfer_two[0]), bt)
    ct = jnp.concatenate([bt, b2t], axis=0)
    c = jnp.transpose(ct)
    ct_full[...] = b2t
    ct_hi[...], ct_lo[...] = split2(ct)
    c_hi[...], c_lo[...] = split2(c)
    s_g[...] = dot_split(b2t, c_hi[...], c_lo[...])
    r_g[lvl] = s_g[...]

    wait(r_a.at[pl.ds(0, n_lvl - 1)], set_recv.at[0])
    for kind in range(2):
        s_b[:, kind] = jnp.swapaxes(r_a[:, kind], 0, 1)
    r_b[leaf] = s_b[leaf]
    over_leaf(lambda p: s_b.at[p], r_b.at[leaf], set_send.at[5], set_recv.at[5])
    over_lvl(lambda p: s_g, r_g.at[lvl], set_send.at[8], set_recv.at[8])
    copy(ct_full, r_ct.at[0], set_send.at[6], set_recv.at[6], after_id)
    copy(ct_full, r_ct.at[1], set_send.at[7], set_recv.at[7], before_id)

    wait(r_coords.at[0], set_recv.at[1])
    wait(r_coords.at[1], set_recv.at[2])
    src, dst = augmented(coords[...])
    src_pts[pts : 2 * pts] = jnp.transpose(src).astype(BF16)
    src_pts[:pts] = jnp.transpose(augmented(r_coords[0])[0]).astype(BF16)
    src_pts[2 * pts :] = jnp.transpose(augmented(r_coords[1])[0]).astype(BF16)
    dst = dst.astype(BF16)
    first = ring * clusters - clusters
    near_scale = (points * (near_lists + 1)) ** (-0.5)

    def near_rows(n, carry):
        at = pl.ds(pl.multiple_of(n * points, points), points)
        value = jnp.exp(dot(src_pts[at, :], dst))
        parts = []
        for c in range(clusters):
            weight = (n == c + clusters).astype(jnp.int32)
            for k in range(near_lists):
                rel = lax.rem(near_list[c, k] - first + total, total)
                weight = weight + (rel == n).astype(jnp.int32)
            scaled = weight.astype(F32) * near_scale
            parts.append(value[:, c * points : (c + 1) * points] * scaled)
        hi, lo = split2(jnp.concatenate(parts, axis=1))
        w_hi[at, :] = hi
        w_lo[at, :] = lo
        return carry

    lax.fori_loop(0, 3 * clusters, near_rows, 0)

    def lanes_of(get):
        tiles = []
        for m in range(n_lvl // 2):
            tiles.append(jnp.where(low, get(2 * m), get(2 * m + 1)))
        return jnp.concatenate(tiles, axis=1)

    wait(r_anch.at[pl.ds(0, n_lvl - 1)], set_recv.at[3])
    src, dst = augmented(lanes_of(lambda p: r_anch[p, 0]))
    wide = n_lvl * ranks
    partners = lanes_of(lambda p: r_anch[p, 1])
    owner = lax.div(iota((wide, wide), 0), ranks).astype(F32)
    count = jnp.zeros((wide, wide), F32)
    for k in range(lower_count):
        count = count + jnp.where(owner == partners[k : k + 1], 1.0, 0.0)
    value = jnp.exp(dot(jnp.transpose(src).astype(BF16), dst.astype(BF16)))
    k1_hi[...], k1_lo[...] = split2(value * count * (lower_count ** (-0.5)))

    wait(r_top.at[pl.ds(0, n_leaf - 1)], set_recv.at[4])
    groups = (leaf, leaf_peer(n_leaf - 1), leaf_peer(1))

    def chosen(lists, get):
        named = [jnp.broadcast_to(lists[k : k + 1], (8, LANES)) for k in range(upper_count)]
        picks = [get(0)] * upper_count
        for q in range(1, n_leaf):
            value = get(q)
            picks = [jnp.where(n == float(q), value, p) for n, p in zip(named, picks)]
        return picks

    for g, group in enumerate(groups):
        tops = chosen(r_top[group, 1], lambda q: r_top[q, 0])
        src, _ = augmented(
            jnp.concatenate([jnp.where(low, tops[m], tops[m + 1]) for m in (0, 2)], axis=1)
        )
        _, dst = augmented(r_top[group, 0])
        value = jnp.exp(dot(jnp.transpose(src).astype(BF16), dst.astype(BF16)))
        first_half = iota(value.shape, 1) < half
        value = jnp.where(first_half, 0.0, value) if g == 0 else jnp.where(first_half, value, 0.0)
        k2_hi[g], k2_lo[g] = split2(value * (upper_count ** (-0.5)))

    wait(r_g.at[pl.ds(0, n_lvl - 1)], set_recv.at[8])
    low_ranks = iota((ranks, LANES), 1) < half
    gamma = r_g[0]
    for p in range(1, n_lvl):
        gamma = gamma + r_g[p]
    tiles = [
        jnp.where(low_ranks, r_g[2 * m], pltpu.roll(r_g[2 * m + 1], half, 1))
        for m in range(n_lvl // 2)
    ]
    tiles.append(jnp.where(low_ranks, 0.0, gamma))
    tg = jnp.concatenate(tiles, axis=1)
    tg_hi[...], tg_lo[...] = split2(jnp.concatenate([jnp.zeros_like(tg), tg], axis=0))
    wait(r_ct.at[0], set_recv.at[6])
    wait(r_ct.at[1], set_recv.at[7])
    z_own = dot_split(ct_full[...], w_hi[pts : 2 * pts], w_lo[pts : 2 * pts])
    z_prev = dot_split(r_ct[0], w_hi[:pts], w_lo[:pts])
    z_next = dot_split(r_ct[1], w_hi[2 * pts :], w_lo[2 * pts :])
    at_first = (lvl == 0).astype(F32)
    at_last = (lvl == n_lvl - 1).astype(F32)
    z_main = z_own + z_prev * (1.0 - at_first) + z_next * (1.0 - at_last)
    z_edge = z_prev * at_first + z_next * at_last
    m_hi[...], m_lo[...] = split2(
        jnp.concatenate([bt, z_main, z_edge, jnp.zeros_like(z_edge)], axis=0)
    )

    wait(r_b.at[pl.ds(0, n_leaf - 1)], set_recv.at[5])
    got_pos = r_b[:, 1].reshape(n_dev, LANES).astype(jnp.int32)
    column = iota((n_dev, pts), 1)
    oh_tree[:, :pts] = jnp.where(column == got_pos[:, 0:1], 1.0, 0.0).astype(BF16)
    oh_tree[:, pts:] = jnp.where(column == got_pos[:, half : half + 1], 1.0, 0.0).astype(BF16)
    wbuf[0] = unpack(oh_tree[...], r_b[:, 0].reshape(n_dev, LANES))

    def send_halo(j):
        copy(wbuf.at[j], r_halo.at[j, 0], halo_send.at[j, 0], halo_recv.at[j, 0], after_id)
        copy(wbuf.at[j], r_halo.at[j, 1], halo_send.at[j, 1], halo_recv.at[j, 1], before_id)

    def scatter(j, value):
        s1[j] = value.reshape(n_lvl, 8, LANES)
        r1[j, lvl] = s1[j, lvl]
        over_lvl(lambda peer: s1.at[j, peer], r1.at[j, lvl], send1.at[j], recv1.at[j])

    def broadcast(j, value):
        s2[j] = value
        r2[j, leaf] = value
        over_leaf(lambda peer: s2.at[j], r2.at[j, leaf], send2.at[j], recv2.at[j])

    def gather(j):
        r3[j, lvl] = s3[j, lvl]
        over_lvl(lambda peer: s3.at[j, peer], r3.at[j, lvl], send3.at[j], recv3.at[j])

    def wait1(j):
        wait(r1.at[j, pl.ds(0, n_lvl - 1)], recv1.at[j])

    def wait2(j):
        wait(r2.at[j, pl.ds(0, n_leaf - 1)], recv2.at[j])

    def wait3(j):
        wait(r3.at[j, pl.ds(0, n_lvl - 1)], recv3.at[j])

    def send_potentials(j, f1, f2, edges):
        for d in range(n_lvl):
            tile = jnp.zeros((8, LANES), F32)
            if f1 is not None:
                tile = f1[:, (d // 2) * LANES : (d // 2 + 1) * LANES]
                if d % 2:
                    tile = pltpu.roll(tile, half, 1)
            s3[j, d, 0] = jnp.where(low, tile, f2)
            s3[j, d, 1] = edges[0] if d == 0 else edges[1] if d == n_lvl - 1 else jnp.zeros_like(f2)
        gather(j)

    def level_one(own, extra):
        tiles = [
            jnp.where(low, own[2 * m], pltpu.roll(own[2 * m + 1], half, 1))
            for m in range(n_lvl // 2)
        ]
        t = jnp.concatenate(tiles, axis=1)
        if extra is not None:
            t = t + extra
        return dot_split(t, k1_hi[...], k1_lo[...])

    def return_leaf(kind, value):
        s_c[kind] = pack(oh_tree[...], value).reshape(n_leaf, n_lvl, LANES)
        r_c[kind, leaf] = s_c[kind, leaf]
        over_leaf(
            lambda p: s_c.at[kind, p], r_c.at[kind, leaf], set_send.at[9 + kind], set_recv.at[9 + kind]
        )

    def return_lvl(kind):
        wait(r_c.at[kind, pl.ds(0, n_leaf - 1)], set_recv.at[9 + kind])
        s_d[kind] = jnp.swapaxes(r_c[kind], 0, 1)
        r_d[kind, lvl] = s_d[kind, lvl]
        over_lvl(
            lambda p: s_d.at[kind, p], r_d.at[kind, lvl], set_send.at[12 + kind], set_recv.at[12 + kind]
        )

    def returned(kind):
        wait(r_d.at[kind, pl.ds(0, n_lvl - 1)], set_recv.at[12 + kind])
        return unpack(oh_user[...], r_d[kind].reshape(n_dev, LANES))

    zero8 = jnp.zeros((8, LANES), F32)
    scatter(0, dot_split(wbuf[0], c_hi[...], c_lo[...]))
    send_halo(0)
    wait1(0)
    got = r1[0]
    broadcast(0, jnp.sum(got, axis=0))
    send_potentials(0, level_one(got, None), zero8, (zero8, zero8))

    def body(j, last):
        near = dot_split(wbuf[j], w_hi[pts : 2 * pts], w_lo[pts : 2 * pts])
        wait(r_halo.at[j, 0], halo_recv.at[j, 0])
        near = near + dot_split(r_halo[j, 0], w_hi[:pts], w_lo[:pts])
        wait(r_halo.at[j, 1], halo_recv.at[j, 1])
        acc[...] = near + dot_split(r_halo[j, 1], w_hi[2 * pts :], w_lo[2 * pts :])

        wait3(j)
        main = r3[j, :, 0].reshape(rows, LANES)
        edge = r3[j, :, 1].reshape(rows, LANES)
        moved = dot_split(jnp.concatenate([main, edge], axis=1), m_hi[...], m_lo[...])
        w_next = acc[...] + moved
        wbuf[j + 1] = w_next
        if not last:
            scatter(j + 1, dot_split(w_next, c_hi[...], c_lo[...]))
            send_halo(j + 1)
        power = wbuf[j] + dot_split(jnp.where(low_rows, 0.0, main), ct_hi[...], ct_lo[...])
        square = jnp.sum(power * power, axis=1, keepdims=True)
        if last:
            part = iota((rows, LANES), 1) // (LANES // 4)
            sums = jnp.where(part == 3, square, 0.0)
            for k in range(3):
                sums = jnp.where(part == k, qbuf[k + 1], sums)
            scatter(j + 1, sums)
            return_lvl(1)
        else:
            qbuf[j] = jnp.broadcast_to(square, (rows, LANES))

            @pl.when(j == 1)
            def _():
                return_leaf(0, power)

            @pl.when(j == 2)
            def _():
                return_lvl(0)

            @pl.when(j == 3)
            def _():
                return_leaf(1, power)

        wait2(j)
        potentials = []
        for g, group in enumerate(groups):
            ups = chosen(r_top[group, 1], lambda q: r2[j, q])
            tiles = [jnp.where(low, pltpu.roll(ups[m], half, 1), ups[m + 1]) for m in (0, 2)]
            potentials.append(dot_split(jnp.concatenate(tiles, axis=1), k2_hi[g], k2_lo[g]))
        f2, edges = potentials[0], potentials[1:]
        if last:
            send_potentials(j + 1, None, f2, edges)
            wait1(j + 1)
            broadcast(j + 1, jnp.sum(r1[j + 1], axis=0))
            return
        add = dot_split(f2, tg_hi[...], tg_lo[...])
        wait1(j + 1)
        got = r1[j + 1]
        broadcast(j + 1, jnp.sum(got, axis=0) + add[:, wide:])
        send_potentials(j + 1, level_one(got, add[:, :wide]), f2, edges)

    def step(j, carry):
        body(j, False)
        return carry

    lax.fori_loop(0, APPLIES - 1, step, 0)
    body(APPLIES - 1, True)

    wait3(APPLIES)
    main = r3[APPLIES, :, 0].reshape(rows, LANES)
    return_leaf(
        2, wbuf[APPLIES] + dot_split(jnp.where(low_rows, 0.0, main), ct_hi[...], ct_lo[...])
    )
    back1 = returned(0)
    back3 = returned(1)
    wait2(APPLIES)
    sums = jnp.sum(r2[APPLIES], axis=0)
    for d in range(n_lvl):
        s3[APPLIES + 1, d, 0] = sums
        s3[APPLIES + 1, d, 1] = sums
    gather(APPLIES + 1)
    return_lvl(2)

    wait3(APPLIES + 1)
    sums = r3[APPLIES + 1, :, 0].reshape(rows, LANES)
    g1, g2, g3, g4 = (sums[:, k * (LANES // 4) : k * (LANES // 4) + 1] for k in range(4))
    step0 = g1 / (g2 + RIDGE * g1 + EPSILON)
    keep = 1.0 - RIDGE * step0
    fresh = keep * keep * g1 - 2.0 * step0 * keep * g2 + step0 * step0 * g3
    lead = keep + fresh / (g1 + EPSILON)
    direction_sq = lead * lead * g1 - 2.0 * lead * step0 * g2 + step0 * step0 * g3
    image_sq = lead * lead * g2 - 2.0 * lead * step0 * g3 + step0 * step0 * g4
    step1 = fresh / (image_sq + RIDGE * direction_sq + EPSILON)
    coeffs[...] = (step0 + step1 * lead) * back1 - (step1 * step0) * back3
    partial = (keep - RIDGE * step1 * lead) * back1 - (
        step0 + step1 * (lead - RIDGE * step0)
    ) * back3
    residual[...] = partial + (step1 * step0) * returned(2)

    wait(r_a.at[pl.ds(0, n_lvl - 1)], set_send.at[0])
    wait(r_coords.at[0], set_send.at[1])
    wait(r_coords.at[1], set_send.at[2])
    wait(r_anch.at[pl.ds(0, n_lvl - 1)], set_send.at[3])
    wait(r_top.at[pl.ds(0, n_leaf - 1)], set_send.at[4])
    wait(r_b.at[pl.ds(0, n_leaf - 1)], set_send.at[5])
    wait(r_ct.at[0], set_send.at[6])
    wait(r_ct.at[1], set_send.at[7])
    wait(r_g.at[pl.ds(0, n_lvl - 1)], set_send.at[8])
    for kind in range(3):
        wait(r_c.at[kind, pl.ds(0, n_leaf - 1)], set_send.at[9 + kind])
        wait(r_d.at[kind, pl.ds(0, n_lvl - 1)], set_send.at[12 + kind])

    def sent(j, carry):
        wait(r1.at[j, pl.ds(0, n_lvl - 1)], send1.at[j])
        wait(r2.at[j, pl.ds(0, n_leaf - 1)], send2.at[j])
        return carry

    lax.fori_loop(0, APPLIES + 1, sent, 0)

    def sent_halo(j, carry):
        wait(wbuf.at[j], halo_send.at[j, 0])
        wait(wbuf.at[j], halo_send.at[j, 1])
        return carry

    lax.fori_loop(0, APPLIES, sent_halo, 0)

    def sent_last(j, carry):
        wait(r3.at[j, pl.ds(0, n_lvl - 1)], send3.at[j])
        return carry

    lax.fori_loop(0, APPLIES + 2, sent_last, 0)


def on_device(
    targets, tree_pos, coords, ubasis, transfer_one, transfer_two, anchors_one, anchors_two,
    near_list, far_one, far_two,
):
    rows, pts = targets.shape
    n_leaf, n_lvl = lax.axis_size("leaf"), lax.axis_size("lvl")
    n_dev = n_leaf * n_lvl
    dim = coords.shape[0]
    ranks = anchors_one.shape[2]
    hbm = pl.BlockSpec(memory_space=pl.ANY)
    vmem = pl.BlockSpec(memory_space=pltpu.VMEM)
    smem = pl.BlockSpec(memory_space=pltpu.SMEM)
    V = pltpu.VMEM
    D = pltpu.SemaphoreType.DMA
    wide = n_lvl * ranks
    deep = far_two.shape[1] * ranks
    arrays = (
        targets, tree_pos.reshape(1, pts), coords, ubasis, transfer_one, transfer_two,
        anchors_one, anchors_two,
    )
    scratch = [V(a.shape, a.dtype) for a in arrays] + [
        V((n_dev, 2 * pts), BF16), V((n_dev, 2 * pts), BF16),
        V((n_lvl, 2, n_leaf, LANES), F32), V((n_lvl, 2, n_leaf, LANES), F32),
        V((n_leaf, 2, n_lvl, LANES), F32), V((n_leaf, 2, n_lvl, LANES), F32),
        V((3, n_leaf, n_lvl, LANES), F32), V((3, n_leaf, n_lvl, LANES), F32),
        V((3, n_lvl, n_leaf, LANES), F32), V((3, n_lvl, n_leaf, LANES), F32),
        V((2, dim, pts), F32),
        V((2, 8, LANES), F32), V((n_lvl, 2, 8, LANES), F32),
        V((2, 8, LANES), F32), V((n_leaf, 2, 8, LANES), F32),
        V((ranks, LANES), F32), V((n_lvl, ranks, LANES), F32),
        V((ranks, pts), F32), V((2, ranks, pts), F32),
        V((3 * pts, 64), BF16),
        V((3 * pts, pts), BF16), V((3 * pts, pts), BF16),
        V((wide, wide), BF16), V((wide, wide), BF16),
        V((3, deep, LANES), BF16), V((3, deep, LANES), BF16),
        V((pts, LANES), BF16), V((pts, LANES), BF16),
        V((LANES, pts), BF16), V((LANES, pts), BF16),
        V((2 * LANES, pts), BF16), V((2 * LANES, pts), BF16),
        V((LANES, wide + LANES), BF16), V((LANES, wide + LANES), BF16),
        V((APPLIES + 1, rows, pts), F32), V((rows, pts), F32),
        V((APPLIES, 2, rows, pts), F32), V((APPLIES - 1, rows, LANES), F32),
        V((APPLIES + 1, n_lvl, 8, LANES), F32), V((APPLIES + 1, n_lvl, 8, LANES), F32),
        V((APPLIES + 1, 8, LANES), F32), V((APPLIES + 1, n_leaf, 8, LANES), F32),
        V((APPLIES + 2, n_lvl, 2, 8, LANES), F32), V((APPLIES + 2, n_lvl, 2, 8, LANES), F32),
        D((len(arrays),)), D((15,)), D((15,)),
        D((APPLIES, 2)), D((APPLIES, 2)),
        D((APPLIES + 1,)), D((APPLIES + 1,)), D((APPLIES + 1,)), D((APPLIES + 1,)),
        D((APPLIES + 2,)), D((APPLIES + 2,)),
    ]
    out = jax.ShapeDtypeStruct((rows, pts), F32)
    body = lambda *refs: kernel((n_leaf, n_lvl), *refs)
    return pl.pallas_call(
        body,
        out_shape=(out, out),
        in_specs=[hbm] * len(arrays) + [smem] * 3,
        out_specs=(vmem, vmem),
        scratch_shapes=scratch,
        compiler_params=pltpu.CompilerParams(
            collective_id=0, has_side_effects=True, vmem_limit_bytes=56 * 1024 * 1024
        ),
    )(*arrays, near_list, far_one, far_two)


def solution(mesh):
    both = ("leaf", "lvl")
    return jax.shard_map(
        on_device,
        mesh=mesh,
        in_specs=(
            P(None, both), P(both), P(None, both), P(both, None, None), P(both, None, None),
            P(both, None, None), P(both, None, None), P("leaf", None, None),
            P(both, None), P(both, None), P("leaf", None),
        ),
        out_specs=(P(None, both), P(None, both)),
        check_vma=False,
    )
```

```python
import jax
import jax.numpy as jnp
from jax import lax
from jax.experimental import pallas as pl
from jax.experimental.pallas import tpu as pltpu
from jax.sharding import PartitionSpec as P

F32 = jnp.float32
BF16 = jnp.bfloat16
MESH = pl.DeviceIdType.MESH
PRECISE = lax.Precision.HIGHEST
DIM = 8
RIDGE = 1.0
EPSILON = 1e-6
APPLIES = 5
LANES = 128


def dot(a, b, ca=1, cb=0):
    return lax.dot_general(a, b, (((ca,), (cb,)), ((), ())), preferred_element_type=F32)


def dot_precise(a, b):
    return lax.dot_general(
        a, b, (((1,), (0,)), ((), ())), precision=PRECISE, preferred_element_type=F32
    )


def split2(x):
    hi = x.astype(BF16)
    return hi, (x - hi.astype(F32)).astype(BF16)


def split3(x):
    hi = x.astype(BF16)
    rest = x - hi.astype(F32)
    mid = rest.astype(BF16)
    return hi, mid, (rest - mid.astype(F32)).astype(BF16)


def dot_split(a, b_hi, b_lo):
    rows = a.shape[0]
    a_hi, a_lo = split2(a)
    both = dot(jnp.concatenate([a_hi, a_lo], axis=0), b_hi)
    return both[:rows] + both[rows:] + dot(a_hi, b_lo)


def iota(shape, dim):
    return lax.broadcasted_iota(jnp.int32, shape, dim)


def augmented(x):
    n = x.shape[1]
    x1, x2, x3 = (p.astype(F32) for p in split3(x))
    sq = jnp.sum(x * x, axis=0, keepdims=True) * (-1.0 / DIM)
    n1, n2, n3 = (p.astype(F32) for p in split3(sq))
    row = iota((8, n), 0)
    lead = jnp.where(row == 0, n1, jnp.where(row == 1, n2, n3))
    tail = jnp.where(row == 3, n1, jnp.where(row == 4, n2, n3))
    zero = jnp.zeros((8, n), F32)
    src_norm = jnp.where(row < 3, lead, jnp.where(row < 6, 1.0, 0.0))
    dst_norm = jnp.where(row < 3, 1.0, jnp.where(row < 6, tail, 0.0))
    q = 2.0 / DIM
    src = jnp.concatenate([x1, x1, x2, x1, x3, x2, src_norm, zero], axis=0)
    dst = jnp.concatenate([x1 * q, x2 * q, x1 * q, x3 * q, x1 * q, x2 * q, dst_norm, zero], axis=0)
    return src, dst


def pack(onehot, x):
    total = None
    for part in split3(x):
        zero = jnp.zeros_like(part)
        wide = jnp.concatenate(
            [jnp.concatenate([part, zero], axis=1), jnp.concatenate([zero, part], axis=1)], axis=0
        )
        term = dot(onehot, wide, 1, 1)
        total = term if total is None else total + term
    return total


def unpack(onehot, g):
    half = g.shape[1] // 2
    cols = onehot.shape[1] // 2
    gt = jnp.transpose(g)
    total = None
    for part in split3(gt):
        term = dot(part, onehot)
        total = term if total is None else total + term
    return total[:half, :cols] + total[half:, cols:]


def kernel(
    sizes,
    targets_h, tree_pos_h, coords_h, ubasis_h, transfer_one_h, transfer_two_h, anchors_one_h,
    anchors_two_h, near_list, far_one, far_two,
    coeffs, residual,
    targets, tree_pos, coords, ubasis, transfer_one, transfer_two, anchors_one, anchors_two,
    oh_user, oh_tree, s_a, r_a, s_b, r_b, s_c, r_c, s_d, r_d,
    r_coords, s_anch, r_anch, s_top, r_top, s_g, r_g, ct_full, r_ct,
    src_pts, w_hi, w_lo, k1_hi, k1_lo, k2_hi, k2_lo, c_hi, c_lo, ct_hi, ct_lo, m_hi, m_lo,
    tg_hi, tg_lo,
    wbuf, acc, r_halo, qbuf, s1, r1, s2, r2, s3, r3,
    in_sem, set_send, set_recv, halo_send, halo_recv, send1, recv1, send2, recv2, send3, recv3,
):
    n_leaf, n_lvl = sizes
    n_dev = n_leaf * n_lvl
    leaf, lvl = lax.axis_index("leaf"), lax.axis_index("lvl")
    rows, pts = targets.shape
    clusters = ubasis.shape[0]
    points = ubasis.shape[2]
    ranks = ubasis.shape[1]
    half = LANES // 2
    total = n_dev * clusters
    near_lists = near_list.shape[1]
    lower_count = far_one.shape[1]
    upper_count = far_two.shape[1]

    inputs = []
    pairs = (
        (tree_pos_h, tree_pos), (targets_h, targets), (transfer_one_h, transfer_one),
        (ubasis_h, ubasis), (transfer_two_h, transfer_two), (coords_h, coords),
        (anchors_one_h, anchors_one), (anchors_two_h, anchors_two),
    )
    for k, (hbm, vmem) in enumerate(pairs):
        inputs.append(pltpu.make_async_copy(hbm, vmem, in_sem.at[k]))
        inputs[-1].start()

    chips_z, cores = 8, 2
    chips_y, chips_x = n_leaf // chips_z, n_lvl // cores

    def others(long, short):
        pairs = [(a, b) for a in range(long) for b in range(short)][1:]
        far = lambda p: min(p[0], long - p[0]) + min(p[1], short - p[1]) * (short > 2)
        return sorted(pairs, key=lambda p: -far(p))

    def shifted(index, short, long, a, b):
        return lax.rem(index // short + a, long) * short + lax.rem(lax.rem(index, short) + b, short)

    leaf_peers = [shifted(leaf, chips_z, chips_y, a, b) for a, b in others(chips_y, chips_z)]
    lvl_peers = [shifted(lvl, cores, chips_x, a, b) for a, b in others(chips_x, cores)]
    leaf_before, leaf_after = lax.rem(leaf + n_leaf - 1, n_leaf), lax.rem(leaf + 1, n_leaf)

    ring = leaf * n_lvl + lvl
    after = lax.rem(ring + 1, n_dev)
    before = lax.rem(ring + n_dev - 1, n_dev)
    after_id = (after // n_lvl, lax.rem(after, n_lvl))
    before_id = (before // n_lvl, lax.rem(before, n_lvl))

    def copy(src, dst, send, recv, device):
        pltpu.make_async_remote_copy(
            src_ref=src, dst_ref=dst, send_sem=send, recv_sem=recv,
            device_id=device, device_id_type=MESH,
        ).start()

    def wait(ref, sem):
        pltpu.make_async_copy(ref, ref, sem).wait()

    def over_lvl(src, dst, send, recv):
        for peer in lvl_peers:
            copy(src(peer), dst, send, recv, (leaf, peer))

    def over_leaf(src, dst, send, recv):
        for peer in leaf_peers:
            copy(src(peer), dst, send, recv, (peer, lvl))

    barrier = pltpu.get_barrier_semaphore()
    for peer in leaf_peers:
        pl.semaphore_signal(barrier, inc=1, device_id=(peer, lvl), device_id_type=MESH)
    for peer in lvl_peers:
        pl.semaphore_signal(barrier, inc=1, device_id=(leaf, peer), device_id_type=MESH)
    pl.semaphore_signal(barrier, inc=1, device_id=after_id, device_id_type=MESH)
    pl.semaphore_signal(barrier, inc=1, device_id=before_id, device_id_type=MESH)

    lane = iota((8, LANES), 1)
    low = lane < half
    row8 = iota((8, LANES), 0)
    low_rows = iota((rows, LANES), 1) < half

    inputs[0].wait()
    tp = tree_pos[...]
    dest = lax.div(tp, pts)
    place = lax.rem(dest, n_lvl) * n_leaf + lax.div(dest, n_lvl)
    hit = iota((n_dev, pts), 0) == place
    hit16 = hit.astype(F32).astype(BF16)
    earlier = (iota((pts, pts), 0) < iota((pts, pts), 1)).astype(F32).astype(BF16)
    seen = dot(hit16, earlier)
    oh_user[:, :pts] = jnp.where(hit & (seen < 0.5), 1.0, 0.0).astype(BF16)
    oh_user[:, pts:] = jnp.where(hit & (seen > 0.5), 1.0, 0.0).astype(BF16)
    inputs[1].wait()
    s_a[:, 0] = pack(oh_user[...], targets[...]).reshape(n_lvl, n_leaf, LANES)
    pos = jnp.broadcast_to(lax.rem(tp, pts).astype(F32), (rows, pts))
    s_a[:, 1] = pack(oh_user[...], pos).reshape(n_lvl, n_leaf, LANES)
    r_a[lvl] = s_a[lvl]

    for k in range(2, len(pairs)):
        inputs[k].wait()
    own_one = jnp.concatenate([anchors_one[0], anchors_one[0]], axis=1)
    own_two = jnp.concatenate([anchors_two[0], anchors_two[0]], axis=1)
    partner = jnp.full((8, LANES), -1.0, F32)
    for k in range(lower_count):
        value = lax.rem(far_one[0, k], n_lvl).astype(F32)
        partner = jnp.where(row8 == k, value, partner)
    s_anch[0] = own_one
    s_anch[1] = partner
    r_anch[lvl] = s_anch[...]
    partner = own_two
    for k in range(upper_count):
        value = far_two[0, k].astype(F32)
        partner = jnp.where(jnp.logical_and(row8 == k, jnp.logical_not(low)), value, partner)
    s_top[...] = partner
    r_top[leaf] = partner

    pl.semaphore_wait(barrier, n_lvl + n_leaf)

    over_lvl(lambda p: s_a.at[p], r_a.at[lvl], set_send.at[0], set_recv.at[0])
    copy(coords, r_coords.at[0], set_send.at[1], set_recv.at[1], after_id)
    copy(coords, r_coords.at[1], set_send.at[2], set_recv.at[2], before_id)
    over_lvl(lambda p: s_anch, r_anch.at[lvl], set_send.at[3], set_recv.at[3])
    over_leaf(lambda p: s_top, r_top.at[leaf], set_send.at[4], set_recv.at[4])

    bt = jnp.concatenate(
        [dot_precise(jnp.transpose(transfer_one[c]), ubasis[c]) for c in range(clusters)], axis=1
    )
    b2t = dot_precise(jnp.transpose(transfer_two[0]), bt)
    ct = jnp.concatenate([bt, b2t], axis=0)
    c = jnp.transpose(ct)
    ct_full[...] = b2t
    ct_hi[...], ct_lo[...] = split2(ct)
    c_hi[...], c_lo[...] = split2(c)
    s_g[...] = dot_split(b2t, c_hi[...], c_lo[...])
    r_g[lvl] = s_g[...]

    wait(r_a.at[pl.ds(0, n_lvl - 1)], set_recv.at[0])
    for kind in range(2):
        s_b[:, kind] = jnp.swapaxes(r_a[:, kind], 0, 1)
    r_b[leaf] = s_b[leaf]
    over_leaf(lambda p: s_b.at[p], r_b.at[leaf], set_send.at[5], set_recv.at[5])
    over_lvl(lambda p: s_g, r_g.at[lvl], set_send.at[8], set_recv.at[8])
    copy(ct_full, r_ct.at[0], set_send.at[6], set_recv.at[6], after_id)
    copy(ct_full, r_ct.at[1], set_send.at[7], set_recv.at[7], before_id)

    wait(r_coords.at[0], set_recv.at[1])
    wait(r_coords.at[1], set_recv.at[2])
    src, dst = augmented(coords[...])
    src_pts[pts : 2 * pts] = jnp.transpose(src).astype(BF16)
    src_pts[:pts] = jnp.transpose(augmented(r_coords[0])[0]).astype(BF16)
    src_pts[2 * pts :] = jnp.transpose(augmented(r_coords[1])[0]).astype(BF16)
    dst = dst.astype(BF16)
    first = ring * clusters - clusters
    near_scale = (points * (near_lists + 1)) ** (-0.5)

    def near_rows(n, carry):
        at = pl.ds(pl.multiple_of(n * points, points), points)
        value = jnp.exp(dot(src_pts[at, :], dst))
        parts = []
        for c in range(clusters):
            weight = (n == c + clusters).astype(jnp.int32)
            for k in range(near_lists):
                rel = lax.rem(near_list[c, k] - first + total, total)
                weight = weight + (rel == n).astype(jnp.int32)
            scaled = weight.astype(F32) * near_scale
            parts.append(value[:, c * points : (c + 1) * points] * scaled)
        hi, lo = split2(jnp.concatenate(parts, axis=1))
        w_hi[at, :] = hi
        w_lo[at, :] = lo
        return carry

    lax.fori_loop(0, 3 * clusters, near_rows, 0)

    def lanes_of(get):
        tiles = []
        for m in range(n_lvl // 2):
            tiles.append(jnp.where(low, get(2 * m), get(2 * m + 1)))
        return jnp.concatenate(tiles, axis=1)

    wait(r_anch.at[pl.ds(0, n_lvl - 1)], set_recv.at[3])
    src, dst = augmented(lanes_of(lambda p: r_anch[p, 0]))
    wide = n_lvl * ranks
    partners = lanes_of(lambda p: r_anch[p, 1])
    owner = lax.div(iota((wide, wide), 0), ranks).astype(F32)
    count = jnp.zeros((wide, wide), F32)
    for k in range(lower_count):
        count = count + jnp.where(owner == partners[k : k + 1], 1.0, 0.0)
    value = jnp.exp(dot(jnp.transpose(src).astype(BF16), dst.astype(BF16)))
    k1_hi[...], k1_lo[...] = split2(value * count * (lower_count ** (-0.5)))

    wait(r_top.at[pl.ds(0, n_leaf - 1)], set_recv.at[4])
    groups = (leaf, leaf_before, leaf_after)

    def chosen(lists, get):
        lists = jnp.where(low, pltpu.roll(lists, half, 1), lists)
        named = [jnp.broadcast_to(lists[k : k + 1], (8, LANES)) for k in range(upper_count)]
        picks = [get(0)] * upper_count
        for q in range(1, n_leaf):
            value = get(q)
            picks = [jnp.where(n == float(q), value, p) for n, p in zip(named, picks)]
        return picks

    for g, group in enumerate(groups):
        tops = chosen(r_top[group], lambda q: r_top[q])
        src, _ = augmented(
            jnp.concatenate(
                [jnp.where(low, tops[m], pltpu.roll(tops[m + 1], half, 1)) for m in (0, 2)], axis=1
            )
        )
        mine = r_top[group]
        _, dst = augmented(jnp.where(low, mine, pltpu.roll(mine, half, 1)))
        value = jnp.exp(dot(jnp.transpose(src).astype(BF16), dst.astype(BF16)))
        first_half = iota(value.shape, 1) < half
        value = jnp.where(first_half, 0.0, value) if g == 0 else jnp.where(first_half, value, 0.0)
        k2_hi[g], k2_lo[g] = split2(value * (upper_count ** (-0.5)))

    wait(r_g.at[pl.ds(0, n_lvl - 1)], set_recv.at[8])
    low_ranks = iota((ranks, LANES), 1) < half
    gamma = r_g[0]
    for p in range(1, n_lvl):
        gamma = gamma + r_g[p]
    tiles = [
        jnp.where(low_ranks, r_g[2 * m], pltpu.roll(r_g[2 * m + 1], half, 1))
        for m in range(n_lvl // 2)
    ]
    tiles.append(jnp.where(low_ranks, 0.0, gamma))
    tg = jnp.concatenate(tiles, axis=1)
    tg_hi[...], tg_lo[...] = split2(jnp.concatenate([jnp.zeros_like(tg), tg], axis=0))
    wait(r_ct.at[0], set_recv.at[6])
    wait(r_ct.at[1], set_recv.at[7])
    z_own = dot_split(ct_full[...], w_hi[pts : 2 * pts], w_lo[pts : 2 * pts])
    z_prev = dot_split(r_ct[0], w_hi[:pts], w_lo[:pts])
    z_next = dot_split(r_ct[1], w_hi[2 * pts :], w_lo[2 * pts :])
    at_first = (lvl == 0).astype(F32)
    at_last = (lvl == n_lvl - 1).astype(F32)
    z_main = z_own + z_prev * (1.0 - at_first) + z_next * (1.0 - at_last)
    z_edge = z_prev * at_first + z_next * at_last
    m_hi[...], m_lo[...] = split2(
        jnp.concatenate([bt, z_main, z_edge, jnp.zeros_like(z_edge)], axis=0)
    )

    wait(r_b.at[pl.ds(0, n_leaf - 1)], set_recv.at[5])
    got_pos = r_b[:, 1].reshape(n_dev, LANES).astype(jnp.int32)
    column = iota((n_dev, pts), 1)
    oh_tree[:, :pts] = jnp.where(column == got_pos[:, 0:1], 1.0, 0.0).astype(BF16)
    oh_tree[:, pts:] = jnp.where(column == got_pos[:, half : half + 1], 1.0, 0.0).astype(BF16)
    wbuf[0] = unpack(oh_tree[...], r_b[:, 0].reshape(n_dev, LANES))

    def send_halo(j):
        copy(wbuf.at[j], r_halo.at[j, 0], halo_send.at[j, 0], halo_recv.at[j, 0], after_id)
        copy(wbuf.at[j], r_halo.at[j, 1], halo_send.at[j, 1], halo_recv.at[j, 1], before_id)

    def scatter(j, value):
        s1[j] = value.reshape(n_lvl, 8, LANES)
        r1[j, lvl] = s1[j, lvl]
        over_lvl(lambda peer: s1.at[j, peer], r1.at[j, lvl], send1.at[j], recv1.at[j])

    def broadcast(j, value):
        s2[j] = value
        r2[j, leaf] = value
        over_leaf(lambda peer: s2.at[j], r2.at[j, leaf], send2.at[j], recv2.at[j])

    def gather(j):
        r3[j, lvl] = s3[j, lvl]
        over_lvl(lambda peer: s3.at[j, peer], r3.at[j, lvl], send3.at[j], recv3.at[j])

    def wait1(j):
        wait(r1.at[j, pl.ds(0, n_lvl - 1)], recv1.at[j])

    def wait2(j):
        wait(r2.at[j, pl.ds(0, n_leaf - 1)], recv2.at[j])

    def wait3(j):
        wait(r3.at[j, pl.ds(0, n_lvl - 1)], recv3.at[j])

    def send_potentials(j, f1, f2, edges):
        for d in range(n_lvl):
            tile = jnp.zeros((8, LANES), F32)
            if f1 is not None:
                tile = f1[:, (d // 2) * LANES : (d // 2 + 1) * LANES]
                if d % 2:
                    tile = pltpu.roll(tile, half, 1)
            s3[j, d, 0] = jnp.where(low, tile, f2)
            s3[j, d, 1] = edges[0] if d == 0 else edges[1] if d == n_lvl - 1 else jnp.zeros_like(f2)
        gather(j)

    def level_one(own, extra):
        tiles = [
            jnp.where(low, own[2 * m], pltpu.roll(own[2 * m + 1], half, 1))
            for m in range(n_lvl // 2)
        ]
        t = jnp.concatenate(tiles, axis=1)
        if extra is not None:
            t = t + extra
        return dot_split(t, k1_hi[...], k1_lo[...])

    def return_leaf(kind, value):
        s_c[kind] = pack(oh_tree[...], value).reshape(n_leaf, n_lvl, LANES)
        r_c[kind, leaf] = s_c[kind, leaf]
        over_leaf(
            lambda p: s_c.at[kind, p], r_c.at[kind, leaf], set_send.at[9 + kind], set_recv.at[9 + kind]
        )

    def return_lvl(kind):
        wait(r_c.at[kind, pl.ds(0, n_leaf - 1)], set_recv.at[9 + kind])
        s_d[kind] = jnp.swapaxes(r_c[kind], 0, 1)
        r_d[kind, lvl] = s_d[kind, lvl]
        over_lvl(
            lambda p: s_d.at[kind, p], r_d.at[kind, lvl], set_send.at[12 + kind], set_recv.at[12 + kind]
        )

    def returned(kind):
        wait(r_d.at[kind, pl.ds(0, n_lvl - 1)], set_recv.at[12 + kind])
        return unpack(oh_user[...], r_d[kind].reshape(n_dev, LANES))

    zero8 = jnp.zeros((8, LANES), F32)
    scatter(0, dot_split(wbuf[0], c_hi[...], c_lo[...]))
    send_halo(0)
    wait1(0)
    got = r1[0]
    broadcast(0, jnp.sum(got, axis=0))
    send_potentials(0, level_one(got, None), zero8, (zero8, zero8))

    def body(j, last):
        near = dot_split(wbuf[j], w_hi[pts : 2 * pts], w_lo[pts : 2 * pts])
        wait(r_halo.at[j, 0], halo_recv.at[j, 0])
        near = near + dot_split(r_halo[j, 0], w_hi[:pts], w_lo[:pts])
        wait(r_halo.at[j, 1], halo_recv.at[j, 1])
        acc[...] = near + dot_split(r_halo[j, 1], w_hi[2 * pts :], w_lo[2 * pts :])

        wait3(j)
        main = r3[j, :, 0].reshape(rows, LANES)
        edge = r3[j, :, 1].reshape(rows, LANES)
        moved = dot_split(jnp.concatenate([main, edge], axis=1), m_hi[...], m_lo[...])
        w_next = acc[...] + moved
        wbuf[j + 1] = w_next
        if not last:
            scatter(j + 1, dot_split(w_next, c_hi[...], c_lo[...]))
            send_halo(j + 1)
        power = wbuf[j] + dot_split(jnp.where(low_rows, 0.0, main), ct_hi[...], ct_lo[...])
        square = jnp.sum(power * power, axis=1, keepdims=True)
        if last:
            part = iota((rows, LANES), 1) // (LANES // 4)
            sums = jnp.where(part == 3, square, 0.0)
            for k in range(3):
                sums = jnp.where(part == k, qbuf[k + 1], sums)
            scatter(j + 1, sums)
            return_lvl(1)
        else:
            qbuf[j] = jnp.broadcast_to(square, (rows, LANES))

            @pl.when(j == 1)
            def _():
                return_leaf(0, power)

            @pl.when(j == 2)
            def _():
                return_lvl(0)

            @pl.when(j == 3)
            def _():
                return_leaf(1, power)

        wait2(j)
        potentials = []
        for g, group in enumerate(groups):
            ups = chosen(r_top[group], lambda q: r2[j, q])
            tiles = [jnp.where(low, pltpu.roll(ups[m], half, 1), ups[m + 1]) for m in (0, 2)]
            potentials.append(dot_split(jnp.concatenate(tiles, axis=1), k2_hi[g], k2_lo[g]))
        f2, edges = potentials[0], potentials[1:]
        if last:
            send_potentials(j + 1, None, f2, edges)
            wait1(j + 1)
            broadcast(j + 1, jnp.sum(r1[j + 1], axis=0))
            return
        add = dot_split(f2, tg_hi[...], tg_lo[...])
        wait1(j + 1)
        got = r1[j + 1]
        send_potentials(j + 1, level_one(got, add[:, :wide]), f2, edges)
        broadcast(j + 1, jnp.sum(got, axis=0) + add[:, wide:])

    def step(j, carry):
        body(j, False)
        return carry

    lax.fori_loop(0, APPLIES - 1, step, 0)
    body(APPLIES - 1, True)

    wait3(APPLIES)
    main = r3[APPLIES, :, 0].reshape(rows, LANES)
    return_leaf(
        2, wbuf[APPLIES] + dot_split(jnp.where(low_rows, 0.0, main), ct_hi[...], ct_lo[...])
    )
    back1 = returned(0)
    back3 = returned(1)
    wait2(APPLIES)
    sums = jnp.sum(r2[APPLIES], axis=0)
    for d in range(n_lvl):
        s3[APPLIES + 1, d, 0] = sums
        s3[APPLIES + 1, d, 1] = sums
    gather(APPLIES + 1)
    return_lvl(2)

    wait3(APPLIES + 1)
    sums = r3[APPLIES + 1, :, 0].reshape(rows, LANES)
    g1, g2, g3, g4 = (sums[:, k * (LANES // 4) : k * (LANES // 4) + 1] for k in range(4))
    step0 = g1 / (g2 + RIDGE * g1 + EPSILON)
    keep = 1.0 - RIDGE * step0
    fresh = keep * keep * g1 - 2.0 * step0 * keep * g2 + step0 * step0 * g3
    lead = keep + fresh / (g1 + EPSILON)
    direction_sq = lead * lead * g1 - 2.0 * lead * step0 * g2 + step0 * step0 * g3
    image_sq = lead * lead * g2 - 2.0 * lead * step0 * g3 + step0 * step0 * g4
    step1 = fresh / (image_sq + RIDGE * direction_sq + EPSILON)
    coeffs[...] = (step0 + step1 * lead) * back1 - (step1 * step0) * back3
    partial = (keep - RIDGE * step1 * lead) * back1 - (
        step0 + step1 * (lead - RIDGE * step0)
    ) * back3
    residual[...] = partial + (step1 * step0) * returned(2)

    wait(r_a.at[pl.ds(0, n_lvl - 1)], set_send.at[0])
    wait(r_coords.at[0], set_send.at[1])
    wait(r_coords.at[1], set_send.at[2])
    wait(r_anch.at[pl.ds(0, n_lvl - 1)], set_send.at[3])
    wait(r_top.at[pl.ds(0, n_leaf - 1)], set_send.at[4])
    wait(r_b.at[pl.ds(0, n_leaf - 1)], set_send.at[5])
    wait(r_ct.at[0], set_send.at[6])
    wait(r_ct.at[1], set_send.at[7])
    wait(r_g.at[pl.ds(0, n_lvl - 1)], set_send.at[8])
    for kind in range(3):
        wait(r_c.at[kind, pl.ds(0, n_leaf - 1)], set_send.at[9 + kind])
        wait(r_d.at[kind, pl.ds(0, n_lvl - 1)], set_send.at[12 + kind])

    def sent(j, carry):
        wait(r1.at[j, pl.ds(0, n_lvl - 1)], send1.at[j])
        wait(r2.at[j, pl.ds(0, n_leaf - 1)], send2.at[j])
        return carry

    lax.fori_loop(0, APPLIES + 1, sent, 0)

    def sent_halo(j, carry):
        wait(wbuf.at[j], halo_send.at[j, 0])
        wait(wbuf.at[j], halo_send.at[j, 1])
        return carry

    lax.fori_loop(0, APPLIES, sent_halo, 0)

    def sent_last(j, carry):
        wait(r3.at[j, pl.ds(0, n_lvl - 1)], send3.at[j])
        return carry

    lax.fori_loop(0, APPLIES + 2, sent_last, 0)


def on_device(
    targets, tree_pos, coords, ubasis, transfer_one, transfer_two, anchors_one, anchors_two,
    near_list, far_one, far_two,
):
    rows, pts = targets.shape
    n_leaf, n_lvl = lax.axis_size("leaf"), lax.axis_size("lvl")
    n_dev = n_leaf * n_lvl
    dim = coords.shape[0]
    ranks = anchors_one.shape[2]
    hbm = pl.BlockSpec(memory_space=pl.ANY)
    vmem = pl.BlockSpec(memory_space=pltpu.VMEM)
    smem = pl.BlockSpec(memory_space=pltpu.SMEM)
    V = pltpu.VMEM
    D = pltpu.SemaphoreType.DMA
    wide = n_lvl * ranks
    deep = far_two.shape[1] * ranks
    arrays = (
        targets, tree_pos.reshape(1, pts), coords, ubasis, transfer_one, transfer_two,
        anchors_one, anchors_two,
    )
    scratch = [V(a.shape, a.dtype) for a in arrays] + [
        V((n_dev, 2 * pts), BF16), V((n_dev, 2 * pts), BF16),
        V((n_lvl, 2, n_leaf, LANES), F32), V((n_lvl, 2, n_leaf, LANES), F32),
        V((n_leaf, 2, n_lvl, LANES), F32), V((n_leaf, 2, n_lvl, LANES), F32),
        V((3, n_leaf, n_lvl, LANES), F32), V((3, n_leaf, n_lvl, LANES), F32),
        V((3, n_lvl, n_leaf, LANES), F32), V((3, n_lvl, n_leaf, LANES), F32),
        V((2, dim, pts), F32),
        V((2, 8, LANES), F32), V((n_lvl, 2, 8, LANES), F32),
        V((8, LANES), F32), V((n_leaf, 8, LANES), F32),
        V((ranks, LANES), F32), V((n_lvl, ranks, LANES), F32),
        V((ranks, pts), F32), V((2, ranks, pts), F32),
        V((3 * pts, 64), BF16),
        V((3 * pts, pts), BF16), V((3 * pts, pts), BF16),
        V((wide, wide), BF16), V((wide, wide), BF16),
        V((3, deep, LANES), BF16), V((3, deep, LANES), BF16),
        V((pts, LANES), BF16), V((pts, LANES), BF16),
        V((LANES, pts), BF16), V((LANES, pts), BF16),
        V((2 * LANES, pts), BF16), V((2 * LANES, pts), BF16),
        V((LANES, wide + LANES), BF16), V((LANES, wide + LANES), BF16),
        V((APPLIES + 1, rows, pts), F32), V((rows, pts), F32),
        V((APPLIES, 2, rows, pts), F32), V((APPLIES - 1, rows, LANES), F32),
        V((APPLIES + 1, n_lvl, 8, LANES), F32), V((APPLIES + 1, n_lvl, 8, LANES), F32),
        V((APPLIES + 1, 8, LANES), F32), V((APPLIES + 1, n_leaf, 8, LANES), F32),
        V((APPLIES + 2, n_lvl, 2, 8, LANES), F32), V((APPLIES + 2, n_lvl, 2, 8, LANES), F32),
        D((len(arrays),)), D((15,)), D((15,)),
        D((APPLIES, 2)), D((APPLIES, 2)),
        D((APPLIES + 1,)), D((APPLIES + 1,)), D((APPLIES + 1,)), D((APPLIES + 1,)),
        D((APPLIES + 2,)), D((APPLIES + 2,)),
    ]
    out = jax.ShapeDtypeStruct((rows, pts), F32)
    body = lambda *refs: kernel((n_leaf, n_lvl), *refs)
    return pl.pallas_call(
        body,
        out_shape=(out, out),
        in_specs=[hbm] * len(arrays) + [smem] * 3,
        out_specs=(vmem, vmem),
        scratch_shapes=scratch,
        compiler_params=pltpu.CompilerParams(
            collective_id=0, has_side_effects=True, vmem_limit_bytes=60 * 1024 * 1024
        ),
    )(*arrays, near_list, far_one, far_two)


def solution(mesh):
    both = ("leaf", "lvl")
    return jax.shard_map(
        on_device,
        mesh=mesh,
        in_specs=(
            P(None, both), P(both), P(None, both), P(both, None, None), P(both, None, None),
            P(both, None, None), P(both, None, None), P("leaf", None, None),
            P(both, None), P(both, None), P("leaf", None),
        ),
        out_specs=(P(None, both), P(None, both)),
        check_vma=False,
    )
```

```python
import jax
import jax.numpy as jnp
from jax import lax
from jax.experimental import pallas as pl
from jax.experimental.pallas import tpu as pltpu
from jax.sharding import PartitionSpec as P

F32 = jnp.float32
BF16 = jnp.bfloat16
MESH = pl.DeviceIdType.MESH
PRECISE = lax.Precision.HIGHEST
DIM = 8
RIDGE = 1.0
EPSILON = 1e-6
APPLIES = 5
LANES = 128


def dot(a, b, ca=1, cb=0):
    return lax.dot_general(a, b, (((ca,), (cb,)), ((), ())), preferred_element_type=F32)


def dot_precise(a, b):
    return lax.dot_general(
        a, b, (((1,), (0,)), ((), ())), precision=PRECISE, preferred_element_type=F32
    )


def split2(x):
    hi = x.astype(BF16)
    return hi, (x - hi.astype(F32)).astype(BF16)


def split3(x):
    hi = x.astype(BF16)
    rest = x - hi.astype(F32)
    mid = rest.astype(BF16)
    return hi, mid, (rest - mid.astype(F32)).astype(BF16)


def dot_split(a, b_hi, b_lo):
    rows = a.shape[0]
    a_hi, a_lo = split2(a)
    both = dot(jnp.concatenate([a_hi, a_lo], axis=0), b_hi)
    return both[:rows] + both[rows:] + dot(a_hi, b_lo)


def iota(shape, dim):
    return lax.broadcasted_iota(jnp.int32, shape, dim)


def augmented(x):
    n = x.shape[1]
    x1, x2, x3 = (p.astype(F32) for p in split3(x))
    sq = jnp.sum(x * x, axis=0, keepdims=True) * (-1.0 / DIM)
    n1, n2, n3 = (p.astype(F32) for p in split3(sq))
    row = iota((8, n), 0)
    lead = jnp.where(row == 0, n1, jnp.where(row == 1, n2, n3))
    tail = jnp.where(row == 3, n1, jnp.where(row == 4, n2, n3))
    zero = jnp.zeros((8, n), F32)
    src_norm = jnp.where(row < 3, lead, jnp.where(row < 6, 1.0, 0.0))
    dst_norm = jnp.where(row < 3, 1.0, jnp.where(row < 6, tail, 0.0))
    q = 2.0 / DIM
    src = jnp.concatenate([x1, x1, x2, x1, x3, x2, src_norm, zero], axis=0)
    dst = jnp.concatenate([x1 * q, x2 * q, x1 * q, x3 * q, x1 * q, x2 * q, dst_norm, zero], axis=0)
    return src, dst


def pack(onehot, x):
    total = None
    for part in split3(x):
        zero = jnp.zeros_like(part)
        wide = jnp.concatenate(
            [jnp.concatenate([part, zero], axis=1), jnp.concatenate([zero, part], axis=1)], axis=0
        )
        term = dot(onehot, wide, 1, 1)
        total = term if total is None else total + term
    return total


def unpack(onehot, g):
    half = g.shape[1] // 2
    cols = onehot.shape[1] // 2
    gt = jnp.transpose(g)
    total = None
    for part in split3(gt):
        term = dot(part, onehot)
        total = term if total is None else total + term
    return total[:half, :cols] + total[half:, cols:]


def kernel(
    sizes,
    targets_h, tree_pos_h, coords_h, ubasis_h, transfer_one_h, transfer_two_h, anchors_one_h,
    anchors_two_h, near_list, far_one, far_two,
    result,
    targets, tree_pos, coords, ubasis, transfer_one, transfer_two, anchors_one, anchors_two,
    oh_user, oh_tree, s_a, r_a, s_b, r_b, s_c, r_c, s_d, r_d, s_e, r_e, s_f, r_f,
    r_coords, s_anch, r_anch, s_top, r_top, s_g, r_g, ct_full, r_ct,
    src_pts, w_hi, w_lo, k1_hi, k1_lo, k2_hi, k2_lo, c_hi, c_lo, ct_hi, ct_lo, m_hi, m_lo, mc_hi, mc_lo,
    tg_hi, tg_lo,
    wbuf, acc, tu_near, r_halo, qbuf, s1, r1, s2, r2, s3, r3,
    in_sem, set_send, set_recv, halo_send, halo_recv, send1, recv1, send2, recv2, send3, recv3,
):
    n_leaf, n_lvl = sizes
    n_dev = n_leaf * n_lvl
    leaf, lvl = lax.axis_index("leaf"), lax.axis_index("lvl")
    rows, pts = targets.shape
    clusters = ubasis.shape[0]
    points = ubasis.shape[2]
    ranks = ubasis.shape[1]
    half = LANES // 2
    total = n_dev * clusters
    near_lists = near_list.shape[1]
    lower_count = far_one.shape[1]
    upper_count = far_two.shape[1]

    inputs = []
    pairs = (
        (tree_pos_h, tree_pos), (targets_h, targets), (transfer_one_h, transfer_one),
        (ubasis_h, ubasis), (transfer_two_h, transfer_two), (coords_h, coords),
        (anchors_one_h, anchors_one), (anchors_two_h, anchors_two),
    )
    for k, (hbm, vmem) in enumerate(pairs):
        inputs.append(pltpu.make_async_copy(hbm, vmem, in_sem.at[k]))
        inputs[-1].start()

    chips_z, cores = 8, 2
    chips_y, chips_x = n_leaf // chips_z, n_lvl // cores

    def others(long, short):
        pairs = [(a, b) for a in range(long) for b in range(short)][1:]
        far = lambda p: min(p[0], long - p[0]) + min(p[1], short - p[1]) * (short > 2)
        return sorted(pairs, key=lambda p: -far(p))

    def shifted(index, short, long, a, b):
        return lax.rem(index // short + a, long) * short + lax.rem(lax.rem(index, short) + b, short)

    leaf_peers = [shifted(leaf, chips_z, chips_y, a, b) for a, b in others(chips_y, chips_z)]
    lvl_peers = [shifted(lvl, cores, chips_x, a, b) for a, b in others(chips_x, cores)]
    leaf_before, leaf_after = lax.rem(leaf + n_leaf - 1, n_leaf), lax.rem(leaf + 1, n_leaf)

    ring = leaf * n_lvl + lvl
    after = lax.rem(ring + 1, n_dev)
    before = lax.rem(ring + n_dev - 1, n_dev)
    after_id = (after // n_lvl, lax.rem(after, n_lvl))
    before_id = (before // n_lvl, lax.rem(before, n_lvl))

    def copy(src, dst, send, recv, device):
        pltpu.make_async_remote_copy(
            src_ref=src, dst_ref=dst, send_sem=send, recv_sem=recv,
            device_id=device, device_id_type=MESH,
        ).start()

    def wait(ref, sem):
        pltpu.make_async_copy(ref, ref, sem).wait()

    def over_lvl(src, dst, send, recv):
        for peer in lvl_peers:
            copy(src(peer), dst, send, recv, (leaf, peer))

    def over_leaf(src, dst, send, recv):
        for peer in leaf_peers:
            copy(src(peer), dst, send, recv, (peer, lvl))

    barrier = pltpu.get_barrier_semaphore()
    for peer in leaf_peers:
        pl.semaphore_signal(barrier, inc=1, device_id=(peer, lvl), device_id_type=MESH)
    for peer in lvl_peers:
        pl.semaphore_signal(barrier, inc=1, device_id=(leaf, peer), device_id_type=MESH)
    pl.semaphore_signal(barrier, inc=1, device_id=after_id, device_id_type=MESH)
    pl.semaphore_signal(barrier, inc=1, device_id=before_id, device_id_type=MESH)

    lane = iota((8, LANES), 1)
    low = lane < half
    row8 = iota((8, LANES), 0)
    low_rows = iota((rows, LANES), 1) < half

    inputs[0].wait()
    tp = tree_pos[...]
    dest = lax.div(tp, pts)
    place = lax.rem(dest, n_lvl) * n_leaf + lax.div(dest, n_lvl)
    hit = iota((n_dev, pts), 0) == place
    hit16 = hit.astype(F32).astype(BF16)
    earlier = (iota((pts, pts), 0) < iota((pts, pts), 1)).astype(F32).astype(BF16)
    seen = dot(hit16, earlier)
    oh_user[:, :pts] = jnp.where(hit & (seen < 0.5), 1.0, 0.0).astype(BF16)
    oh_user[:, pts:] = jnp.where(hit & (seen > 0.5), 1.0, 0.0).astype(BF16)
    inputs[1].wait()
    blocks = n_leaf // 8
    packed = pack(oh_user[...], targets[...])
    s_a[:, :blocks] = packed.reshape(n_lvl, blocks, 8, LANES)
    pos = lax.rem(tp, pts).astype(F32)
    pos_hi = pos.astype(BF16).astype(F32)
    row16 = iota((16, pts), 0)
    terms = jnp.where(row16 == 0, pos_hi, jnp.where(row16 == 1, pos - pos_hi, 0.0)).astype(BF16)
    tile = jnp.zeros((8, LANES), F32)
    for h in range(2):
        both = dot(terms, oh_user[:, h * pts : (h + 1) * pts], 1, 1)
        line = both[0:1] + both[1:2]
        for q in range(n_dev // LANES):
            part = line[:, q * LANES : (q + 1) * LANES]
            tile = jnp.where(row8 == 2 * h + q, part, tile)
    for p in range(n_lvl):
        s_a[p, blocks] = tile
    r_a[lvl] = s_a[lvl]

    for k in range(2, len(pairs)):
        inputs[k].wait()
    own_one = jnp.concatenate([anchors_one[0], anchors_one[0]], axis=1)
    own_two = jnp.concatenate([anchors_two[0], anchors_two[0]], axis=1)
    partner = jnp.full((8, LANES), -1.0, F32)
    for k in range(lower_count):
        value = lax.rem(far_one[0, k], n_lvl).astype(F32)
        partner = jnp.where(row8 == k, value, partner)
    s_anch[0] = own_one
    s_anch[1] = partner
    r_anch[lvl] = s_anch[...]
    partner = own_two
    for k in range(upper_count):
        value = far_two[0, k].astype(F32)
        partner = jnp.where(jnp.logical_and(row8 == k, jnp.logical_not(low)), value, partner)
    s_top[...] = partner
    r_top[leaf] = partner

    pl.semaphore_wait(barrier, n_lvl + n_leaf)

    over_lvl(lambda p: s_a.at[p], r_a.at[lvl], set_send.at[0], set_recv.at[0])
    copy(coords, r_coords.at[0], set_send.at[1], set_recv.at[1], after_id)
    copy(coords, r_coords.at[1], set_send.at[2], set_recv.at[2], before_id)
    over_lvl(lambda p: s_anch, r_anch.at[lvl], set_send.at[3], set_recv.at[3])
    over_leaf(lambda p: s_top, r_top.at[leaf], set_send.at[4], set_recv.at[4])

    bt = jnp.concatenate(
        [dot_precise(jnp.transpose(transfer_one[c]), ubasis[c]) for c in range(clusters)], axis=1
    )
    b2t = dot_precise(jnp.transpose(transfer_two[0]), bt)
    ct = jnp.concatenate([bt, b2t], axis=0)
    c = jnp.transpose(ct)
    ct_full[...] = b2t
    ct_hi[...], ct_lo[...] = split2(ct)
    c_hi[...], c_lo[...] = split2(c)
    s_g[...] = dot_split(b2t, c_hi[...], c_lo[...])
    r_g[lvl] = s_g[...]

    wait(r_a.at[pl.ds(0, n_lvl - 1)], set_recv.at[0])
    s_b[:, :n_lvl] = jnp.swapaxes(r_a[:, :blocks].reshape(n_lvl, n_leaf, LANES), 0, 1)
    per_row = LANES // n_leaf
    mine = []
    for h in range(2):
        line = jnp.where(lvl < per_row, r_a[:, blocks, 2 * h], r_a[:, blocks, 2 * h + 1])
        turned = line
        for k in range(1, per_row):
            here = lax.rem(lvl, per_row) == k
            turned = jnp.where(here, pltpu.roll(line, LANES - k * n_leaf, 1), turned)
        mine.append(turned)
    square = jnp.concatenate(mine + [jnp.zeros((LANES - 16, LANES), F32)], axis=0)
    s_b[:, n_lvl : n_lvl + 1] = jnp.transpose(square)[:n_leaf].reshape(n_leaf, 1, LANES)
    r_b[leaf] = s_b[leaf]
    over_leaf(lambda p: s_b.at[p], r_b.at[leaf], set_send.at[5], set_recv.at[5])
    over_lvl(lambda p: s_g, r_g.at[lvl], set_send.at[8], set_recv.at[8])
    copy(ct_full, r_ct.at[0], set_send.at[6], set_recv.at[6], after_id)
    copy(ct_full, r_ct.at[1], set_send.at[7], set_recv.at[7], before_id)

    wait(r_coords.at[0], set_recv.at[1])
    wait(r_coords.at[1], set_recv.at[2])
    src, dst = augmented(coords[...])
    src_pts[pts : 2 * pts] = jnp.transpose(src).astype(BF16)
    src_pts[:pts] = jnp.transpose(augmented(r_coords[0])[0]).astype(BF16)
    src_pts[2 * pts :] = jnp.transpose(augmented(r_coords[1])[0]).astype(BF16)
    dst = dst.astype(BF16)
    first = ring * clusters - clusters
    near_scale = (points * (near_lists + 1)) ** (-0.5)

    def near_rows(n, carry):
        at = pl.ds(pl.multiple_of(n * points, points), points)
        value = jnp.exp(dot(src_pts[at, :], dst))
        parts = []
        for c in range(clusters):
            weight = (n == c + clusters).astype(jnp.int32)
            for k in range(near_lists):
                rel = lax.rem(near_list[c, k] - first + total, total)
                weight = weight + (rel == n).astype(jnp.int32)
            scaled = weight.astype(F32) * near_scale
            parts.append(value[:, c * points : (c + 1) * points] * scaled)
        hi, lo = split2(jnp.concatenate(parts, axis=1))
        w_hi[at, :] = hi
        w_lo[at, :] = lo
        return carry

    lax.fori_loop(0, 3 * clusters, near_rows, 0)

    def lanes_of(get):
        tiles = []
        for m in range(n_lvl // 2):
            tiles.append(jnp.where(low, get(2 * m), get(2 * m + 1)))
        return jnp.concatenate(tiles, axis=1)

    wait(r_anch.at[pl.ds(0, n_lvl - 1)], set_recv.at[3])
    src, dst = augmented(lanes_of(lambda p: r_anch[p, 0]))
    wide = n_lvl * ranks
    partners = lanes_of(lambda p: r_anch[p, 1])
    owner = lax.div(iota((wide, wide), 0), ranks).astype(F32)
    count = jnp.zeros((wide, wide), F32)
    for k in range(lower_count):
        count = count + jnp.where(owner == partners[k : k + 1], 1.0, 0.0)
    value = jnp.exp(dot(jnp.transpose(src).astype(BF16), dst.astype(BF16)))
    k1_hi[...], k1_lo[...] = split2(value * count * (lower_count ** (-0.5)))

    wait(r_top.at[pl.ds(0, n_leaf - 1)], set_recv.at[4])
    groups = (leaf, leaf_before, leaf_after)

    def chosen(lists, get):
        lists = jnp.where(low, pltpu.roll(lists, half, 1), lists)
        named = [jnp.broadcast_to(lists[k : k + 1], (8, LANES)) for k in range(upper_count)]
        picks = [get(0)] * upper_count
        for q in range(1, n_leaf):
            value = get(q)
            picks = [jnp.where(n == float(q), value, p) for n, p in zip(named, picks)]
        return picks

    for g, group in enumerate(groups):
        tops = chosen(r_top[group], lambda q: r_top[q])
        src, _ = augmented(
            jnp.concatenate(
                [jnp.where(low, tops[m], pltpu.roll(tops[m + 1], half, 1)) for m in (0, 2)], axis=1
            )
        )
        mine = r_top[group]
        _, dst = augmented(jnp.where(low, mine, pltpu.roll(mine, half, 1)))
        value = jnp.exp(dot(jnp.transpose(src).astype(BF16), dst.astype(BF16)))
        first_half = iota(value.shape, 1) < half
        value = jnp.where(first_half, 0.0, value) if g == 0 else jnp.where(first_half, value, 0.0)
        k2_hi[g], k2_lo[g] = split2(value * (upper_count ** (-0.5)))

    wait(r_g.at[pl.ds(0, n_lvl - 1)], set_recv.at[8])
    low_ranks = iota((ranks, LANES), 1) < half
    gamma = r_g[0]
    for p in range(1, n_lvl):
        gamma = gamma + r_g[p]
    tiles = [
        jnp.where(low_ranks, r_g[2 * m], pltpu.roll(r_g[2 * m + 1], half, 1))
        for m in range(n_lvl // 2)
    ]
    tiles.append(jnp.where(low_ranks, 0.0, gamma))
    tg = jnp.concatenate(tiles, axis=1)
    tg_hi[...], tg_lo[...] = split2(jnp.concatenate([jnp.zeros_like(tg), tg], axis=0))
    wait(r_ct.at[0], set_recv.at[6])
    wait(r_ct.at[1], set_recv.at[7])
    z_own = dot_split(ct_full[...], w_hi[pts : 2 * pts], w_lo[pts : 2 * pts])
    z_prev = dot_split(r_ct[0], w_hi[:pts], w_lo[:pts])
    z_next = dot_split(r_ct[1], w_hi[2 * pts :], w_lo[2 * pts :])
    at_first = (lvl == 0).astype(F32)
    at_last = (lvl == n_lvl - 1).astype(F32)
    z_main = z_own + z_prev * (1.0 - at_first) + z_next * (1.0 - at_last)
    z_edge = z_prev * at_first + z_next * at_last
    m = jnp.concatenate([bt, z_main, z_edge, jnp.zeros_like(z_edge)], axis=0)
    m_hi[...], m_lo[...] = split2(m)
    mc_hi[...], mc_lo[...] = split2(dot_split(m, c_hi[...], c_lo[...]))

    wait(r_b.at[pl.ds(0, n_leaf - 1)], set_recv.at[5])
    column = iota((n_dev, pts), 1).astype(F32)
    row3 = iota((n_leaf, n_lvl, LANES), 1)
    lane3 = iota((n_leaf, n_lvl, LANES), 2)
    line = jnp.broadcast_to(r_b[:, n_lvl : n_lvl + 1], (n_leaf, n_lvl, LANES))
    for h in range(2):
        got = jnp.where(lane3 == row3 + h * n_lvl, line, 0.0).reshape(n_dev, LANES)
        got = jnp.sum(got, axis=1, keepdims=True)
        oh_tree[:, h * pts : (h + 1) * pts] = jnp.where(column == got, 1.0, 0.0).astype(BF16)
    wbuf[0] = unpack(oh_tree[...], r_b[:, :n_lvl].reshape(n_dev, LANES))

    def send_halo(j):
        copy(wbuf.at[j], r_halo.at[j, 0], halo_send.at[j, 0], halo_recv.at[j, 0], after_id)
        copy(wbuf.at[j], r_halo.at[j, 1], halo_send.at[j, 1], halo_recv.at[j, 1], before_id)

    def scatter(j, value):
        s1[j] = value.reshape(n_lvl, 8, LANES)
        r1[j, lvl] = s1[j, lvl]
        over_lvl(lambda peer: s1.at[j, peer], r1.at[j, lvl], send1.at[j], recv1.at[j])

    def broadcast(j, value):
        s2[j] = value
        r2[j, leaf] = value
        over_leaf(lambda peer: s2.at[j], r2.at[j, leaf], send2.at[j], recv2.at[j])

    def gather(j):
        r3[j, lvl] = s3[j, lvl]
        over_lvl(lambda peer: s3.at[j, peer], r3.at[j, lvl], send3.at[j], recv3.at[j])

    def wait1(j):
        wait(r1.at[j, pl.ds(0, n_lvl - 1)], recv1.at[j])

    def wait2(j):
        wait(r2.at[j, pl.ds(0, n_leaf - 1)], recv2.at[j])

    def wait3(j):
        wait(r3.at[j, pl.ds(0, n_lvl - 1)], recv3.at[j])

    def send_potentials(j, f1, f2, edges):
        for d in range(n_lvl):
            tile = jnp.zeros((8, LANES), F32)
            if f1 is not None:
                tile = f1[:, (d // 2) * LANES : (d // 2 + 1) * LANES]
                if d % 2:
                    tile = pltpu.roll(tile, half, 1)
            s3[j, d, 0] = jnp.where(low, tile, f2)
            s3[j, d, 1] = edges[0] if d == 0 else edges[1] if d == n_lvl - 1 else jnp.zeros_like(f2)
        gather(j)

    def level_one(own, extra):
        tiles = [
            jnp.where(low, own[2 * m], pltpu.roll(own[2 * m + 1], half, 1))
            for m in range(n_lvl // 2)
        ]
        t = jnp.concatenate(tiles, axis=1)
        if extra is not None:
            t = t + extra
        return dot_split(t, k1_hi[...], k1_lo[...])

    def packed_back(value):
        return pack(oh_tree[...], value).reshape(n_leaf, n_lvl, LANES)

    def unpacked(rows_back):
        return unpack(oh_user[...], rows_back.reshape(n_dev, LANES))

    zero8 = jnp.zeros((8, LANES), F32)
    scatter(0, dot_split(wbuf[0], c_hi[...], c_lo[...]))
    send_halo(0)
    acc[...] = dot_split(wbuf[0], w_hi[pts : 2 * pts], w_lo[pts : 2 * pts])
    wait1(0)
    got = r1[0]
    broadcast(0, jnp.sum(got, axis=0))
    send_potentials(0, level_one(got, None), zero8, (zero8, zero8))

    def body(j, last):
        wait(r_halo.at[j, 0], halo_recv.at[j, 0])
        near = acc[...] + dot_split(r_halo[j, 0], w_hi[:pts], w_lo[:pts])
        wait(r_halo.at[j, 1], halo_recv.at[j, 1])
        near = near + dot_split(r_halo[j, 1], w_hi[2 * pts :], w_lo[2 * pts :])
        acc[...] = near
        if not last:
            tu_near[...] = dot_split(near, c_hi[...], c_lo[...])

        wait3(j)
        main = r3[j, :, 0].reshape(rows, LANES)
        edge = r3[j, :, 1].reshape(rows, LANES)
        moved = jnp.concatenate([main, edge], axis=1)
        if not last:
            scatter(j + 1, tu_near[...] + dot_split(moved, mc_hi[...], mc_lo[...]))
        w_next = acc[...] + dot_split(moved, m_hi[...], m_lo[...])
        wbuf[j + 1] = w_next
        if not last:
            send_halo(j + 1)
            acc[...] = dot_split(w_next, w_hi[pts : 2 * pts], w_lo[pts : 2 * pts])
        power = wbuf[j] + dot_split(jnp.where(low_rows, 0.0, main), ct_hi[...], ct_lo[...])
        square = jnp.sum(power * power, axis=1, keepdims=True)
        if last:
            part = iota((rows, LANES), 1) // (LANES // 4)
            sums = jnp.where(part == 3, square, 0.0)
            for k in range(3):
                sums = jnp.where(part == k, qbuf[k + 1], sums)
            scatter(j + 1, sums)
        else:
            qbuf[j] = jnp.broadcast_to(square, (rows, LANES))

            @pl.when(j == 1)
            def _():
                s_c[:, 0] = packed_back(power)

            @pl.when(j == 3)
            def _():
                s_c[:, 1] = packed_back(power)
                r_c[leaf] = s_c[leaf]
                over_leaf(lambda p: s_c.at[p], r_c.at[leaf], set_send.at[9], set_recv.at[9])

        wait2(j)
        potentials = []
        for g, group in enumerate(groups):
            ups = chosen(r_top[group], lambda q: r2[j, q])
            tiles = [jnp.where(low, pltpu.roll(ups[m], half, 1), ups[m + 1]) for m in (0, 2)]
            potentials.append(dot_split(jnp.concatenate(tiles, axis=1), k2_hi[g], k2_lo[g]))
        f2, edges = potentials[0], potentials[1:]
        if last:
            send_potentials(j + 1, None, f2, edges)
            wait1(j + 1)
            broadcast(j + 1, jnp.sum(r1[j + 1], axis=0))
            return
        add = dot_split(f2, tg_hi[...], tg_lo[...])
        wait1(j + 1)
        got = r1[j + 1]
        send_potentials(j + 1, level_one(got, add[:, :wide]), f2, edges)
        broadcast(j + 1, jnp.sum(got, axis=0) + add[:, wide:])

    def step(j, carry):
        body(j, False)
        return carry

    lax.fori_loop(0, APPLIES - 1, step, 0)
    body(APPLIES - 1, True)

    wait(r_c.at[pl.ds(0, n_leaf - 1)], set_recv.at[9])
    for kind in range(2):
        s_d[:, kind] = jnp.swapaxes(r_c[:, kind], 0, 1)
    r_d[lvl] = s_d[lvl]
    over_lvl(lambda p: s_d.at[p], r_d.at[lvl], set_send.at[10], set_recv.at[10])

    wait3(APPLIES)
    main = r3[APPLIES, :, 0].reshape(rows, LANES)
    s_e[...] = packed_back(
        wbuf[APPLIES] + dot_split(jnp.where(low_rows, 0.0, main), ct_hi[...], ct_lo[...])
    )
    r_e[leaf] = s_e[leaf]
    over_leaf(lambda p: s_e.at[p], r_e.at[leaf], set_send.at[11], set_recv.at[11])
    wait(r_d.at[pl.ds(0, n_lvl - 1)], set_recv.at[10])
    back1 = unpacked(r_d[:, 0])
    back3 = unpacked(r_d[:, 1])
    wait2(APPLIES)
    sums = jnp.sum(r2[APPLIES], axis=0)
    for d in range(n_lvl):
        s3[APPLIES + 1, d, 0] = sums
        s3[APPLIES + 1, d, 1] = sums
    gather(APPLIES + 1)
    wait(r_e.at[pl.ds(0, n_leaf - 1)], set_recv.at[11])
    s_f[...] = jnp.swapaxes(r_e[...], 0, 1)
    r_f[lvl] = s_f[lvl]
    over_lvl(lambda p: s_f.at[p], r_f.at[lvl], set_send.at[12], set_recv.at[12])

    wait3(APPLIES + 1)
    sums = r3[APPLIES + 1, :, 0].reshape(rows, LANES)
    g1, g2, g3, g4 = (sums[:, k * (LANES // 4) : k * (LANES // 4) + 1] for k in range(4))
    step0 = g1 / (g2 + RIDGE * g1 + EPSILON)
    keep = 1.0 - RIDGE * step0
    fresh = keep * keep * g1 - 2.0 * step0 * keep * g2 + step0 * step0 * g3
    lead = keep + fresh / (g1 + EPSILON)
    direction_sq = lead * lead * g1 - 2.0 * lead * step0 * g2 + step0 * step0 * g3
    image_sq = lead * lead * g2 - 2.0 * lead * step0 * g3 + step0 * step0 * g4
    step1 = fresh / (image_sq + RIDGE * direction_sq + EPSILON)
    result[0] = (step0 + step1 * lead) * back1 - (step1 * step0) * back3
    partial = (keep - RIDGE * step1 * lead) * back1 - (
        step0 + step1 * (lead - RIDGE * step0)
    ) * back3
    wait(r_f.at[pl.ds(0, n_lvl - 1)], set_recv.at[12])
    result[1] = partial + (step1 * step0) * unpacked(r_f[...])

    wait(r_a.at[pl.ds(0, n_lvl - 1)], set_send.at[0])
    wait(r_coords.at[0], set_send.at[1])
    wait(r_coords.at[1], set_send.at[2])
    wait(r_anch.at[pl.ds(0, n_lvl - 1)], set_send.at[3])
    wait(r_top.at[pl.ds(0, n_leaf - 1)], set_send.at[4])
    wait(r_b.at[pl.ds(0, n_leaf - 1)], set_send.at[5])
    wait(r_ct.at[0], set_send.at[6])
    wait(r_ct.at[1], set_send.at[7])
    wait(r_g.at[pl.ds(0, n_lvl - 1)], set_send.at[8])
    wait(r_c.at[pl.ds(0, n_leaf - 1)], set_send.at[9])
    wait(r_d.at[pl.ds(0, n_lvl - 1)], set_send.at[10])
    wait(r_e.at[pl.ds(0, n_leaf - 1)], set_send.at[11])
    wait(r_f.at[pl.ds(0, n_lvl - 1)], set_send.at[12])

    def sent(j, carry):
        wait(r1.at[j, pl.ds(0, n_lvl - 1)], send1.at[j])
        wait(r2.at[j, pl.ds(0, n_leaf - 1)], send2.at[j])
        return carry

    lax.fori_loop(0, APPLIES + 1, sent, 0)

    def sent_halo(j, carry):
        wait(wbuf.at[j], halo_send.at[j, 0])
        wait(wbuf.at[j], halo_send.at[j, 1])
        return carry

    lax.fori_loop(0, APPLIES, sent_halo, 0)

    def sent_last(j, carry):
        wait(r3.at[j, pl.ds(0, n_lvl - 1)], send3.at[j])
        return carry

    lax.fori_loop(0, APPLIES + 2, sent_last, 0)


def on_device(
    targets, tree_pos, coords, ubasis, transfer_one, transfer_two, anchors_one, anchors_two,
    near_list, far_one, far_two,
):
    rows, pts = targets.shape
    n_leaf, n_lvl = lax.axis_size("leaf"), lax.axis_size("lvl")
    n_dev = n_leaf * n_lvl
    dim = coords.shape[0]
    ranks = anchors_one.shape[2]
    hbm = pl.BlockSpec(memory_space=pl.ANY)
    vmem = pl.BlockSpec(memory_space=pltpu.VMEM)
    smem = pl.BlockSpec(memory_space=pltpu.SMEM)
    V = pltpu.VMEM
    D = pltpu.SemaphoreType.DMA
    wide = n_lvl * ranks
    deep = far_two.shape[1] * ranks
    arrays = (
        targets, tree_pos.reshape(1, pts), coords, ubasis, transfer_one, transfer_two,
        anchors_one, anchors_two,
    )
    scratch = [V(a.shape, a.dtype) for a in arrays] + [
        V((n_dev, 2 * pts), BF16), V((n_dev, 2 * pts), BF16),
        V((n_lvl, n_leaf // 8 + 1, 8, LANES), F32), V((n_lvl, n_leaf // 8 + 1, 8, LANES), F32),
        V((n_leaf, n_lvl + 1, LANES), F32), V((n_leaf, n_lvl + 1, LANES), F32),
        V((n_leaf, 2, n_lvl, LANES), F32), V((n_leaf, 2, n_lvl, LANES), F32),
        V((n_lvl, 2, n_leaf, LANES), F32), V((n_lvl, 2, n_leaf, LANES), F32),
        V((n_leaf, n_lvl, LANES), F32), V((n_leaf, n_lvl, LANES), F32),
        V((n_lvl, n_leaf, LANES), F32), V((n_lvl, n_leaf, LANES), F32),
        V((2, dim, pts), F32),
        V((2, 8, LANES), F32), V((n_lvl, 2, 8, LANES), F32),
        V((8, LANES), F32), V((n_leaf, 8, LANES), F32),
        V((ranks, LANES), F32), V((n_lvl, ranks, LANES), F32),
        V((ranks, pts), F32), V((2, ranks, pts), F32),
        V((3 * pts, 64), BF16),
        V((3 * pts, pts), BF16), V((3 * pts, pts), BF16),
        V((wide, wide), BF16), V((wide, wide), BF16),
        V((3, deep, LANES), BF16), V((3, deep, LANES), BF16),
        V((pts, LANES), BF16), V((pts, LANES), BF16),
        V((LANES, pts), BF16), V((LANES, pts), BF16),
        V((2 * LANES, pts), BF16), V((2 * LANES, pts), BF16),
        V((2 * LANES, LANES), BF16), V((2 * LANES, LANES), BF16),
        V((LANES, wide + LANES), BF16), V((LANES, wide + LANES), BF16),
        V((APPLIES + 1, rows, pts), F32), V((rows, pts), F32), V((rows, LANES), F32),
        V((APPLIES, 2, rows, pts), F32), V((APPLIES - 1, rows, LANES), F32),
        V((APPLIES + 1, n_lvl, 8, LANES), F32), V((APPLIES + 1, n_lvl, 8, LANES), F32),
        V((APPLIES + 1, 8, LANES), F32), V((APPLIES + 1, n_leaf, 8, LANES), F32),
        V((APPLIES + 2, n_lvl, 2, 8, LANES), F32), V((APPLIES + 2, n_lvl, 2, 8, LANES), F32),
        D((len(arrays),)), D((13,)), D((13,)),
        D((APPLIES, 2)), D((APPLIES, 2)),
        D((APPLIES + 1,)), D((APPLIES + 1,)), D((APPLIES + 1,)), D((APPLIES + 1,)),
        D((APPLIES + 2,)), D((APPLIES + 2,)),
    ]
    out = jax.ShapeDtypeStruct((2, rows, pts), F32)
    body = lambda *refs: kernel((n_leaf, n_lvl), *refs)
    both = pl.pallas_call(
        body,
        out_shape=out,
        in_specs=[hbm] * len(arrays) + [smem] * 3,
        out_specs=vmem,
        scratch_shapes=scratch,
        compiler_params=pltpu.CompilerParams(
            collective_id=0, has_side_effects=True, vmem_limit_bytes=60 * 1024 * 1024
        ),
    )(*arrays, near_list, far_one, far_two)
    return both[0], both[1]


def solution(mesh):
    both = ("leaf", "lvl")
    return jax.shard_map(
        on_device,
        mesh=mesh,
        in_specs=(
            P(None, both), P(both), P(None, both), P(both, None, None), P(both, None, None),
            P(both, None, None), P(both, None, None), P("leaf", None, None),
            P(both, None), P(both, None), P("leaf", None),
        ),
        out_specs=(P(None, both), P(None, both)),
        check_vma=False,
    )
```

```python
import jax
import jax.numpy as jnp
from jax import lax
from jax.experimental import pallas as pl
from jax.experimental.pallas import tpu as pltpu
from jax.sharding import PartitionSpec as P

F32 = jnp.float32
BF16 = jnp.bfloat16
MESH = pl.DeviceIdType.MESH
PRECISE = lax.Precision.HIGHEST
DIM = 8
RIDGE = 1.0
EPSILON = 1e-6
APPLIES = 5
LANES = 128


def dot(a, b, ca=1, cb=0):
    return lax.dot_general(a, b, (((ca,), (cb,)), ((), ())), preferred_element_type=F32)


def dot_precise(a, b):
    return lax.dot_general(
        a, b, (((1,), (0,)), ((), ())), precision=PRECISE, preferred_element_type=F32
    )


def split2(x):
    hi = x.astype(BF16)
    return hi, (x - hi.astype(F32)).astype(BF16)


def split3(x):
    hi = x.astype(BF16)
    rest = x - hi.astype(F32)
    mid = rest.astype(BF16)
    return hi, mid, (rest - mid.astype(F32)).astype(BF16)


def dot_split(a, b_hi, b_lo):
    rows = a.shape[0]
    a_hi, a_lo = split2(a)
    both = dot(jnp.concatenate([a_hi, a_lo], axis=0), b_hi)
    return both[:rows] + both[rows:] + dot(a_hi, b_lo)


def iota(shape, dim):
    return lax.broadcasted_iota(jnp.int32, shape, dim)


def augmented(x):
    n = x.shape[1]
    x1, x2, x3 = (p.astype(F32) for p in split3(x))
    sq = jnp.sum(x * x, axis=0, keepdims=True) * (-1.0 / DIM)
    n1, n2, n3 = (p.astype(F32) for p in split3(sq))
    row = iota((8, n), 0)
    lead = jnp.where(row == 0, n1, jnp.where(row == 1, n2, n3))
    tail = jnp.where(row == 3, n1, jnp.where(row == 4, n2, n3))
    zero = jnp.zeros((8, n), F32)
    src_norm = jnp.where(row < 3, lead, jnp.where(row < 6, 1.0, 0.0))
    dst_norm = jnp.where(row < 3, 1.0, jnp.where(row < 6, tail, 0.0))
    q = 2.0 / DIM
    src = jnp.concatenate([x1, x1, x2, x1, x3, x2, src_norm, zero], axis=0)
    dst = jnp.concatenate([x1 * q, x2 * q, x1 * q, x3 * q, x1 * q, x2 * q, dst_norm, zero], axis=0)
    return src, dst


def pack(onehot, x):
    total = None
    for part in split3(x):
        zero = jnp.zeros_like(part)
        wide = jnp.concatenate(
            [jnp.concatenate([part, zero], axis=1), jnp.concatenate([zero, part], axis=1)], axis=0
        )
        term = dot(onehot, wide, 1, 1)
        total = term if total is None else total + term
    return total


def unpack(onehot, g):
    half = g.shape[1] // 2
    cols = onehot.shape[1] // 2
    gt = jnp.transpose(g)
    total = None
    for part in split3(gt):
        term = dot(part, onehot)
        total = term if total is None else total + term
    return total[:half, :cols] + total[half:, cols:]


def kernel(
    sizes,
    targets_h, tree_pos_h, coords_h, ubasis_h, transfer_one_h, transfer_two_h, anchors_one_h,
    anchors_two_h, near_list, far_one, far_two,
    result,
    targets, tree_pos, coords, ubasis, transfer_one, transfer_two, anchors_one, anchors_two,
    oh_user, oh_tree, s_a, r_a, s_b, r_b, s_c, r_c, s_d, r_d, s_e, r_e, s_f, r_f,
    r_coords, s_anch, r_anch, s_top, r_top, s_g, r_g, ct_full, r_ct,
    src_pts, w_hi, w_lo, k1_hi, k1_lo, k2_hi, k2_lo, c_hi, c_lo, ct_hi, ct_lo, m_hi, m_lo, mc_hi, mc_lo,
    tg_hi, tg_lo,
    wbuf, acc, tu_near, r_halo, qbuf, s1, r1, s2, r2, s3, r3,
    in_sem, set_send, set_recv, halo_send, halo_recv, send1, recv1, send2, recv2, send3, recv3,
):
    n_leaf, n_lvl = sizes
    n_dev = n_leaf * n_lvl
    leaf, lvl = lax.axis_index("leaf"), lax.axis_index("lvl")
    rows, pts = targets.shape
    clusters = ubasis.shape[0]
    points = ubasis.shape[2]
    ranks = ubasis.shape[1]
    half = LANES // 2
    total = n_dev * clusters
    near_lists = near_list.shape[1]
    lower_count = far_one.shape[1]
    upper_count = far_two.shape[1]

    inputs = []
    pairs = (
        (tree_pos_h, tree_pos), (targets_h, targets), (transfer_one_h, transfer_one),
        (ubasis_h, ubasis), (transfer_two_h, transfer_two), (coords_h, coords),
        (anchors_one_h, anchors_one), (anchors_two_h, anchors_two),
    )
    for k, (hbm, vmem) in enumerate(pairs):
        inputs.append(pltpu.make_async_copy(hbm, vmem, in_sem.at[k]))
        inputs[-1].start()

    chips_z, cores = 8, 2
    chips_y, chips_x = n_leaf // chips_z, n_lvl // cores

    def others(long, short):
        pairs = [(a, b) for a in range(long) for b in range(short)][1:]
        far = lambda p: min(p[0], long - p[0]) + min(p[1], short - p[1]) * (short > 2)
        return sorted(pairs, key=lambda p: -far(p))

    def shifted(index, short, long, a, b):
        return lax.rem(index // short + a, long) * short + lax.rem(lax.rem(index, short) + b, short)

    leaf_peers = [shifted(leaf, chips_z, chips_y, a, b) for a, b in others(chips_y, chips_z)]
    lvl_peers = [shifted(lvl, cores, chips_x, a, b) for a, b in others(chips_x, cores)]
    leaf_before, leaf_after = lax.rem(leaf + n_leaf - 1, n_leaf), lax.rem(leaf + 1, n_leaf)

    ring = leaf * n_lvl + lvl
    after = lax.rem(ring + 1, n_dev)
    before = lax.rem(ring + n_dev - 1, n_dev)
    after_id = (after // n_lvl, lax.rem(after, n_lvl))
    before_id = (before // n_lvl, lax.rem(before, n_lvl))

    def copy(src, dst, send, recv, device):
        pltpu.make_async_remote_copy(
            src_ref=src, dst_ref=dst, send_sem=send, recv_sem=recv,
            device_id=device, device_id_type=MESH,
        ).start()

    def wait(ref, sem):
        pltpu.make_async_copy(ref, ref, sem).wait()

    def over_lvl(src, dst, send, recv):
        for peer in lvl_peers:
            copy(src(peer), dst, send, recv, (leaf, peer))

    def over_leaf(src, dst, send, recv):
        for peer in leaf_peers:
            copy(src(peer), dst, send, recv, (peer, lvl))

    barrier = pltpu.get_barrier_semaphore()
    for peer in leaf_peers:
        pl.semaphore_signal(barrier, inc=1, device_id=(peer, lvl), device_id_type=MESH)
    for peer in lvl_peers:
        pl.semaphore_signal(barrier, inc=1, device_id=(leaf, peer), device_id_type=MESH)
    pl.semaphore_signal(barrier, inc=1, device_id=after_id, device_id_type=MESH)
    pl.semaphore_signal(barrier, inc=1, device_id=before_id, device_id_type=MESH)

    lane = iota((8, LANES), 1)
    low = lane < half
    row8 = iota((8, LANES), 0)
    low_rows = iota((rows, LANES), 1) < half

    inputs[0].wait()
    tp = tree_pos[...]
    dest = lax.div(tp, pts)
    place = lax.rem(dest, n_lvl) * n_leaf + lax.div(dest, n_lvl)
    hit = iota((n_dev, pts), 0) == place
    hit16 = hit.astype(F32).astype(BF16)
    earlier = (iota((pts, pts), 0) < iota((pts, pts), 1)).astype(F32).astype(BF16)
    seen = dot(hit16, earlier)
    oh_user[:, :pts] = jnp.where(hit & (seen < 0.5), 1.0, 0.0).astype(BF16)
    oh_user[:, pts:] = jnp.where(hit & (seen > 0.5), 1.0, 0.0).astype(BF16)
    inputs[1].wait()
    blocks = n_leaf // 8
    packed = pack(oh_user[...], targets[...])
    s_a[:, :blocks] = packed.reshape(n_lvl, blocks, 8, LANES)
    pos = lax.rem(tp, pts).astype(F32)
    pos_hi = pos.astype(BF16).astype(F32)
    row16 = iota((16, pts), 0)
    terms = jnp.where(row16 == 0, pos_hi, jnp.where(row16 == 1, pos - pos_hi, 0.0)).astype(BF16)
    tile = jnp.zeros((8, LANES), F32)
    for h in range(2):
        both = dot(terms, oh_user[:, h * pts : (h + 1) * pts], 1, 1)
        line = both[0:1] + both[1:2]
        for q in range(n_dev // LANES):
            part = line[:, q * LANES : (q + 1) * LANES]
            tile = jnp.where(row8 == 2 * h + q, part, tile)
    for p in range(n_lvl):
        s_a[p, blocks] = tile
    r_a[lvl] = s_a[lvl]

    for k in range(2, len(pairs)):
        inputs[k].wait()
    own_one = jnp.concatenate([anchors_one[0], anchors_one[0]], axis=1)
    own_two = jnp.concatenate([anchors_two[0], anchors_two[0]], axis=1)
    partner = jnp.full((8, LANES), -1.0, F32)
    for k in range(lower_count):
        value = lax.rem(far_one[0, k], n_lvl).astype(F32)
        partner = jnp.where(row8 == k, value, partner)
    s_anch[0] = own_one
    s_anch[1] = partner
    r_anch[lvl] = s_anch[...]
    partner = own_two
    for k in range(upper_count):
        value = far_two[0, k].astype(F32)
        partner = jnp.where(jnp.logical_and(row8 == k, jnp.logical_not(low)), value, partner)
    s_top[...] = partner
    r_top[leaf] = partner

    pl.semaphore_wait(barrier, n_lvl + n_leaf)

    over_lvl(lambda p: s_a.at[p], r_a.at[lvl], set_send.at[0], set_recv.at[0])
    copy(coords, r_coords.at[0], set_send.at[1], set_recv.at[1], after_id)
    copy(coords, r_coords.at[1], set_send.at[2], set_recv.at[2], before_id)
    over_lvl(lambda p: s_anch, r_anch.at[lvl], set_send.at[3], set_recv.at[3])
    over_leaf(lambda p: s_top, r_top.at[leaf], set_send.at[4], set_recv.at[4])

    bt = jnp.concatenate(
        [dot_precise(jnp.transpose(transfer_one[c]), ubasis[c]) for c in range(clusters)], axis=1
    )
    b2t = dot_precise(jnp.transpose(transfer_two[0]), bt)
    ct = jnp.concatenate([bt, b2t], axis=0)
    c = jnp.transpose(ct)
    ct_full[...] = b2t
    ct_hi[...], ct_lo[...] = split2(ct)
    c_hi[...], c_lo[...] = split2(c)
    s_g[...] = dot_split(b2t, c_hi[...], c_lo[...])
    r_g[lvl] = s_g[...]

    wait(r_a.at[pl.ds(0, n_lvl - 1)], set_recv.at[0])
    s_b[:, :n_lvl] = jnp.swapaxes(r_a[:, :blocks].reshape(n_lvl, n_leaf, LANES), 0, 1)
    per_row = LANES // n_leaf
    mine = []
    for h in range(2):
        line = jnp.where(lvl < per_row, r_a[:, blocks, 2 * h], r_a[:, blocks, 2 * h + 1])
        turned = line
        for k in range(1, per_row):
            here = lax.rem(lvl, per_row) == k
            turned = jnp.where(here, pltpu.roll(line, LANES - k * n_leaf, 1), turned)
        mine.append(turned)
    square = jnp.concatenate(mine + [jnp.zeros((LANES - 16, LANES), F32)], axis=0)
    s_b[:, n_lvl : n_lvl + 1] = jnp.transpose(square)[:n_leaf].reshape(n_leaf, 1, LANES)
    r_b[leaf] = s_b[leaf]
    over_leaf(lambda p: s_b.at[p], r_b.at[leaf], set_send.at[5], set_recv.at[5])
    over_lvl(lambda p: s_g, r_g.at[lvl], set_send.at[8], set_recv.at[8])
    copy(ct_full, r_ct.at[0], set_send.at[6], set_recv.at[6], after_id)
    copy(ct_full, r_ct.at[1], set_send.at[7], set_recv.at[7], before_id)

    wait(r_coords.at[0], set_recv.at[1])
    wait(r_coords.at[1], set_recv.at[2])
    src, dst = augmented(coords[...])
    src_pts[pts : 2 * pts] = jnp.transpose(src).astype(BF16)
    src_pts[:pts] = jnp.transpose(augmented(r_coords[0])[0]).astype(BF16)
    src_pts[2 * pts :] = jnp.transpose(augmented(r_coords[1])[0]).astype(BF16)
    dst = dst.astype(BF16)
    first = ring * clusters - clusters
    near_scale = (points * (near_lists + 1)) ** (-0.5)

    def near_rows(n, carry):
        at = pl.ds(pl.multiple_of(n * points, points), points)
        value = jnp.exp(dot(src_pts[at, :], dst))
        parts = []
        for c in range(clusters):
            weight = (n == c + clusters).astype(jnp.int32)
            for k in range(near_lists):
                rel = lax.rem(near_list[c, k] - first + total, total)
                weight = weight + (rel == n).astype(jnp.int32)
            scaled = weight.astype(F32) * near_scale
            parts.append(value[:, c * points : (c + 1) * points] * scaled)
        hi, lo = split2(jnp.concatenate(parts, axis=1))
        w_hi[at, :] = hi
        w_lo[at, :] = lo
        return carry

    lax.fori_loop(0, 3 * clusters, near_rows, 0)

    def lanes_of(get):
        tiles = []
        for m in range(n_lvl // 2):
            tiles.append(jnp.where(low, get(2 * m), get(2 * m + 1)))
        return jnp.concatenate(tiles, axis=1)

    wait(r_anch.at[pl.ds(0, n_lvl - 1)], set_recv.at[3])
    src, dst = augmented(lanes_of(lambda p: r_anch[p, 0]))
    wide = n_lvl * ranks
    partners = lanes_of(lambda p: r_anch[p, 1])
    owner = lax.div(iota((wide, wide), 0), ranks).astype(F32)
    count = jnp.zeros((wide, wide), F32)
    for k in range(lower_count):
        count = count + jnp.where(owner == partners[k : k + 1], 1.0, 0.0)
    value = jnp.exp(dot(jnp.transpose(src).astype(BF16), dst.astype(BF16)))
    k1_hi[...], k1_lo[...] = split2(value * count * (lower_count ** (-0.5)))

    wait(r_top.at[pl.ds(0, n_leaf - 1)], set_recv.at[4])
    groups = (leaf, leaf_before, leaf_after)

    def chosen(lists, get):
        lists = jnp.where(low, pltpu.roll(lists, half, 1), lists)
        picks = [get(0)] * upper_count
        named = [jnp.broadcast_to(lists[k : k + 1], picks[0].shape) for k in range(upper_count)]
        for q in range(1, n_leaf):
            value = get(q)
            picks = [jnp.where(n == float(q), value, p) for n, p in zip(named, picks)]
        return picks

    for g, group in enumerate(groups):
        tops = chosen(r_top[group], lambda q: r_top[q])
        src, _ = augmented(
            jnp.concatenate(
                [jnp.where(low, tops[m], pltpu.roll(tops[m + 1], half, 1)) for m in (0, 2)], axis=1
            )
        )
        mine = r_top[group]
        _, dst = augmented(jnp.where(low, mine, pltpu.roll(mine, half, 1)))
        value = jnp.exp(dot(jnp.transpose(src).astype(BF16), dst.astype(BF16)))
        first_half = iota(value.shape, 1) < half
        value = jnp.where(first_half, 0.0, value) if g == 0 else jnp.where(first_half, value, 0.0)
        k2_hi[g], k2_lo[g] = split2(value * (upper_count ** (-0.5)))

    wait(r_g.at[pl.ds(0, n_lvl - 1)], set_recv.at[8])
    low_ranks = iota((ranks, LANES), 1) < half
    gamma = r_g[0]
    for p in range(1, n_lvl):
        gamma = gamma + r_g[p]
    tiles = [
        jnp.where(low_ranks, r_g[2 * m], pltpu.roll(r_g[2 * m + 1], half, 1))
        for m in range(n_lvl // 2)
    ]
    tiles.append(jnp.where(low_ranks, 0.0, gamma))
    tg = jnp.concatenate(tiles, axis=1)
    tg_hi[...], tg_lo[...] = split2(jnp.concatenate([jnp.zeros_like(tg), tg], axis=0))
    wait(r_ct.at[0], set_recv.at[6])
    wait(r_ct.at[1], set_recv.at[7])
    z_own = dot_split(ct_full[...], w_hi[pts : 2 * pts], w_lo[pts : 2 * pts])
    z_prev = dot_split(r_ct[0], w_hi[:pts], w_lo[:pts])
    z_next = dot_split(r_ct[1], w_hi[2 * pts :], w_lo[2 * pts :])
    at_first = (lvl == 0).astype(F32)
    at_last = (lvl == n_lvl - 1).astype(F32)
    z_main = z_own + z_prev * (1.0 - at_first) + z_next * (1.0 - at_last)
    z_edge = z_prev * at_first + z_next * at_last
    m = jnp.concatenate([bt, z_main, z_edge, jnp.zeros_like(z_edge)], axis=0)
    m_hi[...], m_lo[...] = split2(m)
    mc_hi[...], mc_lo[...] = split2(dot_split(m, c_hi[...], c_lo[...]))

    wait(r_b.at[pl.ds(0, n_leaf - 1)], set_recv.at[5])
    column = iota((n_dev, pts), 1).astype(F32)
    row3 = iota((n_leaf, n_lvl, LANES), 1)
    lane3 = iota((n_leaf, n_lvl, LANES), 2)
    line = jnp.broadcast_to(r_b[:, n_lvl : n_lvl + 1], (n_leaf, n_lvl, LANES))
    for h in range(2):
        got = jnp.where(lane3 == row3 + h * n_lvl, line, 0.0).reshape(n_dev, LANES)
        got = jnp.sum(got, axis=1, keepdims=True)
        oh_tree[:, h * pts : (h + 1) * pts] = jnp.where(column == got, 1.0, 0.0).astype(BF16)
    wbuf[0] = unpack(oh_tree[...], r_b[:, :n_lvl].reshape(n_dev, LANES))

    def send_halo(j):
        copy(wbuf.at[j], r_halo.at[j, 0], halo_send.at[j, 0], halo_recv.at[j, 0], after_id)
        copy(wbuf.at[j], r_halo.at[j, 1], halo_send.at[j, 1], halo_recv.at[j, 1], before_id)

    def scatter(j, value):
        s1[j] = value.reshape(n_lvl, 8, LANES)
        over_lvl(lambda peer: s1.at[j, peer], r1.at[j, lvl], send1.at[j], recv1.at[j])
        r1[j, lvl] = s1[j, lvl]

    def broadcast_to(j, peers):
        for peer in peers:
            copy(s2.at[j], r2.at[j, leaf], send2.at[j], recv2.at[j], (peer, lvl))

    far_peers, near_peers = leaf_peers[:12], leaf_peers[12:]

    def broadcast_far(j, lower, upper):
        value = jnp.where(low[:4], lower[:4], upper[4:])
        s2[j] = value
        broadcast_to(j, far_peers)
        r2[j, leaf] = value

    def half_rows(a, b):
        turned_a, turned_b = pltpu.roll(a, half, 1), pltpu.roll(b, half, 1)
        return jnp.concatenate(
            [jnp.where(low[:4], a, turned_b), jnp.where(low[:4], turned_a, b)], axis=0
        )

    def gather(j):
        over_lvl(lambda peer: s3.at[j, peer], r3.at[j, lvl], send3.at[j], recv3.at[j])
        r3[j, lvl] = s3[j, lvl]

    def wait1(j):
        wait(r1.at[j, pl.ds(0, n_lvl - 1)], recv1.at[j])

    def wait2(j):
        wait(r2.at[j, pl.ds(0, n_leaf - 1)], recv2.at[j])

    def wait3(j):
        wait(r3.at[j, pl.ds(0, n_lvl - 1)], recv3.at[j])

    def send_potentials(j, f1, f2, edges):
        for d in range(n_lvl):
            tile = jnp.zeros((8, LANES), F32)
            if f1 is not None:
                tile = f1[:, (d // 2) * LANES : (d // 2 + 1) * LANES]
                if d % 2:
                    tile = pltpu.roll(tile, half, 1)
            s3[j, d, 0] = jnp.where(low, tile, f2)
            s3[j, d, 1] = edges[0] if d == 0 else edges[1] if d == n_lvl - 1 else jnp.zeros_like(f2)
        gather(j)

    def level_one(own, extra):
        tiles = [
            jnp.where(low, own[2 * m], pltpu.roll(own[2 * m + 1], half, 1))
            for m in range(n_lvl // 2)
        ]
        t = jnp.concatenate(tiles, axis=1)
        if extra is not None:
            t = t + extra
        return dot_split(t, k1_hi[...], k1_lo[...])

    def packed_back(value):
        return pack(oh_tree[...], value).reshape(n_leaf, n_lvl, LANES)

    def unpacked(rows_back):
        return unpack(oh_user[...], rows_back.reshape(n_dev, LANES))

    zero8 = jnp.zeros((8, LANES), F32)
    scatter(0, dot_split(wbuf[0], c_hi[...], c_lo[...]))
    send_halo(0)
    acc[...] = dot_split(wbuf[0], w_hi[pts : 2 * pts], w_lo[pts : 2 * pts])
    wait1(0)
    got = r1[0]
    up = jnp.sum(got, axis=0)
    broadcast_far(0, pltpu.roll(up, half, 1), up)
    send_potentials(0, level_one(got, None), zero8, (zero8, zero8))
    broadcast_to(0, near_peers)

    def body(j, last):
        wait(r_halo.at[j, 0], halo_recv.at[j, 0])
        near = acc[...] + dot_split(r_halo[j, 0], w_hi[:pts], w_lo[:pts])
        wait(r_halo.at[j, 1], halo_recv.at[j, 1])
        near = near + dot_split(r_halo[j, 1], w_hi[2 * pts :], w_lo[2 * pts :])
        acc[...] = near
        if not last:
            tu_near[...] = dot_split(near, c_hi[...], c_lo[...])

        wait3(j)
        main = r3[j, :, 0].reshape(rows, LANES)
        edge = r3[j, :, 1].reshape(rows, LANES)
        moved = jnp.concatenate([main, edge], axis=1)
        if not last:
            scatter(j + 1, tu_near[...] + dot_split(moved, mc_hi[...], mc_lo[...]))
        w_next = acc[...] + dot_split(moved, m_hi[...], m_lo[...])
        wbuf[j + 1] = w_next
        if not last:
            send_halo(j + 1)
            acc[...] = dot_split(w_next, w_hi[pts : 2 * pts], w_lo[pts : 2 * pts])
        power = wbuf[j] + dot_split(jnp.where(low_rows, 0.0, main), ct_hi[...], ct_lo[...])
        square = jnp.sum(power * power, axis=1, keepdims=True)
        if last:
            part = lax.rem(iota((rows, LANES), 1), half) // (half // 4)
            sums = jnp.where(part == 3, square, 0.0)
            for k in range(3):
                sums = jnp.where(part == k, qbuf[k + 1], sums)
            scatter(j + 1, sums)
        else:
            qbuf[j] = jnp.broadcast_to(square, (rows, LANES))

            @pl.when(j == 1)
            def _():
                s_c[:, 0] = packed_back(power)

            @pl.when(j == 3)
            def _():
                s_c[:, 1] = packed_back(power)
                r_c[leaf] = s_c[leaf]
                over_leaf(lambda p: s_c.at[p], r_c.at[leaf], set_send.at[9], set_recv.at[9])

        wait2(j)
        potentials = []
        for g, group in enumerate(groups):
            ups = chosen(r_top[group], lambda q: r2[j, q])
            tiles = [half_rows(ups[m], ups[m + 1]) for m in (0, 2)]
            potentials.append(dot_split(jnp.concatenate(tiles, axis=1), k2_hi[g], k2_lo[g]))
        f2, edges = potentials[0], potentials[1:]
        if last:
            send_potentials(j + 1, None, f2, edges)
            wait1(j + 1)
            sums = jnp.sum(r1[j + 1], axis=0)
            broadcast_far(j + 1, sums, sums)
            broadcast_to(j + 1, near_peers)
            return
        add = dot_split(f2, tg_hi[...], tg_lo[...])
        wait1(j + 1)
        got = r1[j + 1]
        up = jnp.sum(got, axis=0) + add[:, wide:]
        broadcast_far(j + 1, pltpu.roll(up, half, 1), up)
        send_potentials(j + 1, level_one(got, add[:, :wide]), f2, edges)
        broadcast_to(j + 1, near_peers)

    def step(j, carry):
        body(j, False)
        return carry

    lax.fori_loop(0, APPLIES - 1, step, 0)
    body(APPLIES - 1, True)

    wait(r_c.at[pl.ds(0, n_leaf - 1)], set_recv.at[9])
    for kind in range(2):
        s_d[:, kind] = jnp.swapaxes(r_c[:, kind], 0, 1)
    r_d[lvl] = s_d[lvl]
    over_lvl(lambda p: s_d.at[p], r_d.at[lvl], set_send.at[10], set_recv.at[10])

    wait3(APPLIES)
    main = r3[APPLIES, :, 0].reshape(rows, LANES)
    s_e[...] = packed_back(
        wbuf[APPLIES] + dot_split(jnp.where(low_rows, 0.0, main), ct_hi[...], ct_lo[...])
    )
    r_e[leaf] = s_e[leaf]
    over_leaf(lambda p: s_e.at[p], r_e.at[leaf], set_send.at[11], set_recv.at[11])
    wait(r_d.at[pl.ds(0, n_lvl - 1)], set_recv.at[10])
    back1 = unpacked(r_d[:, 0])
    back3 = unpacked(r_d[:, 1])
    wait2(APPLIES)
    sums = jnp.sum(r2[APPLIES], axis=0)
    sums = jnp.concatenate([sums, pltpu.roll(sums, half, 1)], axis=0)
    for d in range(n_lvl):
        s3[APPLIES + 1, d, 0] = sums
        s3[APPLIES + 1, d, 1] = sums
    gather(APPLIES + 1)
    wait(r_e.at[pl.ds(0, n_leaf - 1)], set_recv.at[11])
    s_f[...] = jnp.swapaxes(r_e[...], 0, 1)
    r_f[lvl] = s_f[lvl]
    over_lvl(lambda p: s_f.at[p], r_f.at[lvl], set_send.at[12], set_recv.at[12])

    wait3(APPLIES + 1)
    sums = r3[APPLIES + 1, :, 0].reshape(rows, LANES)
    g1, g2, g3, g4 = (sums[:, k * (half // 4) : k * (half // 4) + 1] for k in range(4))
    step0 = g1 / (g2 + RIDGE * g1 + EPSILON)
    keep = 1.0 - RIDGE * step0
    fresh = keep * keep * g1 - 2.0 * step0 * keep * g2 + step0 * step0 * g3
    lead = keep + fresh / (g1 + EPSILON)
    direction_sq = lead * lead * g1 - 2.0 * lead * step0 * g2 + step0 * step0 * g3
    image_sq = lead * lead * g2 - 2.0 * lead * step0 * g3 + step0 * step0 * g4
    step1 = fresh / (image_sq + RIDGE * direction_sq + EPSILON)
    result[0] = (step0 + step1 * lead) * back1 - (step1 * step0) * back3
    partial = (keep - RIDGE * step1 * lead) * back1 - (
        step0 + step1 * (lead - RIDGE * step0)
    ) * back3
    wait(r_f.at[pl.ds(0, n_lvl - 1)], set_recv.at[12])
    result[1] = partial + (step1 * step0) * unpacked(r_f[...])

    wait(r_a.at[pl.ds(0, n_lvl - 1)], set_send.at[0])
    wait(r_coords.at[0], set_send.at[1])
    wait(r_coords.at[1], set_send.at[2])
    wait(r_anch.at[pl.ds(0, n_lvl - 1)], set_send.at[3])
    wait(r_top.at[pl.ds(0, n_leaf - 1)], set_send.at[4])
    wait(r_b.at[pl.ds(0, n_leaf - 1)], set_send.at[5])
    wait(r_ct.at[0], set_send.at[6])
    wait(r_ct.at[1], set_send.at[7])
    wait(r_g.at[pl.ds(0, n_lvl - 1)], set_send.at[8])
    wait(r_c.at[pl.ds(0, n_leaf - 1)], set_send.at[9])
    wait(r_d.at[pl.ds(0, n_lvl - 1)], set_send.at[10])
    wait(r_e.at[pl.ds(0, n_leaf - 1)], set_send.at[11])
    wait(r_f.at[pl.ds(0, n_lvl - 1)], set_send.at[12])

    def sent(j, carry):
        wait(r1.at[j, pl.ds(0, n_lvl - 1)], send1.at[j])
        wait(r2.at[j, pl.ds(0, n_leaf - 1)], send2.at[j])
        return carry

    lax.fori_loop(0, APPLIES + 1, sent, 0)

    def sent_halo(j, carry):
        wait(wbuf.at[j], halo_send.at[j, 0])
        wait(wbuf.at[j], halo_send.at[j, 1])
        return carry

    lax.fori_loop(0, APPLIES, sent_halo, 0)

    def sent_last(j, carry):
        wait(r3.at[j, pl.ds(0, n_lvl - 1)], send3.at[j])
        return carry

    lax.fori_loop(0, APPLIES + 2, sent_last, 0)


def on_device(
    targets, tree_pos, coords, ubasis, transfer_one, transfer_two, anchors_one, anchors_two,
    near_list, far_one, far_two,
):
    rows, pts = targets.shape
    n_leaf, n_lvl = lax.axis_size("leaf"), lax.axis_size("lvl")
    n_dev = n_leaf * n_lvl
    dim = coords.shape[0]
    ranks = anchors_one.shape[2]
    hbm = pl.BlockSpec(memory_space=pl.ANY)
    vmem = pl.BlockSpec(memory_space=pltpu.VMEM)
    smem = pl.BlockSpec(memory_space=pltpu.SMEM)
    V = pltpu.VMEM
    D = pltpu.SemaphoreType.DMA
    wide = n_lvl * ranks
    deep = far_two.shape[1] * ranks
    arrays = (
        targets, tree_pos.reshape(1, pts), coords, ubasis, transfer_one, transfer_two,
        anchors_one, anchors_two,
    )
    scratch = [V(a.shape, a.dtype) for a in arrays] + [
        V((n_dev, 2 * pts), BF16), V((n_dev, 2 * pts), BF16),
        V((n_lvl, n_leaf // 8 + 1, 8, LANES), F32), V((n_lvl, n_leaf // 8 + 1, 8, LANES), F32),
        V((n_leaf, n_lvl + 1, LANES), F32), V((n_leaf, n_lvl + 1, LANES), F32),
        V((n_leaf, 2, n_lvl, LANES), F32), V((n_leaf, 2, n_lvl, LANES), F32),
        V((n_lvl, 2, n_leaf, LANES), F32), V((n_lvl, 2, n_leaf, LANES), F32),
        V((n_leaf, n_lvl, LANES), F32), V((n_leaf, n_lvl, LANES), F32),
        V((n_lvl, n_leaf, LANES), F32), V((n_lvl, n_leaf, LANES), F32),
        V((2, dim, pts), F32),
        V((2, 8, LANES), F32), V((n_lvl, 2, 8, LANES), F32),
        V((8, LANES), F32), V((n_leaf, 8, LANES), F32),
        V((ranks, LANES), F32), V((n_lvl, ranks, LANES), F32),
        V((ranks, pts), F32), V((2, ranks, pts), F32),
        V((3 * pts, 64), BF16),
        V((3 * pts, pts), BF16), V((3 * pts, pts), BF16),
        V((wide, wide), BF16), V((wide, wide), BF16),
        V((3, deep, LANES), BF16), V((3, deep, LANES), BF16),
        V((pts, LANES), BF16), V((pts, LANES), BF16),
        V((LANES, pts), BF16), V((LANES, pts), BF16),
        V((2 * LANES, pts), BF16), V((2 * LANES, pts), BF16),
        V((2 * LANES, LANES), BF16), V((2 * LANES, LANES), BF16),
        V((LANES, wide + LANES), BF16), V((LANES, wide + LANES), BF16),
        V((APPLIES + 1, rows, pts), F32), V((rows, pts), F32), V((rows, LANES), F32),
        V((APPLIES, 2, rows, pts), F32), V((APPLIES - 1, rows, LANES), F32),
        V((APPLIES + 1, n_lvl, 8, LANES), F32), V((APPLIES + 1, n_lvl, 8, LANES), F32),
        V((APPLIES + 1, 4, LANES), F32), V((APPLIES + 1, n_leaf, 4, LANES), F32),
        V((APPLIES + 2, n_lvl, 2, 8, LANES), F32), V((APPLIES + 2, n_lvl, 2, 8, LANES), F32),
        D((len(arrays),)), D((13,)), D((13,)),
        D((APPLIES, 2)), D((APPLIES, 2)),
        D((APPLIES + 1,)), D((APPLIES + 1,)), D((APPLIES + 1,)), D((APPLIES + 1,)),
        D((APPLIES + 2,)), D((APPLIES + 2,)),
    ]
    out = jax.ShapeDtypeStruct((2, rows, pts), F32)
    body = lambda *refs: kernel((n_leaf, n_lvl), *refs)
    both = pl.pallas_call(
        body,
        out_shape=out,
        in_specs=[hbm] * len(arrays) + [smem] * 3,
        out_specs=vmem,
        scratch_shapes=scratch,
        compiler_params=pltpu.CompilerParams(
            collective_id=0, has_side_effects=True, vmem_limit_bytes=60 * 1024 * 1024
        ),
    )(*arrays, near_list, far_one, far_two)
    return both[0], both[1]


def solution(mesh):
    both = ("leaf", "lvl")
    return jax.shard_map(
        on_device,
        mesh=mesh,
        in_specs=(
            P(None, both), P(both), P(None, both), P(both, None, None), P(both, None, None),
            P(both, None, None), P(both, None, None), P("leaf", None, None),
            P(both, None), P(both, None), P("leaf", None),
        ),
        out_specs=(P(None, both), P(None, both)),
        check_vma=False,
    )
```

```python
import jax
import jax.numpy as jnp
from jax import lax
from jax.experimental import pallas as pl
from jax.experimental.pallas import tpu as pltpu
from jax.sharding import PartitionSpec as P

F32 = jnp.float32
BF16 = jnp.bfloat16
MESH = pl.DeviceIdType.MESH
PRECISE = lax.Precision.HIGHEST
DIM = 8
RIDGE = 1.0
EPSILON = 1e-6
APPLIES = 5
LANES = 128


def dot(a, b, ca=1, cb=0):
    return lax.dot_general(a, b, (((ca,), (cb,)), ((), ())), preferred_element_type=F32)


def dot_precise(a, b):
    return lax.dot_general(
        a, b, (((1,), (0,)), ((), ())), precision=PRECISE, preferred_element_type=F32
    )


def split2(x):
    hi = x.astype(BF16)
    return hi, (x - hi.astype(F32)).astype(BF16)


def split3(x):
    hi = x.astype(BF16)
    rest = x - hi.astype(F32)
    mid = rest.astype(BF16)
    return hi, mid, (rest - mid.astype(F32)).astype(BF16)


def dot_split(a, b_hi, b_lo):
    rows = a.shape[0]
    a_hi, a_lo = split2(a)
    both = dot(jnp.concatenate([a_hi, a_lo], axis=0), b_hi)
    return both[:rows] + both[rows:] + dot(a_hi, b_lo)


def iota(shape, dim):
    return lax.broadcasted_iota(jnp.int32, shape, dim)


def augmented(x):
    n = x.shape[1]
    x1, x2, x3 = (p.astype(F32) for p in split3(x))
    sq = jnp.sum(x * x, axis=0, keepdims=True) * (-1.0 / DIM)
    n1, n2, n3 = (p.astype(F32) for p in split3(sq))
    row = iota((8, n), 0)
    lead = jnp.where(row == 0, n1, jnp.where(row == 1, n2, n3))
    tail = jnp.where(row == 3, n1, jnp.where(row == 4, n2, n3))
    zero = jnp.zeros((8, n), F32)
    src_norm = jnp.where(row < 3, lead, jnp.where(row < 6, 1.0, 0.0))
    dst_norm = jnp.where(row < 3, 1.0, jnp.where(row < 6, tail, 0.0))
    q = 2.0 / DIM
    src = jnp.concatenate([x1, x1, x2, x1, x3, x2, src_norm, zero], axis=0)
    dst = jnp.concatenate([x1 * q, x2 * q, x1 * q, x3 * q, x1 * q, x2 * q, dst_norm, zero], axis=0)
    return src, dst


def pack(onehot, x):
    total = None
    for part in split3(x):
        zero = jnp.zeros_like(part)
        wide = jnp.concatenate(
            [jnp.concatenate([part, zero], axis=1), jnp.concatenate([zero, part], axis=1)], axis=0
        )
        term = dot(onehot, wide, 1, 1)
        total = term if total is None else total + term
    return total


def unpack(onehot, g):
    half = g.shape[1] // 2
    cols = onehot.shape[1] // 2
    gt = jnp.transpose(g)
    total = None
    for part in split3(gt):
        term = dot(part, onehot)
        total = term if total is None else total + term
    return total[:half, :cols] + total[half:, cols:]


def kernel(
    sizes,
    targets_h, tree_pos_h, coords_h, ubasis_h, transfer_one_h, transfer_two_h, anchors_one_h,
    anchors_two_h, near_list, far_one, far_two,
    result,
    targets, tree_pos, coords, ubasis, transfer_one, transfer_two, anchors_one, anchors_two,
    oh_user, oh_tree, s_a, r_a, s_b, r_b, s_c, r_c, s_d, r_d, s_e, r_e, s_f, r_f,
    r_coords, s_anch, r_anch, s_top, r_top, s_g, r_g, ct_full, r_ct,
    src_pts, w_hi, w_lo, k1_hi, k1_lo, k2_hi, k2_lo, c_hi, c_lo, ct_hi, ct_lo, m_hi, m_lo, mc_hi, mc_lo,
    tg_hi, tg_lo,
    wbuf, acc, tu_near, r_halo, qbuf, s1, r1, s2, r2, s3, r3,
    in_sem, set_send, set_recv, halo_send, halo_recv, send1, recv1, send2, recv2, send3, recv3,
):
    n_leaf, n_lvl = sizes
    n_dev = n_leaf * n_lvl
    leaf, lvl = lax.axis_index("leaf"), lax.axis_index("lvl")
    rows, pts = targets.shape
    clusters = ubasis.shape[0]
    points = ubasis.shape[2]
    ranks = ubasis.shape[1]
    half = LANES // 2
    total = n_dev * clusters
    near_lists = near_list.shape[1]
    lower_count = far_one.shape[1]
    upper_count = far_two.shape[1]

    inputs = []
    pairs = (
        (tree_pos_h, tree_pos), (targets_h, targets), (transfer_one_h, transfer_one),
        (ubasis_h, ubasis), (transfer_two_h, transfer_two), (coords_h, coords),
        (anchors_one_h, anchors_one), (anchors_two_h, anchors_two),
    )
    for k, (hbm, vmem) in enumerate(pairs):
        inputs.append(pltpu.make_async_copy(hbm, vmem, in_sem.at[k]))
        inputs[-1].start()

    chips_z, cores = 8, 2
    chips_y, chips_x = n_leaf // chips_z, n_lvl // cores

    def others(long, short):
        pairs = [(a, b) for a in range(long) for b in range(short)][1:]
        far = lambda p: min(p[0], long - p[0]) + min(p[1], short - p[1]) * (short > 2)
        return sorted(pairs, key=lambda p: -far(p))

    def shifted(index, short, long, a, b):
        return lax.rem(index // short + a, long) * short + lax.rem(lax.rem(index, short) + b, short)

    leaf_peers = [shifted(leaf, chips_z, chips_y, a, b) for a, b in others(chips_y, chips_z)]
    lvl_peers = [shifted(lvl, cores, chips_x, a, b) for a, b in others(chips_x, cores)]
    leaf_before, leaf_after = lax.rem(leaf + n_leaf - 1, n_leaf), lax.rem(leaf + 1, n_leaf)

    ring = leaf * n_lvl + lvl
    after = lax.rem(ring + 1, n_dev)
    before = lax.rem(ring + n_dev - 1, n_dev)
    after_id = (after // n_lvl, lax.rem(after, n_lvl))
    before_id = (before // n_lvl, lax.rem(before, n_lvl))

    def copy(src, dst, send, recv, device):
        pltpu.make_async_remote_copy(
            src_ref=src, dst_ref=dst, send_sem=send, recv_sem=recv,
            device_id=device, device_id_type=MESH,
        ).start()

    def wait(ref, sem):
        pltpu.make_async_copy(ref, ref, sem).wait()

    def over_lvl(src, dst, send, recv):
        for peer in lvl_peers:
            copy(src(peer), dst, send, recv, (leaf, peer))

    def over_leaf(src, dst, send, recv):
        for peer in leaf_peers:
            copy(src(peer), dst, send, recv, (peer, lvl))

    barrier = pltpu.get_barrier_semaphore()
    for peer in leaf_peers:
        pl.semaphore_signal(barrier, inc=1, device_id=(peer, lvl), device_id_type=MESH)
    for peer in lvl_peers:
        pl.semaphore_signal(barrier, inc=1, device_id=(leaf, peer), device_id_type=MESH)
    pl.semaphore_signal(barrier, inc=1, device_id=after_id, device_id_type=MESH)
    pl.semaphore_signal(barrier, inc=1, device_id=before_id, device_id_type=MESH)

    lane = iota((8, LANES), 1)
    low = lane < half
    row8 = iota((8, LANES), 0)
    low_rows = iota((rows, LANES), 1) < half

    inputs[0].wait()
    tp = tree_pos[...]
    dest = lax.div(tp, pts)
    place = lax.rem(dest, n_lvl) * n_leaf + lax.div(dest, n_lvl)
    hit = iota((n_dev, pts), 0) == place
    hit16 = hit.astype(F32).astype(BF16)
    earlier = (iota((pts, pts), 0) < iota((pts, pts), 1)).astype(F32).astype(BF16)
    seen = dot(hit16, earlier)
    oh_user[:, :pts] = jnp.where(hit & (seen < 0.5), 1.0, 0.0).astype(BF16)
    oh_user[:, pts:] = jnp.where(hit & (seen > 0.5), 1.0, 0.0).astype(BF16)
    inputs[1].wait()
    blocks = n_leaf // 8
    packed = pack(oh_user[...], targets[...])
    s_a[:, :blocks] = packed.reshape(n_lvl, blocks, 8, LANES)
    pos = lax.rem(tp, pts).astype(F32)
    pos_hi = pos.astype(BF16).astype(F32)
    row16 = iota((16, pts), 0)
    terms = jnp.where(row16 == 0, pos_hi, jnp.where(row16 == 1, pos - pos_hi, 0.0)).astype(BF16)
    tile = jnp.zeros((8, LANES), F32)
    for h in range(2):
        both = dot(terms, oh_user[:, h * pts : (h + 1) * pts], 1, 1)
        line = both[0:1] + both[1:2]
        for q in range(n_dev // LANES):
            part = line[:, q * LANES : (q + 1) * LANES]
            tile = jnp.where(row8 == 2 * h + q, part, tile)
    for p in range(n_lvl):
        s_a[p, blocks] = tile
    r_a[lvl] = s_a[lvl]

    for k in range(2, len(pairs)):
        inputs[k].wait()
    own_one = jnp.concatenate([anchors_one[0], anchors_one[0]], axis=1)
    own_two = jnp.concatenate([anchors_two[0], anchors_two[0]], axis=1)
    partner = jnp.full((8, LANES), -1.0, F32)
    for k in range(lower_count):
        value = lax.rem(far_one[0, k], n_lvl).astype(F32)
        partner = jnp.where(row8 == k, value, partner)
    s_anch[0] = own_one
    s_anch[1] = partner
    r_anch[lvl] = s_anch[...]
    partner = own_two
    for k in range(upper_count):
        value = far_two[0, k].astype(F32)
        partner = jnp.where(jnp.logical_and(row8 == k, jnp.logical_not(low)), value, partner)
    s_top[...] = partner
    r_top[leaf] = partner

    pl.semaphore_wait(barrier, n_lvl + n_leaf)

    over_lvl(lambda p: s_a.at[p], r_a.at[lvl], set_send.at[0], set_recv.at[0])
    copy(coords, r_coords.at[0], set_send.at[1], set_recv.at[1], after_id)
    copy(coords, r_coords.at[1], set_send.at[2], set_recv.at[2], before_id)
    over_lvl(lambda p: s_anch, r_anch.at[lvl], set_send.at[3], set_recv.at[3])
    over_leaf(lambda p: s_top, r_top.at[leaf], set_send.at[4], set_recv.at[4])

    bt = jnp.concatenate(
        [dot_precise(jnp.transpose(transfer_one[c]), ubasis[c]) for c in range(clusters)], axis=1
    )
    b2t = dot_precise(jnp.transpose(transfer_two[0]), bt)
    ct = jnp.concatenate([bt, b2t], axis=0)
    c = jnp.transpose(ct)
    ct_full[...] = b2t
    ct_hi[...], ct_lo[...] = split2(ct)
    c_hi[...], c_lo[...] = split2(c)
    s_g[...] = dot_split(b2t, c_hi[...], c_lo[...])
    r_g[lvl] = s_g[...]

    wait(r_a.at[pl.ds(0, n_lvl - 1)], set_recv.at[0])
    s_b[:, :n_lvl] = jnp.swapaxes(r_a[:, :blocks].reshape(n_lvl, n_leaf, LANES), 0, 1)
    per_row = LANES // n_leaf
    mine = []
    for h in range(2):
        line = jnp.where(lvl < per_row, r_a[:, blocks, 2 * h], r_a[:, blocks, 2 * h + 1])
        turned = line
        for k in range(1, per_row):
            here = lax.rem(lvl, per_row) == k
            turned = jnp.where(here, pltpu.roll(line, LANES - k * n_leaf, 1), turned)
        mine.append(turned)
    square = jnp.concatenate(mine + [jnp.zeros((LANES - 16, LANES), F32)], axis=0)
    s_b[:, n_lvl : n_lvl + 1] = jnp.transpose(square)[:n_leaf].reshape(n_leaf, 1, LANES)
    r_b[leaf] = s_b[leaf]
    over_leaf(lambda p: s_b.at[p], r_b.at[leaf], set_send.at[5], set_recv.at[5])
    over_lvl(lambda p: s_g, r_g.at[lvl], set_send.at[8], set_recv.at[8])
    copy(ct_full, r_ct.at[0], set_send.at[6], set_recv.at[6], after_id)
    copy(ct_full, r_ct.at[1], set_send.at[7], set_recv.at[7], before_id)

    wait(r_coords.at[0], set_recv.at[1])
    wait(r_coords.at[1], set_recv.at[2])
    src, dst = augmented(coords[...])
    src_pts[pts : 2 * pts] = jnp.transpose(src).astype(BF16)
    src_pts[:pts] = jnp.transpose(augmented(r_coords[0])[0]).astype(BF16)
    src_pts[2 * pts :] = jnp.transpose(augmented(r_coords[1])[0]).astype(BF16)
    dst = dst.astype(BF16)
    first = ring * clusters - clusters
    near_scale = (points * (near_lists + 1)) ** (-0.5)

    def near_rows(n, carry):
        at = pl.ds(pl.multiple_of(n * points, points), points)
        value = jnp.exp(dot(src_pts[at, :], dst))
        parts = []
        for c in range(clusters):
            weight = (n == c + clusters).astype(jnp.int32)
            for k in range(near_lists):
                rel = lax.rem(near_list[c, k] - first + total, total)
                weight = weight + (rel == n).astype(jnp.int32)
            scaled = weight.astype(F32) * near_scale
            parts.append(value[:, c * points : (c + 1) * points] * scaled)
        hi, lo = split2(jnp.concatenate(parts, axis=1))
        w_hi[at, :] = hi
        w_lo[at, :] = lo
        return carry

    lax.fori_loop(0, 3 * clusters, near_rows, 0)

    def lanes_of(get):
        tiles = []
        for m in range(n_lvl // 2):
            tiles.append(jnp.where(low, get(2 * m), get(2 * m + 1)))
        return jnp.concatenate(tiles, axis=1)

    wait(r_anch.at[pl.ds(0, n_lvl - 1)], set_recv.at[3])
    src, dst = augmented(lanes_of(lambda p: r_anch[p, 0]))
    wide = n_lvl * ranks
    partners = lanes_of(lambda p: r_anch[p, 1])
    owner = lax.div(iota((wide, wide), 0), ranks).astype(F32)
    count = jnp.zeros((wide, wide), F32)
    for k in range(lower_count):
        count = count + jnp.where(owner == partners[k : k + 1], 1.0, 0.0)
    value = jnp.exp(dot(jnp.transpose(src).astype(BF16), dst.astype(BF16)))
    k1_hi[...], k1_lo[...] = split2(value * count * (lower_count ** (-0.5)))

    wait(r_top.at[pl.ds(0, n_leaf - 1)], set_recv.at[4])
    groups = (leaf, leaf_before, leaf_after)

    def chosen(lists, get):
        lists = jnp.where(low, pltpu.roll(lists, half, 1), lists)
        picks = [get(0)] * upper_count
        named = [jnp.broadcast_to(lists[k : k + 1], picks[0].shape) for k in range(upper_count)]
        for q in range(1, n_leaf):
            value = get(q)
            picks = [jnp.where(n == float(q), value, p) for n, p in zip(named, picks)]
        return picks

    for g, group in enumerate(groups):
        tops = chosen(r_top[group], lambda q: r_top[q])
        src, _ = augmented(
            jnp.concatenate(
                [jnp.where(low, tops[m], pltpu.roll(tops[m + 1], half, 1)) for m in (0, 2)], axis=1
            )
        )
        mine = r_top[group]
        _, dst = augmented(jnp.where(low, mine, pltpu.roll(mine, half, 1)))
        value = jnp.exp(dot(jnp.transpose(src).astype(BF16), dst.astype(BF16)))
        first_half = iota(value.shape, 1) < half
        value = jnp.where(first_half, 0.0, value) if g == 0 else jnp.where(first_half, value, 0.0)
        k2_hi[g], k2_lo[g] = split2(value * (upper_count ** (-0.5)))

    wait(r_g.at[pl.ds(0, n_lvl - 1)], set_recv.at[8])
    low_ranks = iota((ranks, LANES), 1) < half
    gamma = r_g[0]
    for p in range(1, n_lvl):
        gamma = gamma + r_g[p]
    tiles = [
        jnp.where(low_ranks, r_g[2 * m], pltpu.roll(r_g[2 * m + 1], half, 1))
        for m in range(n_lvl // 2)
    ]
    tiles.append(jnp.where(low_ranks, 0.0, gamma))
    tg = jnp.concatenate(tiles, axis=1)
    tg_hi[...], tg_lo[...] = split2(jnp.concatenate([jnp.zeros_like(tg), tg], axis=0))
    wait(r_ct.at[0], set_recv.at[6])
    wait(r_ct.at[1], set_recv.at[7])
    z_own = dot_split(ct_full[...], w_hi[pts : 2 * pts], w_lo[pts : 2 * pts])
    z_prev = dot_split(r_ct[0], w_hi[:pts], w_lo[:pts])
    z_next = dot_split(r_ct[1], w_hi[2 * pts :], w_lo[2 * pts :])
    at_first = (lvl == 0).astype(F32)
    at_last = (lvl == n_lvl - 1).astype(F32)
    z_main = z_own + z_prev * (1.0 - at_first) + z_next * (1.0 - at_last)
    z_edge = z_prev * at_first + z_next * at_last
    m = jnp.concatenate([bt, z_main, z_edge, jnp.zeros_like(z_edge)], axis=0)
    m_hi[...], m_lo[...] = split2(m)
    mc_hi[...], mc_lo[...] = split2(dot_split(m, c_hi[...], c_lo[...]))

    wait(r_b.at[pl.ds(0, n_leaf - 1)], set_recv.at[5])
    column = iota((n_dev, pts), 1).astype(F32)
    row3 = iota((n_leaf, n_lvl, LANES), 1)
    lane3 = iota((n_leaf, n_lvl, LANES), 2)
    line = jnp.broadcast_to(r_b[:, n_lvl : n_lvl + 1], (n_leaf, n_lvl, LANES))
    for h in range(2):
        got = jnp.where(lane3 == row3 + h * n_lvl, line, 0.0).reshape(n_dev, LANES)
        got = jnp.sum(got, axis=1, keepdims=True)
        oh_tree[:, h * pts : (h + 1) * pts] = jnp.where(column == got, 1.0, 0.0).astype(BF16)
    wbuf[0] = unpack(oh_tree[...], r_b[:, :n_lvl].reshape(n_dev, LANES))

    def send_halo(j):
        copy(wbuf.at[j], r_halo.at[j, 0], halo_send.at[j, 0], halo_recv.at[j, 0], after_id)
        copy(wbuf.at[j], r_halo.at[j, 1], halo_send.at[j, 1], halo_recv.at[j, 1], before_id)

    def scatter(j, value):
        s1[j] = value.reshape(n_lvl, 8, LANES)
        over_lvl(lambda peer: s1.at[j, peer], r1.at[j, lvl], send1.at[j], recv1.at[j])
        r1[j, lvl] = s1[j, lvl]

    def broadcast_to(j, peers):
        for peer in peers:
            copy(s2.at[j], r2.at[j, leaf], send2.at[j], recv2.at[j], (peer, lvl))

    far_peers, near_peers = leaf_peers[:5], leaf_peers[5:]

    def broadcast_far(j, lower, upper):
        value = jnp.where(low[:4], lower[:4], upper[4:])
        s2[j] = value
        broadcast_to(j, far_peers)
        r2[j, leaf] = value

    def half_rows(a, b):
        turned_a, turned_b = pltpu.roll(a, half, 1), pltpu.roll(b, half, 1)
        return jnp.concatenate(
            [jnp.where(low[:4], a, turned_b), jnp.where(low[:4], turned_a, b)], axis=0
        )

    def gather(j):
        over_lvl(lambda peer: s3.at[j, peer], r3.at[j, lvl], send3.at[j], recv3.at[j])
        r3[j, lvl] = s3[j, lvl]

    def wait1(j):
        wait(r1.at[j, pl.ds(0, n_lvl - 1)], recv1.at[j])

    def wait2(j):
        wait(r2.at[j, pl.ds(0, n_leaf - 1)], recv2.at[j])

    def wait3(j):
        wait(r3.at[j, pl.ds(0, n_lvl - 1)], recv3.at[j])

    def send_potentials(j, f1, f2, edges):
        for d in range(n_lvl):
            tile = jnp.zeros((8, LANES), F32)
            if f1 is not None:
                tile = f1[:, (d // 2) * LANES : (d // 2 + 1) * LANES]
                if d % 2:
                    tile = pltpu.roll(tile, half, 1)
            s3[j, d, 0] = jnp.where(low, tile, f2)
            s3[j, d, 1] = edges[0] if d == 0 else edges[1] if d == n_lvl - 1 else jnp.zeros_like(f2)
        gather(j)

    def level_one(own, extra):
        tiles = [
            jnp.where(low, own[2 * m], pltpu.roll(own[2 * m + 1], half, 1))
            for m in range(n_lvl // 2)
        ]
        t = jnp.concatenate(tiles, axis=1)
        if extra is not None:
            t = t + extra
        return dot_split(t, k1_hi[...], k1_lo[...])

    def packed_back(value):
        return pack(oh_tree[...], value).reshape(n_leaf, n_lvl, LANES)

    def return_leaf(kind, value):
        s_c[kind] = packed_back(value)
        r_c[kind, leaf] = s_c[kind, leaf]
        sems = set_send.at[(9, 13)[kind]], set_recv.at[(9, 13)[kind]]
        over_leaf(lambda p: s_c.at[kind, p], r_c.at[kind, leaf], *sems)

    def unpacked(rows_back):
        return unpack(oh_user[...], rows_back.reshape(n_dev, LANES))

    zero8 = jnp.zeros((8, LANES), F32)
    scatter(0, dot_split(wbuf[0], c_hi[...], c_lo[...]))
    send_halo(0)
    acc[...] = dot_split(wbuf[0], w_hi[pts : 2 * pts], w_lo[pts : 2 * pts])
    wait1(0)
    got = r1[0]
    up = jnp.sum(got, axis=0)
    broadcast_far(0, pltpu.roll(up, half, 1), up)
    send_potentials(0, level_one(got, None), zero8, (zero8, zero8))
    broadcast_to(0, near_peers)

    def body(j, last):
        wait(r_halo.at[j, 0], halo_recv.at[j, 0])
        near = acc[...] + dot_split(r_halo[j, 0], w_hi[:pts], w_lo[:pts])
        wait(r_halo.at[j, 1], halo_recv.at[j, 1])
        near = near + dot_split(r_halo[j, 1], w_hi[2 * pts :], w_lo[2 * pts :])
        acc[...] = near
        if not last:
            tu_near[...] = dot_split(near, c_hi[...], c_lo[...])

        wait3(j)
        main = r3[j, :, 0].reshape(rows, LANES)
        edge = r3[j, :, 1].reshape(rows, LANES)
        moved = jnp.concatenate([main, edge], axis=1)
        if not last:
            scatter(j + 1, tu_near[...] + dot_split(moved, mc_hi[...], mc_lo[...]))
        w_next = acc[...] + dot_split(moved, m_hi[...], m_lo[...])
        wbuf[j + 1] = w_next
        if not last:
            send_halo(j + 1)
            acc[...] = dot_split(w_next, w_hi[pts : 2 * pts], w_lo[pts : 2 * pts])
        power = wbuf[j] + dot_split(jnp.where(low_rows, 0.0, main), ct_hi[...], ct_lo[...])
        square = jnp.sum(power * power, axis=1, keepdims=True)
        if last:
            part = lax.rem(iota((rows, LANES), 1), half) // (half // 4)
            sums = jnp.where(part == 3, square, 0.0)
            for k in range(3):
                sums = jnp.where(part == k, qbuf[k + 1], sums)
            scatter(j + 1, sums)
        else:
            qbuf[j] = jnp.broadcast_to(square, (rows, LANES))

            @pl.when(j == 1)
            def _():
                return_leaf(0, power)

            @pl.when(j == 3)
            def _():
                return_leaf(1, power)

        wait2(j)
        potentials = []
        for g, group in enumerate(groups):
            ups = chosen(r_top[group], lambda q: r2[j, q])
            tiles = [half_rows(ups[m], ups[m + 1]) for m in (0, 2)]
            potentials.append(dot_split(jnp.concatenate(tiles, axis=1), k2_hi[g], k2_lo[g]))
        f2, edges = potentials[0], potentials[1:]
        if last:
            send_potentials(j + 1, None, f2, edges)
            wait1(j + 1)
            sums = jnp.sum(r1[j + 1], axis=0)
            broadcast_far(j + 1, sums, sums)
            broadcast_to(j + 1, near_peers)
            return
        add = dot_split(f2, tg_hi[...], tg_lo[...])
        wait1(j + 1)
        got = r1[j + 1]
        up = jnp.sum(got, axis=0) + add[:, wide:]
        broadcast_far(j + 1, pltpu.roll(up, half, 1), up)
        send_potentials(j + 1, level_one(got, add[:, :wide]), f2, edges)
        broadcast_to(j + 1, near_peers)

    def step(j, carry):
        body(j, False)
        return carry

    lax.fori_loop(0, APPLIES - 1, step, 0)
    body(APPLIES - 1, True)

    for kind in range(2):
        wait(r_c.at[kind, pl.ds(0, n_leaf - 1)], set_recv.at[(9, 13)[kind]])
        s_d[:, kind] = jnp.swapaxes(r_c[kind], 0, 1)
    r_d[lvl] = s_d[lvl]
    over_lvl(lambda p: s_d.at[p], r_d.at[lvl], set_send.at[10], set_recv.at[10])

    wait3(APPLIES)
    main = r3[APPLIES, :, 0].reshape(rows, LANES)
    s_e[...] = packed_back(
        wbuf[APPLIES] + dot_split(jnp.where(low_rows, 0.0, main), ct_hi[...], ct_lo[...])
    )
    r_e[leaf] = s_e[leaf]
    over_leaf(lambda p: s_e.at[p], r_e.at[leaf], set_send.at[11], set_recv.at[11])
    wait(r_d.at[pl.ds(0, n_lvl - 1)], set_recv.at[10])
    back1 = unpacked(r_d[:, 0])
    back3 = unpacked(r_d[:, 1])
    wait2(APPLIES)
    sums = jnp.sum(r2[APPLIES], axis=0)
    sums = jnp.concatenate([sums, pltpu.roll(sums, half, 1)], axis=0)
    for d in range(n_lvl):
        s3[APPLIES + 1, d, 0] = sums
        s3[APPLIES + 1, d, 1] = sums
    gather(APPLIES + 1)
    wait(r_e.at[pl.ds(0, n_leaf - 1)], set_recv.at[11])
    s_f[...] = jnp.swapaxes(r_e[...], 0, 1)
    r_f[lvl] = s_f[lvl]
    over_lvl(lambda p: s_f.at[p], r_f.at[lvl], set_send.at[12], set_recv.at[12])

    wait3(APPLIES + 1)
    sums = r3[APPLIES + 1, :, 0].reshape(rows, LANES)
    g1, g2, g3, g4 = (sums[:, k * (half // 4) : k * (half // 4) + 1] for k in range(4))
    step0 = g1 / (g2 + RIDGE * g1 + EPSILON)
    keep = 1.0 - RIDGE * step0
    fresh = keep * keep * g1 - 2.0 * step0 * keep * g2 + step0 * step0 * g3
    lead = keep + fresh / (g1 + EPSILON)
    direction_sq = lead * lead * g1 - 2.0 * lead * step0 * g2 + step0 * step0 * g3
    image_sq = lead * lead * g2 - 2.0 * lead * step0 * g3 + step0 * step0 * g4
    step1 = fresh / (image_sq + RIDGE * direction_sq + EPSILON)
    result[0] = (step0 + step1 * lead) * back1 - (step1 * step0) * back3
    partial = (keep - RIDGE * step1 * lead) * back1 - (
        step0 + step1 * (lead - RIDGE * step0)
    ) * back3
    wait(r_f.at[pl.ds(0, n_lvl - 1)], set_recv.at[12])
    result[1] = partial + (step1 * step0) * unpacked(r_f[...])

    wait(r_a.at[pl.ds(0, n_lvl - 1)], set_send.at[0])
    wait(r_coords.at[0], set_send.at[1])
    wait(r_coords.at[1], set_send.at[2])
    wait(r_anch.at[pl.ds(0, n_lvl - 1)], set_send.at[3])
    wait(r_top.at[pl.ds(0, n_leaf - 1)], set_send.at[4])
    wait(r_b.at[pl.ds(0, n_leaf - 1)], set_send.at[5])
    wait(r_ct.at[0], set_send.at[6])
    wait(r_ct.at[1], set_send.at[7])
    wait(r_g.at[pl.ds(0, n_lvl - 1)], set_send.at[8])
    wait(r_c.at[0, pl.ds(0, n_leaf - 1)], set_send.at[9])
    wait(r_c.at[1, pl.ds(0, n_leaf - 1)], set_send.at[13])
    wait(r_d.at[pl.ds(0, n_lvl - 1)], set_send.at[10])
    wait(r_e.at[pl.ds(0, n_leaf - 1)], set_send.at[11])
    wait(r_f.at[pl.ds(0, n_lvl - 1)], set_send.at[12])

    def sent(j, carry):
        wait(r1.at[j, pl.ds(0, n_lvl - 1)], send1.at[j])
        wait(r2.at[j, pl.ds(0, n_leaf - 1)], send2.at[j])
        return carry

    lax.fori_loop(0, APPLIES + 1, sent, 0)

    def sent_halo(j, carry):
        wait(wbuf.at[j], halo_send.at[j, 0])
        wait(wbuf.at[j], halo_send.at[j, 1])
        return carry

    lax.fori_loop(0, APPLIES, sent_halo, 0)

    def sent_last(j, carry):
        wait(r3.at[j, pl.ds(0, n_lvl - 1)], send3.at[j])
        return carry

    lax.fori_loop(0, APPLIES + 2, sent_last, 0)


def on_device(
    targets, tree_pos, coords, ubasis, transfer_one, transfer_two, anchors_one, anchors_two,
    near_list, far_one, far_two,
):
    rows, pts = targets.shape
    n_leaf, n_lvl = lax.axis_size("leaf"), lax.axis_size("lvl")
    n_dev = n_leaf * n_lvl
    dim = coords.shape[0]
    ranks = anchors_one.shape[2]
    hbm = pl.BlockSpec(memory_space=pl.ANY)
    vmem = pl.BlockSpec(memory_space=pltpu.VMEM)
    smem = pl.BlockSpec(memory_space=pltpu.SMEM)
    V = pltpu.VMEM
    D = pltpu.SemaphoreType.DMA
    wide = n_lvl * ranks
    deep = far_two.shape[1] * ranks
    arrays = (
        targets, tree_pos.reshape(1, pts), coords, ubasis, transfer_one, transfer_two,
        anchors_one, anchors_two,
    )
    scratch = [V(a.shape, a.dtype) for a in arrays] + [
        V((n_dev, 2 * pts), BF16), V((n_dev, 2 * pts), BF16),
        V((n_lvl, n_leaf // 8 + 1, 8, LANES), F32), V((n_lvl, n_leaf // 8 + 1, 8, LANES), F32),
        V((n_leaf, n_lvl + 1, LANES), F32), V((n_leaf, n_lvl + 1, LANES), F32),
        V((2, n_leaf, n_lvl, LANES), F32), V((2, n_leaf, n_lvl, LANES), F32),
        V((n_lvl, 2, n_leaf, LANES), F32), V((n_lvl, 2, n_leaf, LANES), F32),
        V((n_leaf, n_lvl, LANES), F32), V((n_leaf, n_lvl, LANES), F32),
        V((n_lvl, n_leaf, LANES), F32), V((n_lvl, n_leaf, LANES), F32),
        V((2, dim, pts), F32),
        V((2, 8, LANES), F32), V((n_lvl, 2, 8, LANES), F32),
        V((8, LANES), F32), V((n_leaf, 8, LANES), F32),
        V((ranks, LANES), F32), V((n_lvl, ranks, LANES), F32),
        V((ranks, pts), F32), V((2, ranks, pts), F32),
        V((3 * pts, 64), BF16),
        V((3 * pts, pts), BF16), V((3 * pts, pts), BF16),
        V((wide, wide), BF16), V((wide, wide), BF16),
        V((3, deep, LANES), BF16), V((3, deep, LANES), BF16),
        V((pts, LANES), BF16), V((pts, LANES), BF16),
        V((LANES, pts), BF16), V((LANES, pts), BF16),
        V((2 * LANES, pts), BF16), V((2 * LANES, pts), BF16),
        V((2 * LANES, LANES), BF16), V((2 * LANES, LANES), BF16),
        V((LANES, wide + LANES), BF16), V((LANES, wide + LANES), BF16),
        V((APPLIES + 1, rows, pts), F32), V((rows, pts), F32), V((rows, LANES), F32),
        V((APPLIES, 2, rows, pts), F32), V((APPLIES - 1, rows, LANES), F32),
        V((APPLIES + 1, n_lvl, 8, LANES), F32), V((APPLIES + 1, n_lvl, 8, LANES), F32),
        V((APPLIES + 1, 4, LANES), F32), V((APPLIES + 1, n_leaf, 4, LANES), F32),
        V((APPLIES + 2, n_lvl, 2, 8, LANES), F32), V((APPLIES + 2, n_lvl, 2, 8, LANES), F32),
        D((len(arrays),)), D((14,)), D((14,)),
        D((APPLIES, 2)), D((APPLIES, 2)),
        D((APPLIES + 1,)), D((APPLIES + 1,)), D((APPLIES + 1,)), D((APPLIES + 1,)),
        D((APPLIES + 2,)), D((APPLIES + 2,)),
    ]
    out = jax.ShapeDtypeStruct((2, rows, pts), F32)
    body = lambda *refs: kernel((n_leaf, n_lvl), *refs)
    both = pl.pallas_call(
        body,
        out_shape=out,
        in_specs=[hbm] * len(arrays) + [smem] * 3,
        out_specs=vmem,
        scratch_shapes=scratch,
        compiler_params=pltpu.CompilerParams(
            collective_id=0, has_side_effects=True, vmem_limit_bytes=60 * 1024 * 1024
        ),
    )(*arrays, near_list, far_one, far_two)
    return both[0], both[1]


def solution(mesh):
    both = ("leaf", "lvl")
    return jax.shard_map(
        on_device,
        mesh=mesh,
        in_specs=(
            P(None, both), P(both), P(None, both), P(both, None, None), P(both, None, None),
            P(both, None, None), P(both, None, None), P("leaf", None, None),
            P(both, None), P(both, None), P("leaf", None),
        ),
        out_specs=(P(None, both), P(None, both)),
        check_vma=False,
    )
```

```python
import jax
import jax.numpy as jnp
from jax import lax
from jax.experimental import pallas as pl
from jax.experimental.pallas import tpu as pltpu
from jax.sharding import PartitionSpec as P

F32 = jnp.float32
BF16 = jnp.bfloat16
MESH = pl.DeviceIdType.MESH
PRECISE = lax.Precision.HIGHEST
DIM = 8
RIDGE = 1.0
EPSILON = 1e-6
APPLIES = 5
LANES = 128


def dot(a, b, ca=1, cb=0):
    return lax.dot_general(a, b, (((ca,), (cb,)), ((), ())), preferred_element_type=F32)


def dot_precise(a, b):
    return lax.dot_general(
        a, b, (((1,), (0,)), ((), ())), precision=PRECISE, preferred_element_type=F32
    )


def split2(x):
    hi = x.astype(BF16)
    return hi, (x - hi.astype(F32)).astype(BF16)


def split3(x):
    hi = x.astype(BF16)
    rest = x - hi.astype(F32)
    mid = rest.astype(BF16)
    return hi, mid, (rest - mid.astype(F32)).astype(BF16)


def dot_split(a, b_hi, b_lo):
    rows = a.shape[0]
    a_hi, a_lo = split2(a)
    both = dot(jnp.concatenate([a_hi, a_lo], axis=0), b_hi)
    return both[:rows] + both[rows:] + dot(a_hi, b_lo)


def iota(shape, dim):
    return lax.broadcasted_iota(jnp.int32, shape, dim)


def augmented(x):
    n = x.shape[1]
    x1, x2, x3 = (p.astype(F32) for p in split3(x))
    sq = jnp.sum(x * x, axis=0, keepdims=True) * (-1.0 / DIM)
    n1, n2, n3 = (p.astype(F32) for p in split3(sq))
    row = iota((8, n), 0)
    lead = jnp.where(row == 0, n1, jnp.where(row == 1, n2, n3))
    tail = jnp.where(row == 3, n1, jnp.where(row == 4, n2, n3))
    zero = jnp.zeros((8, n), F32)
    src_norm = jnp.where(row < 3, lead, jnp.where(row < 6, 1.0, 0.0))
    dst_norm = jnp.where(row < 3, 1.0, jnp.where(row < 6, tail, 0.0))
    q = 2.0 / DIM
    src = jnp.concatenate([x1, x1, x2, x1, x3, x2, src_norm, zero], axis=0)
    dst = jnp.concatenate([x1 * q, x2 * q, x1 * q, x3 * q, x1 * q, x2 * q, dst_norm, zero], axis=0)
    return src, dst


def pack(onehot, x):
    total = None
    for part in split3(x):
        zero = jnp.zeros_like(part)
        wide = jnp.concatenate(
            [jnp.concatenate([part, zero], axis=1), jnp.concatenate([zero, part], axis=1)], axis=0
        )
        term = dot(onehot, wide, 1, 1)
        total = term if total is None else total + term
    return total


def unpack(onehot, g):
    half = g.shape[1] // 2
    cols = onehot.shape[1] // 2
    gt = jnp.transpose(g)
    total = None
    for part in split3(gt):
        term = dot(part, onehot)
        total = term if total is None else total + term
    return total[:half, :cols] + total[half:, cols:]


def kernel(
    sizes,
    targets_h, tree_pos_h, coords_h, ubasis_h, transfer_one_h, transfer_two_h, anchors_one_h,
    anchors_two_h, near_list, far_one, far_two,
    result,
    targets, tree_pos, coords, ubasis, transfer_one, transfer_two, anchors_one, anchors_two,
    oh_user, oh_tree, s_a, r_a, s_b, r_b, s_c, r_c, s_d, r_d, s_e, r_e, s_f, r_f,
    r_coords, s_anch, r_anch, s_top, r_top, s_g, r_g, ct_full, r_ct,
    src_pts, w_hi, w_lo, k1_hi, k1_lo, k2_hi, k2_lo, c_hi, c_lo, ct_hi, ct_lo, m_hi, m_lo, mc_hi, mc_lo,
    tg_hi, tg_lo,
    wbuf, acc, tu_near, r_halo, qbuf, s1, r1, s2, r2, s3, r3,
    in_sem, set_send, set_recv, halo_send, halo_recv, send1, recv1, send2, recv2, send3, recv3,
):
    n_leaf, n_lvl = sizes
    n_dev = n_leaf * n_lvl
    leaf, lvl = lax.axis_index("leaf"), lax.axis_index("lvl")
    rows, pts = targets.shape
    clusters = ubasis.shape[0]
    points = ubasis.shape[2]
    ranks = ubasis.shape[1]
    half = LANES // 2
    total = n_dev * clusters
    near_lists = near_list.shape[1]
    lower_count = far_one.shape[1]
    upper_count = far_two.shape[1]

    inputs = []
    pairs = (
        (tree_pos_h, tree_pos), (targets_h, targets), (transfer_one_h, transfer_one),
        (ubasis_h, ubasis), (transfer_two_h, transfer_two), (coords_h, coords),
        (anchors_one_h, anchors_one), (anchors_two_h, anchors_two),
    )
    for k, (hbm, vmem) in enumerate(pairs):
        inputs.append(pltpu.make_async_copy(hbm, vmem, in_sem.at[k]))
        inputs[-1].start()

    chips_z, cores = 8, 2
    chips_y, chips_x = n_leaf // chips_z, n_lvl // cores

    def others(long, short):
        pairs = [(a, b) for a in range(long) for b in range(short)][1:]
        far = lambda p: min(p[0], long - p[0]) + min(p[1], short - p[1]) * (short > 2)
        return sorted(pairs, key=lambda p: -far(p))

    def shifted(index, short, long, a, b):
        return lax.rem(index // short + a, long) * short + lax.rem(lax.rem(index, short) + b, short)

    leaf_peers = [shifted(leaf, chips_z, chips_y, a, b) for a, b in others(chips_y, chips_z)]
    lvl_peers = [shifted(lvl, cores, chips_x, a, b) for a, b in others(chips_x, cores)]
    leaf_before, leaf_after = lax.rem(leaf + n_leaf - 1, n_leaf), lax.rem(leaf + 1, n_leaf)

    ring = leaf * n_lvl + lvl
    after = lax.rem(ring + 1, n_dev)
    before = lax.rem(ring + n_dev - 1, n_dev)
    after_id = (after // n_lvl, lax.rem(after, n_lvl))
    before_id = (before // n_lvl, lax.rem(before, n_lvl))

    def copy(src, dst, send, recv, device):
        pltpu.make_async_remote_copy(
            src_ref=src, dst_ref=dst, send_sem=send, recv_sem=recv,
            device_id=device, device_id_type=MESH,
        ).start()

    def wait(ref, sem):
        pltpu.make_async_copy(ref, ref, sem).wait()

    def over_lvl(src, dst, send, recv):
        for peer in lvl_peers:
            copy(src(peer), dst, send, recv, (leaf, peer))

    def over_leaf(src, dst, send, recv):
        for peer in leaf_peers:
            copy(src(peer), dst, send, recv, (peer, lvl))

    barrier = pltpu.get_barrier_semaphore()
    for peer in leaf_peers:
        pl.semaphore_signal(barrier, inc=1, device_id=(peer, lvl), device_id_type=MESH)
    for peer in lvl_peers:
        pl.semaphore_signal(barrier, inc=1, device_id=(leaf, peer), device_id_type=MESH)
    pl.semaphore_signal(barrier, inc=1, device_id=after_id, device_id_type=MESH)
    pl.semaphore_signal(barrier, inc=1, device_id=before_id, device_id_type=MESH)

    lane = iota((8, LANES), 1)
    low = lane < half
    row8 = iota((8, LANES), 0)
    low_rows = iota((rows, LANES), 1) < half

    inputs[0].wait()
    tp = tree_pos[...]
    dest = lax.div(tp, pts)
    place = lax.rem(dest, n_lvl) * n_leaf + lax.div(dest, n_lvl)
    hit = iota((n_dev, pts), 0) == place
    hit16 = hit.astype(F32).astype(BF16)
    earlier = (iota((pts, pts), 0) < iota((pts, pts), 1)).astype(F32).astype(BF16)
    seen = dot(hit16, earlier)
    oh_user[:, :pts] = jnp.where(hit & (seen < 0.5), 1.0, 0.0).astype(BF16)
    oh_user[:, pts:] = jnp.where(hit & (seen > 0.5), 1.0, 0.0).astype(BF16)
    inputs[1].wait()
    blocks = n_leaf // 8
    packed = pack(oh_user[...], targets[...])
    s_a[:, :blocks] = packed.reshape(n_lvl, blocks, 8, LANES)
    pos = lax.rem(tp, pts).astype(F32)
    pos_hi = pos.astype(BF16).astype(F32)
    row16 = iota((16, pts), 0)
    terms = jnp.where(row16 == 0, pos_hi, jnp.where(row16 == 1, pos - pos_hi, 0.0)).astype(BF16)
    tile = jnp.zeros((8, LANES), F32)
    for h in range(2):
        both = dot(terms, oh_user[:, h * pts : (h + 1) * pts], 1, 1)
        line = both[0:1] + both[1:2]
        for q in range(n_dev // LANES):
            part = line[:, q * LANES : (q + 1) * LANES]
            tile = jnp.where(row8 == 2 * h + q, part, tile)
    for p in range(n_lvl):
        s_a[p, blocks] = tile
    r_a[lvl] = s_a[lvl]

    for k in range(2, len(pairs)):
        inputs[k].wait()
    own_one = jnp.concatenate([anchors_one[0], anchors_one[0]], axis=1)
    own_two = jnp.concatenate([anchors_two[0], anchors_two[0]], axis=1)
    partner = jnp.full((8, LANES), -1.0, F32)
    for k in range(lower_count):
        value = lax.rem(far_one[0, k], n_lvl).astype(F32)
        partner = jnp.where(row8 == k, value, partner)
    s_anch[0] = own_one
    s_anch[1] = partner
    r_anch[lvl] = s_anch[...]
    partner = own_two
    for k in range(upper_count):
        value = far_two[0, k].astype(F32)
        partner = jnp.where(jnp.logical_and(row8 == k, jnp.logical_not(low)), value, partner)
    s_top[...] = partner
    r_top[leaf] = partner

    pl.semaphore_wait(barrier, n_lvl + n_leaf)

    over_lvl(lambda p: s_a.at[p], r_a.at[lvl], set_send.at[0], set_recv.at[0])
    copy(coords, r_coords.at[0], set_send.at[1], set_recv.at[1], after_id)
    copy(coords, r_coords.at[1], set_send.at[2], set_recv.at[2], before_id)
    over_lvl(lambda p: s_anch, r_anch.at[lvl], set_send.at[3], set_recv.at[3])
    over_leaf(lambda p: s_top, r_top.at[leaf], set_send.at[4], set_recv.at[4])

    bt = jnp.concatenate(
        [dot_precise(jnp.transpose(transfer_one[c]), ubasis[c]) for c in range(clusters)], axis=1
    )
    b2t = dot_precise(jnp.transpose(transfer_two[0]), bt)
    ct = jnp.concatenate([bt, b2t], axis=0)
    c = jnp.transpose(ct)
    ct_full[...] = b2t
    ct_hi[...], ct_lo[...] = split2(ct)
    c_hi[...], c_lo[...] = split2(c)
    s_g[...] = dot_split(b2t, c_hi[...], c_lo[...])
    r_g[lvl] = s_g[...]

    wait(r_a.at[pl.ds(0, n_lvl - 1)], set_recv.at[0])
    s_b[:, :n_lvl] = jnp.swapaxes(r_a[:, :blocks].reshape(n_lvl, n_leaf, LANES), 0, 1)
    per_row = LANES // n_leaf
    mine = []
    for h in range(2):
        line = jnp.where(lvl < per_row, r_a[:, blocks, 2 * h], r_a[:, blocks, 2 * h + 1])
        turned = line
        for k in range(1, per_row):
            here = lax.rem(lvl, per_row) == k
            turned = jnp.where(here, pltpu.roll(line, LANES - k * n_leaf, 1), turned)
        mine.append(turned)
    square = jnp.concatenate(mine + [jnp.zeros((LANES - 16, LANES), F32)], axis=0)
    s_b[:, n_lvl : n_lvl + 1] = jnp.transpose(square)[:n_leaf].reshape(n_leaf, 1, LANES)
    r_b[leaf] = s_b[leaf]
    over_leaf(lambda p: s_b.at[p], r_b.at[leaf], set_send.at[5], set_recv.at[5])
    over_lvl(lambda p: s_g, r_g.at[lvl], set_send.at[8], set_recv.at[8])
    copy(ct_full, r_ct.at[0], set_send.at[6], set_recv.at[6], after_id)
    copy(ct_full, r_ct.at[1], set_send.at[7], set_recv.at[7], before_id)

    wait(r_coords.at[0], set_recv.at[1])
    wait(r_coords.at[1], set_recv.at[2])
    src, dst = augmented(coords[...])
    src_pts[pts : 2 * pts] = jnp.transpose(src).astype(BF16)
    src_pts[:pts] = jnp.transpose(augmented(r_coords[0])[0]).astype(BF16)
    src_pts[2 * pts :] = jnp.transpose(augmented(r_coords[1])[0]).astype(BF16)
    dst = dst.astype(BF16)
    first = ring * clusters - clusters
    near_scale = (points * (near_lists + 1)) ** (-0.5)

    def near_rows(n, carry):
        at = pl.ds(pl.multiple_of(n * points, points), points)
        value = jnp.exp(dot(src_pts[at, :], dst))
        parts = []
        for c in range(clusters):
            weight = (n == c + clusters).astype(jnp.int32)
            for k in range(near_lists):
                rel = lax.rem(near_list[c, k] - first + total, total)
                weight = weight + (rel == n).astype(jnp.int32)
            scaled = weight.astype(F32) * near_scale
            parts.append(value[:, c * points : (c + 1) * points] * scaled)
        hi, lo = split2(jnp.concatenate(parts, axis=1))
        w_hi[at, :] = hi
        w_lo[at, :] = lo
        return carry

    lax.fori_loop(0, 3 * clusters, near_rows, 0)

    def lanes_of(get):
        tiles = []
        for m in range(n_lvl // 2):
            tiles.append(jnp.where(low, get(2 * m), get(2 * m + 1)))
        return jnp.concatenate(tiles, axis=1)

    wait(r_anch.at[pl.ds(0, n_lvl - 1)], set_recv.at[3])
    src, dst = augmented(lanes_of(lambda p: r_anch[p, 0]))
    wide = n_lvl * ranks
    partners = lanes_of(lambda p: r_anch[p, 1])
    owner = lax.div(iota((wide, wide), 0), ranks).astype(F32)
    count = jnp.zeros((wide, wide), F32)
    for k in range(lower_count):
        count = count + jnp.where(owner == partners[k : k + 1], 1.0, 0.0)
    value = jnp.exp(dot(jnp.transpose(src).astype(BF16), dst.astype(BF16)))
    k1_hi[...], k1_lo[...] = split2(value * count * (lower_count ** (-0.5)))

    wait(r_top.at[pl.ds(0, n_leaf - 1)], set_recv.at[4])
    groups = (leaf, leaf_before, leaf_after)

    def chosen(lists, get):
        lists = jnp.where(low, pltpu.roll(lists, half, 1), lists)
        picks = [get(0)] * upper_count
        named = [jnp.broadcast_to(lists[k : k + 1], picks[0].shape) for k in range(upper_count)]
        for q in range(1, n_leaf):
            value = get(q)
            picks = [jnp.where(n == float(q), value, p) for n, p in zip(named, picks)]
        return picks

    for g, group in enumerate(groups):
        tops = chosen(r_top[group], lambda q: r_top[q])
        src, _ = augmented(
            jnp.concatenate(
                [jnp.where(low, tops[m], pltpu.roll(tops[m + 1], half, 1)) for m in (0, 2)], axis=1
            )
        )
        mine = r_top[group]
        _, dst = augmented(jnp.where(low, mine, pltpu.roll(mine, half, 1)))
        value = jnp.exp(dot(jnp.transpose(src).astype(BF16), dst.astype(BF16)))
        first_half = iota(value.shape, 1) < half
        value = jnp.where(first_half, 0.0, value) if g == 0 else jnp.where(first_half, value, 0.0)
        k2_hi[g], k2_lo[g] = split2(value * (upper_count ** (-0.5)))

    wait(r_g.at[pl.ds(0, n_lvl - 1)], set_recv.at[8])
    low_ranks = iota((ranks, LANES), 1) < half
    gamma = r_g[0]
    for p in range(1, n_lvl):
        gamma = gamma + r_g[p]
    tiles = [
        jnp.where(low_ranks, r_g[2 * m], pltpu.roll(r_g[2 * m + 1], half, 1))
        for m in range(n_lvl // 2)
    ]
    tiles.append(jnp.where(low_ranks, 0.0, gamma))
    tg = jnp.concatenate(tiles, axis=1)
    tg_hi[...], tg_lo[...] = split2(jnp.concatenate([jnp.zeros_like(tg), tg], axis=0))
    wait(r_ct.at[0], set_recv.at[6])
    wait(r_ct.at[1], set_recv.at[7])
    z_own = dot_split(ct_full[...], w_hi[pts : 2 * pts], w_lo[pts : 2 * pts])
    z_prev = dot_split(r_ct[0], w_hi[:pts], w_lo[:pts])
    z_next = dot_split(r_ct[1], w_hi[2 * pts :], w_lo[2 * pts :])
    at_first = (lvl == 0).astype(F32)
    at_last = (lvl == n_lvl - 1).astype(F32)
    z_main = z_own + z_prev * (1.0 - at_first) + z_next * (1.0 - at_last)
    z_edge = z_prev * at_first + z_next * at_last
    m = jnp.concatenate([bt, z_main, z_edge, jnp.zeros_like(z_edge)], axis=0)
    m_hi[...], m_lo[...] = split2(m)
    mc_hi[...], mc_lo[...] = split2(dot_split(m, c_hi[...], c_lo[...]))

    wait(r_b.at[pl.ds(0, n_leaf - 1)], set_recv.at[5])
    column = iota((n_dev, pts), 1).astype(F32)
    row3 = iota((n_leaf, n_lvl, LANES), 1)
    lane3 = iota((n_leaf, n_lvl, LANES), 2)
    line = jnp.broadcast_to(r_b[:, n_lvl : n_lvl + 1], (n_leaf, n_lvl, LANES))
    for h in range(2):
        got = jnp.where(lane3 == row3 + h * n_lvl, line, 0.0).reshape(n_dev, LANES)
        got = jnp.sum(got, axis=1, keepdims=True)
        oh_tree[:, h * pts : (h + 1) * pts] = jnp.where(column == got, 1.0, 0.0).astype(BF16)
    wbuf[0] = unpack(oh_tree[...], r_b[:, :n_lvl].reshape(n_dev, LANES))

    def send_halo(j):
        copy(wbuf.at[j], r_halo.at[j, 0], halo_send.at[j, 0], halo_recv.at[j, 0], after_id)
        copy(wbuf.at[j], r_halo.at[j, 1], halo_send.at[j, 1], halo_recv.at[j, 1], before_id)

    def scatter(j, value):
        s1[j] = value.reshape(n_lvl, 8, LANES)
        over_lvl(lambda peer: s1.at[j, peer], r1.at[j, lvl], send1.at[j], recv1.at[j])
        r1[j, lvl] = s1[j, lvl]

    def broadcast_to(j, peers):
        for peer in peers:
            copy(s2.at[j], r2.at[j, leaf], send2.at[j], recv2.at[j], (peer, lvl))

    far_peers, near_peers = leaf_peers[:5], leaf_peers[5:]

    def broadcast_far(j, lower, upper):
        value = jnp.where(low[:4], lower[:4], upper[4:])
        s2[j] = value
        broadcast_to(j, far_peers)
        r2[j, leaf] = value

    def half_rows(a, b):
        turned_a, turned_b = pltpu.roll(a, half, 1), pltpu.roll(b, half, 1)
        return jnp.concatenate(
            [jnp.where(low[:4], a, turned_b), jnp.where(low[:4], turned_a, b)], axis=0
        )

    def gather(j):
        over_lvl(lambda peer: s3.at[j, peer], r3.at[j, lvl], send3.at[j], recv3.at[j])
        r3[j, lvl] = s3[j, lvl]

    def wait1(j):
        wait(r1.at[j, pl.ds(0, n_lvl - 1)], recv1.at[j])

    def wait2(j):
        wait(r2.at[j, pl.ds(0, n_leaf - 1)], recv2.at[j])

    def wait3(j):
        wait(r3.at[j, pl.ds(0, n_lvl - 1)], recv3.at[j])

    def send_potentials(j, f1, f2, edges):
        for d in range(n_lvl):
            tile = jnp.zeros((8, LANES), F32)
            if f1 is not None:
                tile = f1[:, (d // 2) * LANES : (d // 2 + 1) * LANES]
                if d % 2:
                    tile = pltpu.roll(tile, half, 1)
            s3[j, d, 0] = jnp.where(low, tile, f2)
            s3[j, d, 1] = edges[0] if d == 0 else edges[1] if d == n_lvl - 1 else jnp.zeros_like(f2)
        gather(j)

    def level_one(own, extra):
        tiles = [
            jnp.where(low, own[2 * m], pltpu.roll(own[2 * m + 1], half, 1))
            for m in range(n_lvl // 2)
        ]
        t = jnp.concatenate(tiles, axis=1)
        if extra is not None:
            t = t + extra
        return dot_split(t, k1_hi[...], k1_lo[...])

    def packed_back(value):
        return pack(oh_tree[...], value).reshape(n_leaf, n_lvl, LANES)

    def return_leaf(kind, value):
        s_c[kind] = packed_back(value)
        r_c[kind, leaf] = s_c[kind, leaf]
        sems = set_send.at[(9, 13)[kind]], set_recv.at[(9, 13)[kind]]
        over_leaf(lambda p: s_c.at[kind, p], r_c.at[kind, leaf], *sems)

    def unpacked(rows_back):
        return unpack(oh_user[...], rows_back.reshape(n_dev, LANES))

    zero8 = jnp.zeros((8, LANES), F32)
    scatter(0, dot_split(wbuf[0], c_hi[...], c_lo[...]))
    send_halo(0)
    acc[...] = dot_split(wbuf[0], w_hi[pts : 2 * pts], w_lo[pts : 2 * pts])
    wait1(0)
    got = r1[0]
    up = jnp.sum(got, axis=0)
    broadcast_far(0, pltpu.roll(up, half, 1), up)
    send_potentials(0, level_one(got, None), zero8, (zero8, zero8))
    broadcast_to(0, near_peers)

    def body(j, last):
        wait(r_halo.at[j, 0], halo_recv.at[j, 0])
        near = acc[...] + dot_split(r_halo[j, 0], w_hi[:pts], w_lo[:pts])
        wait(r_halo.at[j, 1], halo_recv.at[j, 1])
        near = near + dot_split(r_halo[j, 1], w_hi[2 * pts :], w_lo[2 * pts :])
        acc[...] = near
        if not last:
            tu_near[...] = dot_split(near, c_hi[...], c_lo[...])

        wait3(j)
        main = r3[j, :, 0].reshape(rows, LANES)
        edge = r3[j, :, 1].reshape(rows, LANES)
        moved = jnp.concatenate([main, edge], axis=1)
        if not last:
            scatter(j + 1, tu_near[...] + dot_split(moved, mc_hi[...], mc_lo[...]))
        w_next = acc[...] + dot_split(moved, m_hi[...], m_lo[...])
        wbuf[j + 1] = w_next
        if not last:
            send_halo(j + 1)
            acc[...] = dot_split(w_next, w_hi[pts : 2 * pts], w_lo[pts : 2 * pts])
        power = wbuf[j] + dot_split(jnp.where(low_rows, 0.0, main), ct_hi[...], ct_lo[...])
        square = jnp.sum(power * power, axis=1, keepdims=True)
        if last:
            part = lax.rem(iota((rows, LANES), 1), half) // (half // 4)
            sums = jnp.where(part == 3, square, 0.0)
            for k in range(3):
                sums = jnp.where(part == k, qbuf[k + 1], sums)
            scatter(j + 1, sums)
        else:
            qbuf[j] = jnp.broadcast_to(square, (rows, LANES))

            @pl.when(j == 1)
            def _():
                return_leaf(0, power)

            @pl.when(j == 3)
            def _():
                return_leaf(1, power)

        wait2(j)
        potentials = []
        for g, group in enumerate(groups):
            ups = chosen(r_top[group], lambda q: r2[j, q])
            tiles = [half_rows(ups[m], ups[m + 1]) for m in (0, 2)]
            potentials.append(dot_split(jnp.concatenate(tiles, axis=1), k2_hi[g], k2_lo[g]))
        f2, edges = potentials[0], potentials[1:]
        if last:
            send_potentials(j + 1, None, f2, edges)
            wait1(j + 1)
            sums = jnp.sum(r1[j + 1], axis=0)
            broadcast_far(j + 1, sums, sums)
            broadcast_to(j + 1, near_peers)
            return
        add = dot_split(f2, tg_hi[...], tg_lo[...])
        wait1(j + 1)
        got = r1[j + 1]
        up = jnp.sum(got, axis=0) + add[:, wide:]
        broadcast_far(j + 1, pltpu.roll(up, half, 1), up)
        send_potentials(j + 1, level_one(got, add[:, :wide]), f2, edges)
        broadcast_to(j + 1, near_peers)

    def step(j, carry):
        body(j, False)
        return carry

    lax.fori_loop(0, APPLIES - 1, step, 0)
    body(APPLIES - 1, True)

    wait3(APPLIES)
    main = r3[APPLIES, :, 0].reshape(rows, LANES)
    s_e[...] = packed_back(
        wbuf[APPLIES] + dot_split(jnp.where(low_rows, 0.0, main), ct_hi[...], ct_lo[...])
    )
    r_e[leaf] = s_e[leaf]
    over_leaf(lambda p: s_e.at[p], r_e.at[leaf], set_send.at[11], set_recv.at[11])
    for kind in range(2):
        wait(r_c.at[kind, pl.ds(0, n_leaf - 1)], set_recv.at[(9, 13)[kind]])
        s_d[:, kind] = jnp.swapaxes(r_c[kind], 0, 1)
    r_d[lvl] = s_d[lvl]
    over_lvl(lambda p: s_d.at[p], r_d.at[lvl], set_send.at[10], set_recv.at[10])
    wait2(APPLIES)
    sums = jnp.sum(r2[APPLIES], axis=0)
    sums = jnp.concatenate([sums, pltpu.roll(sums, half, 1)], axis=0)
    for d in range(n_lvl):
        s3[APPLIES + 1, d, 0] = sums
        s3[APPLIES + 1, d, 1] = sums
    gather(APPLIES + 1)
    wait(r_e.at[pl.ds(0, n_leaf - 1)], set_recv.at[11])
    s_f[...] = jnp.swapaxes(r_e[...], 0, 1)
    r_f[lvl] = s_f[lvl]
    over_lvl(lambda p: s_f.at[p], r_f.at[lvl], set_send.at[12], set_recv.at[12])

    wait(r_d.at[pl.ds(0, n_lvl - 1)], set_recv.at[10])
    back1 = unpacked(r_d[:, 0])
    back3 = unpacked(r_d[:, 1])
    wait3(APPLIES + 1)
    sums = r3[APPLIES + 1, :, 0].reshape(rows, LANES)
    g1, g2, g3, g4 = (sums[:, k * (half // 4) : k * (half // 4) + 1] for k in range(4))
    step0 = g1 / (g2 + RIDGE * g1 + EPSILON)
    keep = 1.0 - RIDGE * step0
    fresh = keep * keep * g1 - 2.0 * step0 * keep * g2 + step0 * step0 * g3
    lead = keep + fresh / (g1 + EPSILON)
    direction_sq = lead * lead * g1 - 2.0 * lead * step0 * g2 + step0 * step0 * g3
    image_sq = lead * lead * g2 - 2.0 * lead * step0 * g3 + step0 * step0 * g4
    step1 = fresh / (image_sq + RIDGE * direction_sq + EPSILON)
    result[0] = (step0 + step1 * lead) * back1 - (step1 * step0) * back3
    partial = (keep - RIDGE * step1 * lead) * back1 - (
        step0 + step1 * (lead - RIDGE * step0)
    ) * back3
    wait(r_f.at[pl.ds(0, n_lvl - 1)], set_recv.at[12])
    result[1] = partial + (step1 * step0) * unpacked(r_f[...])

    wait(r_a.at[pl.ds(0, n_lvl - 1)], set_send.at[0])
    wait(r_coords.at[0], set_send.at[1])
    wait(r_coords.at[1], set_send.at[2])
    wait(r_anch.at[pl.ds(0, n_lvl - 1)], set_send.at[3])
    wait(r_top.at[pl.ds(0, n_leaf - 1)], set_send.at[4])
    wait(r_b.at[pl.ds(0, n_leaf - 1)], set_send.at[5])
    wait(r_ct.at[0], set_send.at[6])
    wait(r_ct.at[1], set_send.at[7])
    wait(r_g.at[pl.ds(0, n_lvl - 1)], set_send.at[8])
    wait(r_c.at[0, pl.ds(0, n_leaf - 1)], set_send.at[9])
    wait(r_c.at[1, pl.ds(0, n_leaf - 1)], set_send.at[13])
    wait(r_d.at[pl.ds(0, n_lvl - 1)], set_send.at[10])
    wait(r_e.at[pl.ds(0, n_leaf - 1)], set_send.at[11])
    wait(r_f.at[pl.ds(0, n_lvl - 1)], set_send.at[12])

    def sent(j, carry):
        wait(r1.at[j, pl.ds(0, n_lvl - 1)], send1.at[j])
        wait(r2.at[j, pl.ds(0, n_leaf - 1)], send2.at[j])
        return carry

    lax.fori_loop(0, APPLIES + 1, sent, 0)

    def sent_halo(j, carry):
        wait(wbuf.at[j], halo_send.at[j, 0])
        wait(wbuf.at[j], halo_send.at[j, 1])
        return carry

    lax.fori_loop(0, APPLIES, sent_halo, 0)

    def sent_last(j, carry):
        wait(r3.at[j, pl.ds(0, n_lvl - 1)], send3.at[j])
        return carry

    lax.fori_loop(0, APPLIES + 2, sent_last, 0)


def on_device(
    targets, tree_pos, coords, ubasis, transfer_one, transfer_two, anchors_one, anchors_two,
    near_list, far_one, far_two,
):
    rows, pts = targets.shape
    n_leaf, n_lvl = lax.axis_size("leaf"), lax.axis_size("lvl")
    n_dev = n_leaf * n_lvl
    dim = coords.shape[0]
    ranks = anchors_one.shape[2]
    hbm = pl.BlockSpec(memory_space=pl.ANY)
    vmem = pl.BlockSpec(memory_space=pltpu.VMEM)
    smem = pl.BlockSpec(memory_space=pltpu.SMEM)
    V = pltpu.VMEM
    D = pltpu.SemaphoreType.DMA
    wide = n_lvl * ranks
    deep = far_two.shape[1] * ranks
    arrays = (
        targets, tree_pos.reshape(1, pts), coords, ubasis, transfer_one, transfer_two,
        anchors_one, anchors_two,
    )
    scratch = [V(a.shape, a.dtype) for a in arrays] + [
        V((n_dev, 2 * pts), BF16), V((n_dev, 2 * pts), BF16),
        V((n_lvl, n_leaf // 8 + 1, 8, LANES), F32), V((n_lvl, n_leaf // 8 + 1, 8, LANES), F32),
        V((n_leaf, n_lvl + 1, LANES), F32), V((n_leaf, n_lvl + 1, LANES), F32),
        V((2, n_leaf, n_lvl, LANES), F32), V((2, n_leaf, n_lvl, LANES), F32),
        V((n_lvl, 2, n_leaf, LANES), F32), V((n_lvl, 2, n_leaf, LANES), F32),
        V((n_leaf, n_lvl, LANES), F32), V((n_leaf, n_lvl, LANES), F32),
        V((n_lvl, n_leaf, LANES), F32), V((n_lvl, n_leaf, LANES), F32),
        V((2, dim, pts), F32),
        V((2, 8, LANES), F32), V((n_lvl, 2, 8, LANES), F32),
        V((8, LANES), F32), V((n_leaf, 8, LANES), F32),
        V((ranks, LANES), F32), V((n_lvl, ranks, LANES), F32),
        V((ranks, pts), F32), V((2, ranks, pts), F32),
        V((3 * pts, 64), BF16),
        V((3 * pts, pts), BF16), V((3 * pts, pts), BF16),
        V((wide, wide), BF16), V((wide, wide), BF16),
        V((3, deep, LANES), BF16), V((3, deep, LANES), BF16),
        V((pts, LANES), BF16), V((pts, LANES), BF16),
        V((LANES, pts), BF16), V((LANES, pts), BF16),
        V((2 * LANES, pts), BF16), V((2 * LANES, pts), BF16),
        V((2 * LANES, LANES), BF16), V((2 * LANES, LANES), BF16),
        V((LANES, wide + LANES), BF16), V((LANES, wide + LANES), BF16),
        V((APPLIES + 1, rows, pts), F32), V((rows, pts), F32), V((rows, LANES), F32),
        V((APPLIES, 2, rows, pts), F32), V((APPLIES - 1, rows, LANES), F32),
        V((APPLIES + 1, n_lvl, 8, LANES), F32), V((APPLIES + 1, n_lvl, 8, LANES), F32),
        V((APPLIES + 1, 4, LANES), F32), V((APPLIES + 1, n_leaf, 4, LANES), F32),
        V((APPLIES + 2, n_lvl, 2, 8, LANES), F32), V((APPLIES + 2, n_lvl, 2, 8, LANES), F32),
        D((len(arrays),)), D((14,)), D((14,)),
        D((APPLIES, 2)), D((APPLIES, 2)),
        D((APPLIES + 1,)), D((APPLIES + 1,)), D((APPLIES + 1,)), D((APPLIES + 1,)),
        D((APPLIES + 2,)), D((APPLIES + 2,)),
    ]
    out = jax.ShapeDtypeStruct((2, rows, pts), F32)
    body = lambda *refs: kernel((n_leaf, n_lvl), *refs)
    both = pl.pallas_call(
        body,
        out_shape=out,
        in_specs=[hbm] * len(arrays) + [smem] * 3,
        out_specs=vmem,
        scratch_shapes=scratch,
        compiler_params=pltpu.CompilerParams(
            collective_id=0, has_side_effects=True, vmem_limit_bytes=60 * 1024 * 1024
        ),
    )(*arrays, near_list, far_one, far_two)
    return both[0], both[1]


def solution(mesh):
    both = ("leaf", "lvl")
    return jax.shard_map(
        on_device,
        mesh=mesh,
        in_specs=(
            P(None, both), P(both), P(None, both), P(both, None, None), P(both, None, None),
            P(both, None, None), P(both, None, None), P("leaf", None, None),
            P(both, None), P(both, None), P("leaf", None),
        ),
        out_specs=(P(None, both), P(None, both)),
        check_vma=False,
    )
```
